32 devices in a mesh: dp: 16 (over z, y, x), pipe: 2 (over core).
Axes of the slice: x: 2, y: 2, z: 4, core: 2. Of those that a mesh axis runs over, the one named last changes fastest.
Arguments:
- boundary: float32 [2, 16384, 512], P('pipe', 'dp'), may hold values from -6 to 6
- positions: bfloat16 [2, 512, 512], P(None, 'pipe'), may hold values from -3 to 3
- w_in: bfloat16 [2, 512, 1536], P(None, 'pipe'), may hold values from -0.25 to 0.25
- qv_bias: bfloat16 [2, 1024], P(None, 'pipe'), may hold values from -3 to 3
- w_out: bfloat16 [2, 512, 512], P(None, 'pipe'), may hold values from -1 to 1
- out_bias: bfloat16 [2, 512], P(None, 'pipe'), may hold values from -2 to 2
- gain_one: bfloat16 [2, 512], P(None, 'pipe'), may hold values from 0.25 to 1.75
- shift_one: bfloat16 [2, 512], P(None, 'pipe'), may hold values from -2 to 2
- w_up: bfloat16 [2, 512, 2048], P(None, 'pipe'), may hold values from -0.25 to 0.25
- up_bias: bfloat16 [2, 2048], P(None, 'pipe'), may hold values from -3 to 3
- w_down: bfloat16 [2, 2048, 512], P(None, 'pipe'), may hold values from -0.125 to 0.125
- down_bias: bfloat16 [2, 512], P(None, 'pipe'), may hold values from -2 to 2
- gain_two: bfloat16 [2, 512], P(None, 'pipe'), may hold values from 0.25 to 1.75
- shift_two: bfloat16 [2, 512], P(None, 'pipe'), may hold values from -2 to 2
- segment_ids: int32 [32, 512], P('dp'), may hold values from 0 to 7, never falling along the last dimension, each value on 1 to 256 neighbouring positions
Outputs:
- boundary_out: float32 [2, 16384, 512], P('pipe', 'dp')
- grad_positions: float32 [2, 512, 512], P(None, 'pipe')
- grad_w_in: float32 [2, 512, 1536], P(None, 'pipe')
- grad_qv_bias: float32 [2, 1024], P(None, 'pipe')
- grad_w_out: float32 [2, 512, 512], P(None, 'pipe')
- grad_out_bias: float32 [2, 512], P(None, 'pipe')
- grad_gain_one: float32 [2, 512], P(None, 'pipe')
- grad_shift_one: float32 [2, 512], P(None, 'pipe')
- grad_w_up: float32 [2, 512, 2048], P(None, 'pipe')
- grad_up_bias: float32 [2, 2048], P(None, 'pipe')
- grad_w_down: float32 [2, 2048, 512], P(None, 'pipe')
- grad_down_bias: float32 [2, 512], P(None, 'pipe')
- grad_gain_two: float32 [2, 512], P(None, 'pipe')
- grad_shift_two: float32 [2, 512], P(None, 'pipe')
The draws below stay inside these ranges and needn't reach their ends.
Inputs may be any that keep to these rules, and one draw needn't show every extreme that they name: `segment_ids`: within each window the document numbers never fall; every document has 1 to 256 bytes and one of each window has exactly 256.
All inputs are finite; a program needn't handle non-finite values.
Results may differ from the reference program's by a relative error of at most 0.03.
Values may be sent and summed in bfloat16 or wider, within the bound.
No kernel may reach another device: no remote copies, remote signals or barrier semaphores. Data moves between devices by JAX's collectives and lax.ppermute only.
A program may use at most 192 MiB of HBM per device.

```python
import math
import jax
import jax.numpy as jnp
import numpy as np
from jax import lax

D = 512
HEADS = 8
HEAD = 64
FF = 2048
WIN = 512
LAYERS = 2
WINDOWS = 32
TOKENS = 16384
N_PIPE = 2


def block_scale(rng, dims, cuts, least, high):
    def one(dim, parts):
        heights = jax.random.uniform(jax.random.fold_in(jax.random.fold_in(rng, 6), dim), (parts,), jnp.float32, least / len(cuts), high / len(cuts))
        return jnp.repeat(jnp.exp(heights), dims[dim] // parts).reshape((-1,) + (1,) * (len(dims) - dim - 1))

    factor_of = one(*cuts[0])
    for cut in cuts[1:]:
        factor_of = factor_of * one(*cut)
    return factor_of


def profile(count, total, reach, skew):
    weights = [(1 << 20) // math.isqrt(rank ** skew) + 1 for rank in range(2, count + 1)]
    spare, counts = total - reach - (count - 1), [1] * (count - 1)
    while spare > 0:
        movable = [i for i in range(count - 1) if counts[i] < reach]
        pool, budget = sum([weights[i] for i in movable]), spare
        for i in movable:
            addition = min(reach - counts[i], max(1, budget * weights[i] // pool), spare)
            counts[i] = counts[i] + addition
            spare = spare - addition
    return np.array([reach] + counts)


def uneven_parts(rng, amount, total, limit, skew):
    if amount == 2:
        one = jax.random.randint(rng, (), max(1, total - limit), min(limit, total - 1) + 1)
        return jnp.stack([one, total - one])
    lengths = jnp.asarray(profile(amount, total, limit, skew), jnp.int32)
    twos = (amount - 1) // 2
    giver, receiver = lengths[1:1 + 2 * twos:2], lengths[2:2 + 2 * twos:2]
    margin = jnp.minimum(giver - 1, limit - receiver)
    moved = jax.random.randint(jax.random.fold_in(rng, 1), (twos,), 0, 1 << 20) % (margin + 1)
    lengths = lengths.at[1:1 + 2 * twos:2].set(giver - moved).at[2:2 + 2 * twos:2].set(receiver + moved)
    return lengths[jax.random.permutation(jax.random.fold_in(rng, 2), amount)]


def gaussian(key, shape, width, limit, cuts=(), kind=jnp.bfloat16):
    entries = jax.random.normal(key, shape, jnp.float32) * width
    if len(cuts) > 0:
        entries = block_scale(key, shape, cuts, -0.22, 0.18) * entries
    return jnp.clip(entries, min=-limit, max=limit).astype(kind)


def setup_inputs(seed: int = 0) -> dict:
    arg_keys = jax.random.split(jax.random.key(seed), 16)
    return {
        "boundary": gaussian(arg_keys[0], (N_PIPE, TOKENS, D), 1.0, 6.0, ((0, 2), (1, 16)), jnp.float32),
        "positions": gaussian(arg_keys[1], (LAYERS, WIN, D), 0.5, 3.0, ((1, 2),)),
        "w_in": gaussian(arg_keys[2], (LAYERS, D, 3 * D), D ** -0.5, 0.25, ((1, 2),)),
        "qv_bias": gaussian(arg_keys[3], (LAYERS, 2 * D), 0.5, 3.0, ((1, 2),)),
        "w_out": gaussian(arg_keys[4], (LAYERS, D, D), (D // 16) ** -0.5, 1.0, ((1, 2),)),
        "out_bias": gaussian(arg_keys[5], (LAYERS, D), 0.3, 2.0, ((1, 2),)),
        "gain_one": jnp.clip(1.0 + 0.15 * jax.random.normal(arg_keys[6], (LAYERS, D), jnp.float32), 0.25, 1.75).astype(jnp.bfloat16),
        "shift_one": gaussian(arg_keys[7], (LAYERS, D), 0.3, 2.0, ((1, 2),)),
        "w_up": gaussian(arg_keys[8], (LAYERS, D, FF), D ** -0.5, 0.25, ((1, 2),)),
        "up_bias": gaussian(arg_keys[9], (LAYERS, FF), 0.5, 3.0, ((1, 2),)),
        "w_down": gaussian(arg_keys[10], (LAYERS, FF, D), FF ** -0.5, 0.125, ((1, 2),)),
        "down_bias": gaussian(arg_keys[11], (LAYERS, D), 0.3, 2.0, ((1, 2),)),
        "gain_two": jnp.clip(1.0 + 0.15 * jax.random.normal(arg_keys[12], (LAYERS, D), jnp.float32), 0.25, 1.75).astype(jnp.bfloat16),
        "shift_two": gaussian(arg_keys[13], (LAYERS, D), 0.3, 2.0, ((1, 2),)),
        "segment_ids": jax.vmap(lambda own: jnp.searchsorted(jnp.cumsum(uneven_parts(own, 8, WIN, WIN // 2, 2)), jnp.arange(WIN), side="right"))(jax.random.split(arg_keys[14], WINDOWS)).reshape((WINDOWS, WIN)).astype(jnp.int32),
    }


@jax.custom_vjp
def low(v):
    return lax.optimization_barrier(v.astype(jnp.bfloat16)).astype(jnp.float32)

@jax.custom_vjp
def low_back(v):
    return v

def low_keep(v):
    return (low(v), None)

def low_pass(kept, grad):
    return (grad,)

def back_keep(v):
    return (v, None)

def back_low(kept, grad):
    return (low(grad),)
low.defvjp(low_keep, low_pass)
low_back.defvjp(back_keep, back_low)
highest_precision = lax.Precision.HIGHEST
masked_score = -1e+30
norm_epsilon = 1e-05

def layer_norm(values, norm_gain, norm_shift):
    average = lax.optimization_barrier(jnp.mean(values, axis=-1, keepdims=True))
    centred = values - average
    variance = lax.optimization_barrier(jnp.mean(centred * centred, axis=-1, keepdims=True))
    return centred * lax.rsqrt(variance + norm_epsilon) * norm_gain + norm_shift

def one_layer(inputs, segments, params, layer_index):
    positions, w_in, qv_bias, w_out, out_bias, gain_one, shift_one, w_up, up_bias, w_down, down_bias, gain_two, shift_two = [array_in[layer_index] for array_in in params]
    window_count = inputs.shape[0]
    shifted = inputs + positions
    lowered = low(shifted)
    bias_all = jnp.concatenate([qv_bias[:D], jnp.zeros((D,), jnp.float32), qv_bias[D:]])
    projected = low_back(low(jnp.einsum('bwd,de->bwe', lowered, w_in, precision=highest_precision) + bias_all))
    projected = projected.reshape(window_count, WIN, 3, HEADS, HEAD)
    queries = projected[:, :, 0]
    keys_all = projected[:, :, 1]
    values_all = projected[:, :, 2]
    score_scale = 1.0 / math.sqrt(HEAD)
    scores = low_back(jnp.einsum('bqhe,bkhe->bhqk', queries, keys_all, precision=highest_precision) * score_scale)
    row_index = jnp.arange(WIN)
    allowed = (segments[:, :, None] == segments[:, None, :]) & (row_index[:, None] >= row_index[None, :])
    scores = jnp.where(allowed[:, None], scores, masked_score)
    weights_soft = low(jax.nn.softmax(scores, axis=-1))
    attended = low_back(low(jnp.einsum('bhqk,bkhe->bqhe', weights_soft, values_all, precision=highest_precision)))
    attended = attended.reshape(window_count, WIN, D)
    branch = low_back(jnp.einsum('bwd,de->bwe', attended, w_out, precision=highest_precision) + out_bias)
    hidden = layer_norm(shifted + branch, gain_one, shift_one)
    pre_act = low_back(jnp.einsum('bwd,df->bwf', low(hidden), w_up, precision=highest_precision) + up_bias)
    activated = low(jax.nn.gelu(pre_act))
    feed_out = low_back(jnp.einsum('bwf,fd->bwd', activated, w_down, precision=highest_precision) + down_bias)
    return layer_norm(hidden + feed_out, gain_two, shift_two)

def all_layers(inputs, segments, params):
    middle = inputs
    for layer_index in range(LAYERS):
        if layer_index > 0:
            middle = low_back(low(middle))
        middle = one_layer(middle, segments, params, layer_index)
    return middle

def reference(boundary, positions, w_in, qv_bias, w_out, out_bias, gain_one, shift_one, w_up, up_bias, w_down, down_bias, gain_two, shift_two, segment_ids):
    params = tuple((array_in.astype(jnp.float32) for array_in in (positions, w_in, qv_bias, w_out, out_bias, gain_one, shift_one, w_up, up_bias, w_down, down_bias, gain_two, shift_two)))
    group_size = math.gcd(WINDOWS, 8)
    rounds = WINDOWS // group_size
    inputs = boundary[0].astype(jnp.float32).reshape(rounds, group_size, WIN, D)
    cotangent = boundary[1].astype(jnp.float32).reshape(rounds, group_size, WIN, D)
    segments_all = segment_ids.reshape(rounds, group_size, WIN)

    def accumulate(totals, block_items):
        block_in, block_cot, block_seg = block_items

        def forward_block(inputs_here, params_here):
            return all_layers(inputs_here, block_seg, params_here)
        outputs, pullback = jax.vjp(forward_block, block_in, params)
        grad_in, grad_params = pullback(block_cot)
        return (jax.tree.map(jnp.add, totals, grad_params), (outputs, grad_in))
    zero_totals = jax.tree.map(jnp.zeros_like, params)
    totals, (outputs, grad_in) = lax.scan(accumulate, zero_totals, (inputs, cotangent, segments_all))
    boundary_out = jnp.stack([grad_in.reshape(TOKENS, D), outputs.reshape(TOKENS, D)])
    grad_positions, grad_w_in, grad_qv_bias, grad_w_out, grad_out_bias, grad_gain_one, grad_shift_one, grad_w_up, grad_up_bias, grad_w_down, grad_down_bias, grad_gain_two, grad_shift_two = totals
    return (boundary_out, grad_positions, grad_w_in, grad_qv_bias, grad_w_out, grad_out_bias, grad_gain_one, grad_shift_one, grad_w_up, grad_up_bias, grad_w_down, grad_down_bias, grad_gain_two, grad_shift_two)
```

```python
import functools
import math

import jax
import jax.numpy as jnp
from jax import lax
from jax.experimental import pallas as pl
from jax.experimental.pallas import tpu as pltpu
from jax.sharding import PartitionSpec as P

HEADS = 8
EPS = 1e-05
MASKED = -1e30
REACH = 256
BLOCK = 128
F32, BF16 = jnp.float32, jnp.bfloat16
GELU_C = math.sqrt(2.0 / math.pi)
VMEM_LIMIT = 58 * 1024 * 1024


def nn(a, b):
    return lax.dot_general(a, b, (((1,), (0,)), ((), ())), preferred_element_type=F32)


def nt(a, b):
    return lax.dot_general(a, b, (((1,), (1,)), ((), ())), preferred_element_type=F32)


def col_sums(x):
    return jnp.sum(x.reshape(x.shape[0] // 8, 8, x.shape[1]), axis=0)


def by_rows(rows, chunk, body, init=0, unroll=1):
    def step(i, carry):
        return body(pl.ds(pl.multiple_of(i * chunk, chunk), chunk), carry)

    return lax.fori_loop(0, rows // chunk, step, init, unroll=unroll)


class Copies:
    def __init__(self, sems):
        self.sems, self.count, self.open = sems, 0, []

    def start(self, source, target):
        copy = pltpu.make_async_copy(source, target, self.sems.at[self.count])
        copy.start()
        self.count += 1
        self.open.append(copy)
        return copy

    def wait(self, *copies):
        for copy in copies:
            copy.wait()
            self.open = [c for c in self.open if c is not copy]

    def finish(self):
        self.wait(*list(self.open))


class Vectors:
    def __init__(self, own, other, part, sizes):
        self.own, self.other, self.part, self.sizes = own, other, part, sizes

    def get(self, layer, name):
        at = 0
        for key, size in self.sizes:
            if key == name:
                break
            at += size
        own = self.own[:, at : at + size].astype(F32)[layer : layer + 1]
        other = self.other[:, at : at + size].astype(F32)[layer : layer + 1]
        low = jnp.where(self.part == 0, own, other)
        high = jnp.where(self.part == 0, other, own)
        return jnp.concatenate([low, high], axis=1)


def halves_in(copies, own, other, layer, target, part):
    rows = own.shape[1]
    mine = pl.ds(pl.multiple_of(part * rows, rows), rows)
    theirs = pl.ds(pl.multiple_of((1 - part) * rows, rows), rows)
    return (
        copies.start(own.at[layer], target.at[mine]),
        copies.start(other.at[layer], target.at[theirs]),
    )


def pack_vectors(vectors, part, keep_ref, send_ref):
    keep, send = [], []
    for vector in vectors:
        half = vector.shape[1] // 2
        low, high = vector[:, :half], vector[:, half:]
        mine = jnp.where(part == 0, low, high)
        theirs = jnp.where(part == 0, high, low)
        for j in range(half // 128):
            keep.append(mine[:, j * 128 : (j + 1) * 128])
            send.append(theirs[:, j * 128 : (j + 1) * 128])
    spare = jnp.zeros((keep_ref.shape[0] - len(keep), 128), F32)
    keep_ref[...] = jnp.concatenate(keep + [spare], axis=0).astype(keep_ref.dtype)
    send_ref[...] = jnp.concatenate(send + [spare], axis=0).astype(send_ref.dtype)


def norm_stats(r):
    centred = r - jnp.mean(r, axis=-1, keepdims=True)
    scale = lax.rsqrt(jnp.mean(centred * centred, axis=-1, keepdims=True) + EPS)
    return centred * scale, scale


def norm_backward(r, g, gain):
    xhat, scale = norm_stats(r)
    gy = g * gain
    mean_one = jnp.mean(gy, axis=-1, keepdims=True)
    mean_two = jnp.mean(gy * xhat, axis=-1, keepdims=True)
    return scale * (gy - mean_one - xhat * mean_two), col_sums(g * xhat), col_sums(g)


def key_range(i):
    return max(0, i * BLOCK + 1 - REACH) // BLOCK * BLOCK, (i + 1) * BLOCK


def head_masks(scale):
    lane = lax.broadcasted_iota(jnp.int32, (1, 128), 1)
    first = jnp.where(lane < 64, scale, 0.0).astype(BF16)
    second = jnp.where(lane < 64, 0.0, scale).astype(BF16)
    return first, second


def stacked(x, masks):
    return jnp.concatenate([x * masks[0], x * masks[1]], axis=0)


def write_bias(seg_ref, bias_ref):
    length = seg_ref.shape[1]
    seg = seg_ref[...].astype(F32)
    columns = jnp.broadcast_to(seg, (128, length))
    for j in range(length // 128):
        rows = pl.ds(j * 128, 128)
        own = jnp.broadcast_to(jnp.transpose(columns[:, j * 128 : (j + 1) * 128])[:, :1], (128, length))
        key = lax.broadcasted_iota(jnp.int32, (128, length), 0) + j * 128
        query = lax.broadcasted_iota(jnp.int32, (128, length), 1)
        bias_ref[rows, :] = jnp.where((own == seg) & (key <= query), 0.0, MASKED)


def attention_core(qkv_ref, vt_ref, bias_ref, p_ref, ot_ref, width):
    masks = head_masks(1.0 / math.sqrt(width // HEADS))
    length = qkv_ref.shape[0]
    for pair in range(HEADS // 2):
        lanes = slice(pair * 128, (pair + 1) * 128)
        for i in range(length // BLOCK):
            low, high = key_range(i)
            queries = slice(i * BLOCK, (i + 1) * BLOCK)
            q = stacked(qkv_ref[queries, lanes], masks)
            k = qkv_ref[low:high, width + pair * 128 : width + (pair + 1) * 128]
            bias = bias_ref[low:high, queries]
            s = nt(k, q) + jnp.concatenate([bias, bias], axis=1)
            e = jnp.exp(s - jnp.max(s, axis=0, keepdims=True))
            p = (e * (1.0 / jnp.sum(e, axis=0, keepdims=True))).astype(BF16)
            p_ref[pair * (length // BLOCK) + i, : high - low, :] = p
            o = nn(vt_ref[lanes, low:high], p)
            ot_ref[pair * 128 : pair * 128 + 64, queries] = o[:64, :BLOCK].astype(BF16)
            ot_ref[pair * 128 + 64 : pair * 128 + 128, queries] = o[64:, BLOCK:].astype(BF16)


def attention_forward(u_ref, ub_ref, w_in, w_out, vectors, layer, seg_ref, s):
    length, width = u_ref.shape
    qv = vectors.get(layer, "qv_bias")
    for j in range(3):
        bias = (qv[:, :width], 0.0, qv[:, width:])[j]
        cols = slice(j * width, (j + 1) * width)
        s.qkv[:, cols] = (nn(ub_ref[...], w_in[:, cols]) + bias).astype(BF16)
    s.vt[...] = jnp.transpose(s.qkv[:, 2 * width :])
    write_bias(seg_ref, s.bias)
    attention_core(s.qkv, s.vt, s.bias, s.p, s.ot, width)
    out_bias = vectors.get(layer, "out_bias")
    gain, shift = vectors.get(layer, "gain_one"), vectors.get(layer, "shift_one")
    o = jnp.transpose(s.ot[...])
    s.r1[...] = nn(o, w_out[...])

    def rows(at, carry):
        r = u_ref[at, :] + (s.r1[at, :] + out_bias)
        s.r1[at, :] = r
        h = norm_stats(r)[0] * gain + shift
        s.h[at, :] = h
        s.hb[at, :] = h.astype(BF16)
        return carry

    by_rows(length, 64, rows)


def feed_forward(h_ref, hb_ref, w_up, w_down, vectors, layer, s, finish):
    length, width = h_ref.shape
    hidden = w_up.shape[1]
    up_bias = vectors.get(layer, "up_bias")
    tile = 512
    for j in range(hidden // tile):
        cols = slice(j * tile, (j + 1) * tile)
        bias = up_bias[:, cols]
        s.z[j % 2] = nn(hb_ref[...], w_up[:, cols])

        def rows(at, carry, j=j, cols=cols, bias=bias):
            v = s.z[j % 2, at, :] + bias
            v2 = v * v
            half = 0.5 + 0.5 * jnp.tanh(v * (GELU_C + (GELU_C * 0.044715) * v2))
            m = v * half
            s.m[at, cols] = m.astype(BF16)
            slope = half + m * (1.0 - half) * (2 * GELU_C + (6 * GELU_C * 0.044715) * v2)
            s.d[at, cols] = slope.astype(BF16)
            return carry

        by_rows(length, 32, rows)
    s.r2[...] = nn(s.m[...], w_down[...])
    down_bias = vectors.get(layer, "down_bias")
    gain, shift = vectors.get(layer, "gain_two"), vectors.get(layer, "shift_two")

    def last(at, carry):
        r = h_ref[at, :] + (s.r2[at, :] + down_bias)
        s.r2[at, :] = r
        finish(at, norm_stats(r)[0] * gain + shift)
        return carry

    by_rows(length, 64, last)


def feed_backward(g_ref, r2_ref, hb_ref, m_ref, d_ref, w_up, w_down, vectors, layer, part, s):
    length, width = r2_ref.shape
    hidden = w_up.shape[1]
    gain = vectors.get(layer, "gain_two")
    zero = jnp.zeros((8, width), F32)

    def rows(at, carry):
        dr, d_gain, d_shift = norm_backward(r2_ref[at, :], g_ref[at, :].astype(F32), gain)
        df = dr.astype(BF16)
        s.dh[at, :] = dr
        s.df[at, :] = df
        return carry[0] + d_gain, carry[1] + d_shift, carry[2] + col_sums(df.astype(F32))

    d_gain, d_shift, d_down = by_rows(length, 64, rows, (zero, zero, zero))
    tile = 512
    d_up = []
    for j in range(hidden // tile):
        cols = slice(j * tile, (j + 1) * tile)
        s.z[j % 2] = nt(s.df[...], w_down[cols, :])

        def scale(at, carry, j=j, cols=cols):
            dz = (s.z[j % 2, at, :] * d_ref[at, cols].astype(F32)).astype(BF16)
            s.dz[at, cols] = dz
            return carry + col_sums(dz.astype(F32))

        d_up.append(by_rows(length, 64, scale, jnp.zeros((8, tile), F32)))
    half = width // 2
    s.hbt[...] = jnp.transpose(hb_ref[...])
    for which, target in ((part, s.up_keep), (1 - part, s.up_send)):
        left = s.hbt[pl.ds(pl.multiple_of(which * half, half), half), :]
        for j in range(hidden // tile):
            cols = slice(j * tile, (j + 1) * tile)
            target[:, cols] = nn(left, s.dz[:, cols]).astype(BF16)
    half = hidden // 2
    for which, target in ((part, s.down_keep), (1 - part, s.down_send)):
        for j in range(half // 256):
            at = pl.multiple_of(which * half + j * 256, 256)
            left = jnp.transpose(m_ref[:, pl.ds(at, 256)])
            target[j * 256 : (j + 1) * 256, :] = nn(left, s.df[...]).astype(BF16)
    s.dh[...] += nt(s.dz[...], w_up[...])
    summed = [jnp.sum(x, axis=0, keepdims=True) for x in [jnp.concatenate(d_up, axis=1), d_down, d_gain, d_shift]]
    pack_vectors(summed, part, s.vec_keep, s.vec_send)


def attention_backward(dh_ref, r1_ref, ub_ref, ot_ref, qkv_ref, p_ref, w_in, w_out, vectors, layer, part, s):
    length, width = r1_ref.shape
    gain = vectors.get(layer, "gain_one")
    zero = jnp.zeros((8, width), F32)

    def rows(at, carry):
        dr, d_gain, d_shift = norm_backward(r1_ref[at, :], dh_ref[at, :], gain)
        da = dr.astype(BF16)
        s.du[at, :] = dr
        s.da[at, :] = da
        return carry[0] + d_gain, carry[1] + d_shift, carry[2] + col_sums(da.astype(F32))

    d_gain, d_shift, d_out = by_rows(length, 64, rows, (zero, zero, zero))
    s.do[...] = nt(s.da[...], w_out[...]).astype(BF16)
    half = width // 2
    for which, target in ((part, s.a_keep), (1 - part, s.a_send)):
        at = pl.ds(pl.multiple_of(which * half, half), half)
        target[:, :width] = nn(ot_ref[at, :], s.da[...]).astype(BF16)
    s.kt[...] = jnp.transpose(qkv_ref[:, width : 2 * width])
    scale = 1.0 / math.sqrt(width // HEADS)
    q_masks, o_masks = head_masks(scale), head_masks(1.0)
    blocks = length // BLOCK
    for pair in range(HEADS // 2):
        lanes = slice(pair * 128, (pair + 1) * 128)
        k_lanes = slice(width + pair * 128, width + (pair + 1) * 128)
        v_lanes = slice(2 * width + pair * 128, 2 * width + (pair + 1) * 128)
        dk = [jnp.zeros((BLOCK, 128), F32)] * blocks
        dv = [jnp.zeros((BLOCK, 128), F32)] * blocks
        for i in range(blocks):
            low, high = key_range(i)
            queries = slice(i * BLOCK, (i + 1) * BLOCK)
            q = stacked(qkv_ref[queries, lanes], q_masks)
            do = stacked(s.do[queries, lanes], o_masks)
            pb = p_ref[pair * blocks + i, : high - low, :]
            p = pb.astype(F32)
            dp = nt(qkv_ref[low:high, v_lanes], do)
            ds = (p * (dp - jnp.sum(dp * p, axis=0, keepdims=True))).astype(BF16)
            more_v, more_k = nn(pb, do), nn(ds, q)
            for b in range(low // BLOCK, high // BLOCK):
                piece = slice(b * BLOCK - low, (b + 1) * BLOCK - low)
                dk[b] = dk[b] + more_k[piece]
                dv[b] = dv[b] + more_v[piece]
            dq = nn(s.kt[lanes, low:high], ds) * scale
            s.dqt[pair * 128 : pair * 128 + 64, queries] = dq[:64, :BLOCK].astype(BF16)
            s.dqt[pair * 128 + 64 : pair * 128 + 128, queries] = dq[64:, BLOCK:].astype(BF16)
        for b in range(blocks):
            s.dqkv[b * BLOCK : (b + 1) * BLOCK, k_lanes] = dk[b].astype(BF16)
            s.dqkv[b * BLOCK : (b + 1) * BLOCK, v_lanes] = dv[b].astype(BF16)
    s.dqkv[:, :width] = jnp.transpose(s.dqt[...])

    def sums(at, carry):
        return (
            carry[0] + col_sums(s.dqkv[at, :width].astype(F32)),
            carry[1] + col_sums(s.dqkv[at, 2 * width :].astype(F32)),
        )

    d_query, d_value = by_rows(length, 64, sums, (zero, zero))
    s.du[...] += nt(s.dqkv[...], w_in[...])
    s.ubt[...] = jnp.transpose(ub_ref[...])
    for which, target, position in ((part, s.in_keep, s.a_keep), (1 - part, s.in_send, s.a_send)):
        at = pl.ds(pl.multiple_of(which * half, half), half)
        left = s.ubt[at, :]
        for j in range(3):
            cols = slice(j * width, (j + 1) * width)
            target[:, cols] = nn(left, s.dqkv[:, cols]).astype(BF16)
        position[:, width : 2 * width] = s.du[at, :].astype(BF16)
    summed = [jnp.concatenate([d_query, d_value], axis=1), d_out, d_gain, d_shift]
    pack_vectors([jnp.sum(x, axis=0, keepdims=True) for x in summed], part, s.vec_keep, s.vec_send)


class Names:
    pass


def call(name, body, inputs, outputs, scratch, flops):
    names_in, names_out, names_scratch = list(inputs), list(outputs), list(scratch)

    def kernel(*refs):
        groups = []
        at = 0
        for names in (names_in, names_out, names_scratch):
            group = Names()
            for key in names:
                setattr(group, key, refs[at])
                at += 1
            groups.append(group)
        copies = Copies(refs[at])
        body(*groups, copies)
        copies.finish()

    moved = sum(math.prod(x.shape) * x.dtype.itemsize for x in list(inputs.values()) + list(outputs.values()))
    results = pl.pallas_call(
        kernel,
        name=name,
        out_shape=tuple(outputs.values()),
        in_specs=[pl.BlockSpec(memory_space=pl.ANY)] * len(inputs),
        out_specs=tuple([pl.BlockSpec(memory_space=pl.ANY)] * len(outputs)),
        scratch_shapes=[pltpu.VMEM(x.shape, x.dtype) for x in scratch.values()] + [pltpu.SemaphoreType.DMA((48,))],
        compiler_params=pltpu.CompilerParams(vmem_limit_bytes=VMEM_LIMIT),
        cost_estimate=pl.CostEstimate(flops=flops, bytes_accessed=moved, transcendentals=0),
    )(*inputs.values())
    return dict(zip(names_out, results))


def shape(dims, dtype):
    return jax.ShapeDtypeStruct(tuple(dims), dtype)


EXCHANGES = {"x": 1, "y": 2, "z": 4, "w": 8}


def mirrored(value, axis, distance):
    size = lax.axis_size(axis)
    return lax.ppermute(value, axis, [(i, i ^ distance) for i in range(size)])


def side(axis, distance):
    return (lax.axis_index(axis) // distance) % 2


def reduce_over(value, axis, order):
    for distance in order[:-1]:
        half = value.shape[0] // 2
        bit = side(axis, distance)
        theirs = lax.dynamic_slice_in_dim(value, (1 - bit) * half, half, 0)
        mine = lax.dynamic_slice_in_dim(value, bit * half, half, 0)
        value = mine + mirrored(theirs, axis, distance)
    value = value + mirrored(value, axis, order[-1])
    for distance in order[-2::-1]:
        other = mirrored(value, axis, distance)
        low = side(axis, distance) == 0
        value = jnp.concatenate([jnp.where(low, value, other), jnp.where(low, other, value)], axis=0)
    return value


def orders(size):
    bits = [1 << i for i in range(size.bit_length() - 1)]
    side_bits = (len(bits) - 1) // 3
    xs, ys, zs = bits[:side_bits], bits[side_bits : 2 * side_bits], bits[2 * side_bits :]
    return xs + zs[:1] + ys + zs[1:], ys + zs[:1] + xs + zs[1:]


def per_device(
    boundary,
    positions,
    w_in,
    qv_bias,
    w_out,
    out_bias,
    gain_one,
    shift_one,
    w_up,
    up_bias,
    w_down,
    down_bias,
    gain_two,
    shift_two,
    segment_ids,
):
    part = lax.axis_index("pipe")
    window_count, length = segment_ids.shape
    layers, half, width = positions.shape
    hidden = w_up.shape[2]
    blocks = length // BLOCK

    def other_core(x):
        return mirrored(x, "pipe", 1)

    small = (qv_bias, out_bias, gain_one, shift_one, up_bias, down_bias, gain_two, shift_two)
    small_names = ("qv_bias", "out_bias", "gain_one", "shift_one", "up_bias", "down_bias", "gain_two", "shift_two")
    sizes = [(key, x.shape[1]) for key, x in zip(small_names, small)]
    vec = jnp.concatenate(small, axis=1)
    windows = boundary.reshape(window_count, length, width)
    got = other_core(lax.dynamic_index_in_dim(windows, 1 - part, 0, keepdims=False))
    vec2, pos2, w_in2, w_out2 = other_core(vec), other_core(positions), other_core(w_in), other_core(w_out)
    w_up2, w_down2 = other_core(w_up), other_core(w_down)
    seg = lax.dynamic_index_in_dim(segment_ids, part, 0, keepdims=True)

    square, wide = (length, width), (length, hidden)
    qkv_shape, p_shape = (length, 3 * width), (HEADS // 2 * blocks, min(length, REACH + BLOCK), 2 * BLOCK)
    vec_in = dict(vec=vec, vec2=vec2)
    vec_scratch = dict(vec=shape(vec.shape, BF16), vec2=shape(vec.shape, BF16))
    attention_in = dict(pos=positions, pos2=pos2, w_in=w_in, w_in2=w_in2, w_out=w_out, w_out2=w_out2, seg=seg)
    attention_out = dict(
        ub=shape(square, BF16), qkv=shape(qkv_shape, BF16), p=shape(p_shape, BF16), ot=shape(square, BF16),
        r1=shape(square, F32),
    )
    attention_scratch = dict(
        pos=shape(square, BF16), w_in=shape((width, 3 * width), BF16), w_out=shape((width, width), BF16),
        seg=shape(seg.shape, seg.dtype), u=shape(square, F32), ub=shape(square, BF16), qkv=shape(qkv_shape, BF16),
        vt=shape(square, BF16), bias=shape((length, length), F32), p=shape(p_shape, BF16), ot=shape(square, BF16),
        r1=shape(square, F32), h=shape(square, F32), hb=shape(square, BF16),
    )
    feed_in = dict(w_up=w_up, w_up2=w_up2, w_down=w_down, w_down2=w_down2)
    feed_weights = dict(w_up=shape((width, hidden), BF16), w_down=shape((hidden, width), BF16))
    feed_scratch = dict(
        z=shape((2, length, 512), F32), m=shape(wide, BF16), d=shape(wide, BF16), r2=shape(square, F32)
    )
    vec_grads = dict(vec_keep=shape((16, 128), BF16), vec_send=shape((16, 128), BF16))
    feed_grads = dict(
        up_keep=shape((half, hidden), BF16), up_send=shape((half, hidden), BF16),
        down_keep=shape((hidden // 2, width), BF16), down_send=shape((hidden // 2, width), BF16), **vec_grads,
    )
    attention_grads = dict(
        a_keep=shape((half, 2 * width), BF16), a_send=shape((half, 2 * width), BF16),
        in_keep=shape((half, 3 * width), BF16), in_send=shape((half, 3 * width), BF16), **vec_grads,
    )
    flops_attention = 2 * length * width * (4 * width + length)
    flops_feed = 4 * length * width * hidden

    def vectors_of(i, s, copies, place):
        copies.wait(copies.start(i.vec, s.vec), copies.start(i.vec2, s.vec2))
        return Vectors(s.vec, s.vec2, place, sizes)

    def both_windows(i, s, copies, place):
        at = pl.ds(pl.multiple_of(place * length, length), length)
        return copies.start(i.rows.at[0, at], s.xg.at[place]), copies.start(i.got, s.xg.at[1 - place])

    def attention_first(i, o, s, copies):
        place = lax.axis_index("pipe")
        x = both_windows(i, s, copies, place)
        pos = halves_in(copies, i.pos, i.pos2, 0, s.pos, place)
        win = halves_in(copies, i.w_in, i.w_in2, 0, s.w_in, place)
        seg_copy = copies.start(i.seg, s.seg)
        wout = halves_in(copies, i.w_out, i.w_out2, 0, s.w_out, place)
        vectors = vectors_of(i, s, copies, place)
        copies.wait(*x, *pos)

        def rows(at, carry):
            u = s.xg[0, at, :] + s.pos[at, :].astype(F32)
            s.u[at, :] = u
            s.ub[at, :] = u.astype(BF16)
            return carry

        by_rows(length, 64, rows)
        copies.start(s.ub, o.ub)
        copies.wait(*win, *wout, seg_copy)
        attention_forward(s.u, s.ub, s.w_in, s.w_out, vectors, 0, s.seg, s)
        for key in ("qkv", "p", "ot", "r1", "h"):
            copies.start(getattr(s, key), getattr(o, key))

    first = call(
        "attention_first", attention_first,
        dict(rows=boundary, got=got, **vec_in, **attention_in),
        dict(**attention_out, h=shape(square, F32)),
        dict(xg=shape((2,) + square, F32), **vec_scratch, **attention_scratch),
        flops_attention,
    )

    def middle(i, o, s, copies):
        place = lax.axis_index("pipe")
        h_in = copies.start(i.h, s.h0)
        up = halves_in(copies, i.w_up, i.w_up2, 0, s.w_up, place)
        down = halves_in(copies, i.w_down, i.w_down2, 0, s.w_down, place)
        vectors = vectors_of(i, s, copies, place)
        pos = halves_in(copies, i.pos, i.pos2, 1, s.pos, place)
        win = halves_in(copies, i.w_in, i.w_in2, 1, s.w_in, place)
        wout = halves_in(copies, i.w_out, i.w_out2, 1, s.w_out, place)
        seg_copy = copies.start(i.seg, s.seg)
        last_up = halves_in(copies, i.w_up, i.w_up2, 1, s.last_up, place)
        last_down = halves_in(copies, i.w_down, i.w_down2, 1, s.last_down, place)
        xg = both_windows(i, s, copies, place)
        copies.wait(h_in, *up, *down, *pos)

        def lower(at, carry):
            s.hb0[at, :] = s.h0[at, :].astype(BF16)
            return carry

        by_rows(length, 64, lower)

        def next_input(at, y):
            u = y.astype(BF16).astype(F32) + s.pos[at, :].astype(F32)
            s.u[at, :] = u
            s.ub[at, :] = u.astype(BF16)

        feed_forward(s.h0, s.hb0, s.w_up, s.w_down, vectors, 0, s, next_input)
        kept = [copies.start(getattr(s, a), getattr(o, b)) for a, b in (("m", "m0"), ("d", "d0"), ("r2", "r20"), ("hb0", "hb0"), ("ub", "ub"))]
        copies.wait(*win, *wout, seg_copy)
        attention_forward(s.u, s.ub, s.w_in, s.w_out, vectors, 1, s.seg, s)
        for key in ("qkv", "p", "ot", "r1"):
            copies.start(getattr(s, key), getattr(o, key))
        copies.wait(*kept, *last_up, *last_down, *xg)

        def result(at, y):
            s.y[at, :] = y

        feed_forward(s.h, s.hb, s.last_up, s.last_down, vectors, 1, s, result)
        copies.start(s.y, o.y)
        feed_backward(s.xg.at[1], s.r2, s.hb, s.m, s.d, s.last_up, s.last_down, vectors, 1, place, s)
        for key in list(feed_grads) + ["dh"]:
            copies.start(getattr(s, key), getattr(o, key))

    mid = call(
        "middle", middle,
        dict(h=first["h"], rows=boundary, got=got, **vec_in, **attention_in, **feed_in),
        dict(
            **attention_out, m0=shape(wide, BF16), d0=shape(wide, BF16), r20=shape(square, F32),
            hb0=shape(square, BF16), y=shape(square, F32), dh=shape(square, F32), **feed_grads,
        ),
        dict(
            h0=shape(square, F32), hb0=shape(square, BF16), xg=shape((2,) + square, F32), **vec_scratch,
            **attention_scratch, **feed_weights, last_up=feed_weights["w_up"], last_down=feed_weights["w_down"],
            **feed_scratch, y=shape(square, F32), dh=shape(square, F32), df=shape(square, BF16),
            dz=shape(wide, BF16), hbt=shape(square, BF16), **feed_grads,
        ),
        flops_attention + 4 * flops_feed,
    )

    def backward_attention(layer, source, dh, extra):
        def body(i, o, s, copies):
            place = lax.axis_index("pipe")
            loads = [copies.start(getattr(i, key), getattr(s, key)) for key in ("dh", "r1")]
            wout = halves_in(copies, i.w_out, i.w_out2, layer, s.w_out, place)
            vectors = vectors_of(i, s, copies, place)
            rest = [copies.start(getattr(i, key), getattr(s, key)) for key in ("ot", "qkv", "p", "ub")]
            win = halves_in(copies, i.w_in, i.w_in2, layer, s.w_in, place)
            copies.wait(*loads, *wout, *rest, *win)
            attention_backward(
                s.dh, s.r1, s.ub, s.ot, s.qkv, s.p, s.w_in, s.w_out, vectors, layer, place, s
            )
            if layer > 0:

                def lower(at, carry):
                    s.g[at, :] = s.du[at, :].astype(BF16)
                    return carry

                by_rows(length, 64, lower)
                copies.start(s.g, o.g)
            else:
                copies.start(s.du, o.du)
            for key in attention_grads:
                copies.start(getattr(s, key), getattr(o, key))

        result = dict(g=shape(square, BF16)) if layer > 0 else dict(du=shape(square, F32))
        return call(
            f"attention_backward_{layer}", body,
            dict(
                dh=dh, **{key: source[key] for key in ("r1", "ot", "qkv", "p", "ub")}, **vec_in,
                w_in=w_in, w_in2=w_in2, w_out=w_out, w_out2=w_out2,
            ),
            dict(**result, **attention_grads),
            dict(
                dh=shape(square, F32), r1=shape(square, F32), ot=shape(square, BF16), qkv=shape(qkv_shape, BF16),
                p=shape(p_shape, BF16), ub=shape(square, BF16), **vec_scratch,
                w_in=shape((width, 3 * width), BF16), w_out=shape((width, width), BF16),
                du=shape(square, F32), da=shape(square, BF16), do=shape(square, BF16), kt=shape(square, BF16),
                dqt=shape(square, BF16), dqkv=shape(qkv_shape, BF16), ubt=shape(square, BF16),
                g=shape(square, BF16), **attention_grads,
            ),
            2 * flops_attention,
        )

    last_attention = backward_attention(1, mid, mid["dh"], None)

    def feed_back(i, o, s, copies):
        place = lax.axis_index("pipe")
        loads = [copies.start(getattr(i, key), getattr(s, key)) for key in ("g", "r2", "d", "hb", "m")]
        down = halves_in(copies, i.w_down, i.w_down2, 0, s.w_down, place)
        up = halves_in(copies, i.w_up, i.w_up2, 0, s.w_up, place)
        vectors = vectors_of(i, s, copies, place)
        copies.wait(*loads, *down, *up)
        feed_backward(s.g, s.r2, s.hb, s.m, s.d, s.w_up, s.w_down, vectors, 0, place, s)
        for key in list(feed_grads) + ["dh"]:
            copies.start(getattr(s, key), getattr(o, key))

    first_feed = call(
        "feed_backward_0", feed_back,
        dict(g=last_attention["g"], r2=mid["r20"], d=mid["d0"], hb=mid["hb0"], m=mid["m0"], **vec_in, **feed_in),
        dict(dh=shape(square, F32), **feed_grads),
        dict(
            g=shape(square, BF16), hb=shape(square, BF16), **vec_scratch, **feed_weights, **feed_scratch,
            dh=shape(square, F32), df=shape(square, BF16), dz=shape(wide, BF16), hbt=shape(square, BF16), **feed_grads,
        ),
        2 * flops_feed,
    )
    first_attention = backward_attention(0, first, first_feed["dh"], None)

    mine = jnp.where(part == 0, mid["y"], first_attention["du"])
    theirs = other_core(mine)
    boundary_out = jnp.stack(
        [jnp.where(part == 0, first_attention["du"], theirs), jnp.where(part == 0, theirs, mid["y"])]
    ).reshape(1, window_count * length, width)

    orders_of = orders(lax.axis_size("dp"))

    def shared(group, key, which):
        total = group[key + "_keep"] + other_core(group[key + "_send"])
        return reduce_over(total, "dp", orders_of[which])

    up = [None, shared(mid, "up", 0)]
    down = [None, shared(mid, "down", 1)]
    inner = [None, shared(last_attention, "in", 0)]
    rest = [None, shared(last_attention, "a", 1)]
    up[0], down[0] = shared(first_feed, "up", 1), shared(first_feed, "down", 0)
    inner[0] = shared(first_attention, "in", 1)
    groups = (first_attention, first_feed, last_attention, mid)
    vec_group = {
        "v" + end: jnp.concatenate([g["vec" + end] for g in groups], axis=0) for end in ("_keep", "_send")
    }
    vec_total = reduce_over(vec_group["v_keep"] + other_core(vec_group["v_send"]), "dp", orders_of[0])
    rest[0] = shared(first_attention, "a", 0)

    def out(pieces):
        return jnp.stack(pieces).astype(F32)

    def vec_out(offset, count):
        rows = [vec_total[at + offset : at + offset + count] for at in (0, 32)]
        return out([r.reshape(count * 128) for r in rows])

    a = width // 256
    u = hidden // 256
    return (
        boundary_out,
        out([r[:, width:] for r in rest]),
        out(inner),
        vec_out(0, 2 * a),
        out([r[:, :width] for r in rest]),
        vec_out(2 * a, a),
        vec_out(3 * a, a),
        vec_out(4 * a, a),
        out(up),
        vec_out(16, u),
        out(down),
        vec_out(16 + u, a),
        vec_out(16 + u + a, a),
        vec_out(16 + u + 2 * a, a),
    )


def solution(mesh):
    rows, vector = P(None, "pipe", None), P(None, "pipe")
    both = P("pipe", "dp", None)
    params = (rows, rows, vector, rows, vector, vector, vector, rows, vector, rows, vector, vector, vector)
    return jax.shard_map(
        per_device,
        mesh=mesh,
        in_specs=(both,) + params + (P("dp", None),),
        out_specs=(both,) + params,
        check_vma=False,
    )
```

```python
import functools
import math

import jax
import jax.numpy as jnp
from jax import lax
from jax.experimental import pallas as pl
from jax.experimental.pallas import tpu as pltpu
from jax.sharding import PartitionSpec as P

HEADS = 8
EPS = 1e-05
MASKED = -1e30
REACH = 256
BLOCK = 128
F32, BF16 = jnp.float32, jnp.bfloat16
GELU_C = math.sqrt(2.0 / math.pi)
VMEM_LIMIT = 58 * 1024 * 1024
ROWS = 512


def nn(a, b):
    return lax.dot_general(a, b, (((1,), (0,)), ((), ())), preferred_element_type=F32)


def nt(a, b):
    return lax.dot_general(a, b, (((1,), (1,)), ((), ())), preferred_element_type=F32)


def col_sums(x):
    return jnp.sum(x.reshape(x.shape[0] // 8, 8, x.shape[1]), axis=0)


def by_rows(rows, chunk, body, init=0, unroll=1):
    def step(i, carry):
        return body(pl.ds(pl.multiple_of(i * chunk, chunk), chunk), carry)

    return lax.fori_loop(0, rows // chunk, step, init, unroll=unroll)


def in_blocks(rows, chunk, body, init=0):
    carry = init
    for at in range(0, rows, chunk):
        carry = body(slice(at, at + chunk), carry)
    return carry


class Copies:
    def __init__(self, sems):
        self.sems, self.count, self.open = sems, 0, []

    def make(self, source, target):
        copy = pltpu.make_async_copy(source, target, self.sems.at[self.count])
        self.count += 1
        self.open.append(copy)
        return copy

    def start(self, source, target):
        copy = self.make(source, target)
        copy.start()
        return copy

    def wait(self, *copies):
        for copy in copies:
            copy.wait()
            self.open = [c for c in self.open if c is not copy]

    def finish(self):
        self.wait(*list(self.open))


class Vectors:
    def __init__(self, own, other, part, sizes):
        self.own, self.other, self.part, self.sizes = own, other, part, sizes

    def get(self, layer, name):
        at = 0
        for key, size in self.sizes:
            if key == name:
                break
            at += size
        own = self.own[:, at : at + size].astype(F32)[layer : layer + 1]
        other = self.other[:, at : at + size].astype(F32)[layer : layer + 1]
        low = jnp.where(self.part == 0, own, other)
        high = jnp.where(self.part == 0, other, own)
        return jnp.concatenate([low, high], axis=1)


def halves_in(copies, own, other, layer, target, part):
    rows = own.shape[1]
    mine = pl.ds(pl.multiple_of(part * rows, rows), rows)
    theirs = pl.ds(pl.multiple_of((1 - part) * rows, rows), rows)
    return (
        copies.start(own.at[layer], target.at[mine]),
        copies.start(other.at[layer], target.at[theirs]),
    )


def pack_vectors(vectors, part, keep_ref, send_ref):
    keep, send = [], []
    for vector in vectors:
        half = vector.shape[1] // 2
        low, high = vector[:, :half], vector[:, half:]
        mine = jnp.where(part == 0, low, high)
        theirs = jnp.where(part == 0, high, low)
        for j in range(half // 128):
            keep.append(mine[:, j * 128 : (j + 1) * 128])
            send.append(theirs[:, j * 128 : (j + 1) * 128])
    spare = jnp.zeros((keep_ref.shape[0] - len(keep), 128), F32)
    keep_ref[...] = jnp.concatenate(keep + [spare], axis=0).astype(keep_ref.dtype)
    send_ref[...] = jnp.concatenate(send + [spare], axis=0).astype(send_ref.dtype)


def norm_stats(r):
    centred = r - jnp.mean(r, axis=-1, keepdims=True)
    scale = lax.rsqrt(jnp.mean(centred * centred, axis=-1, keepdims=True) + EPS)
    return centred * scale, scale


def norm_backward(r, g, gain):
    xhat, scale = norm_stats(r)
    gy = g * gain
    mean_one = jnp.mean(gy, axis=-1, keepdims=True)
    mean_two = jnp.mean(gy * xhat, axis=-1, keepdims=True)
    return scale * (gy - mean_one - xhat * mean_two), col_sums(g * xhat), col_sums(g)


def key_range(i):
    return max(0, i * BLOCK + 1 - REACH) // BLOCK * BLOCK, (i + 1) * BLOCK


def head_masks(scale):
    lane = lax.broadcasted_iota(jnp.int32, (1, 128), 1)
    first = jnp.where(lane < 64, scale, 0.0).astype(BF16)
    second = jnp.where(lane < 64, 0.0, scale).astype(BF16)
    return first, second


def stacked(x, masks):
    return jnp.concatenate([x * masks[0], x * masks[1]], axis=0)


def write_bias(seg_ref, bias_ref):
    length = seg_ref.shape[1]
    seg = seg_ref[...].astype(F32)
    columns = jnp.broadcast_to(seg, (128, length))
    for j in range(length // 128):
        rows = pl.ds(j * 128, 128)
        own = jnp.broadcast_to(jnp.transpose(columns[:, j * 128 : (j + 1) * 128])[:, :1], (128, length))
        key = lax.broadcasted_iota(jnp.int32, (128, length), 0) + j * 128
        query = lax.broadcasted_iota(jnp.int32, (128, length), 1)
        bias_ref[rows, :] = jnp.where((own == seg) & (key <= query), 0.0, MASKED)


def staggered(count, stages):
    held = {}
    for tick in range(count + len(stages) - 1):
        for number, stage in enumerate(stages):
            t = tick - number
            if 0 <= t < count:
                held[t] = stage(t, held.pop(t, None))


def attention_core(qkv_ref, vt_ref, bias_ref, p_ref, ot_ref, width):
    masks = head_masks(1.0 / math.sqrt(width // HEADS))
    blocks = qkv_ref.shape[0] // BLOCK

    def place(t):
        pair, i = divmod(t, blocks)
        low, high = key_range(i)
        return pair * 128, slice(i * BLOCK, (i + 1) * BLOCK), low, high

    def score(t, unused):
        lane, queries, low, high = place(t)
        q = stacked(qkv_ref[queries, lane : lane + 128], masks)
        return nt(qkv_ref[low:high, width + lane : width + lane + 128], q)

    def soften(t, s):
        lane, queries, low, high = place(t)
        bias = bias_ref[low:high, queries]
        s = s + jnp.concatenate([bias, bias], axis=1)
        e = jnp.exp(s - jnp.max(s, axis=0, keepdims=True))
        p = (e * (1.0 / jnp.sum(e, axis=0, keepdims=True))).astype(BF16)
        p_ref[t, : high - low, :] = p
        return p

    def attend(t, p):
        lane, queries, low, high = place(t)
        o = nn(vt_ref[lane : lane + 128, low:high], p)
        ot_ref[lane : lane + 64, queries] = o[:64, :BLOCK].astype(BF16)
        ot_ref[lane + 64 : lane + 128, queries] = o[64:, BLOCK:].astype(BF16)

    staggered(HEADS // 2 * blocks, (score, soften, attend))


def attention_forward(u_ref, ub_ref, w_in, w_out, vectors, layer, seg_ref, s, need, done):
    length, width = u_ref.shape
    need("seg")
    write_bias(seg_ref, s.bias)
    qv = vectors.get(layer, "qv_bias")
    need("w_in")
    for j in range(3):
        bias = (qv[:, :width], 0.0, qv[:, width:])[j]
        cols = slice(j * width, (j + 1) * width)
        s.qkv[:, cols] = (nn(ub_ref[...], w_in[:, cols]) + bias).astype(BF16)
    done("qkv")
    s.vt[...] = jnp.transpose(s.qkv[:, 2 * width :])
    attention_core(s.qkv, s.vt, s.bias, s.p, s.ot, width)
    done("p", "ot")
    out_bias = vectors.get(layer, "out_bias")
    gain, shift = vectors.get(layer, "gain_one"), vectors.get(layer, "shift_one")
    o = jnp.transpose(s.ot[...])
    need("w_out")
    r = u_ref[...] + (nn(o, w_out[...]) + out_bias)
    s.r1[...] = r
    done("r1")
    h = norm_stats(r)[0] * gain + shift
    s.h[...] = h
    s.hb[...] = h.astype(BF16)


def feed_forward(h_ref, hb_ref, w_up, w_down, vectors, layer, s, need, done):
    length, width = h_ref.shape
    hidden = w_up.shape[1]
    up_bias = vectors.get(layer, "up_bias")
    tile = 256
    need("w_up")
    for j in range(hidden // tile):
        cols = slice(j * tile, (j + 1) * tile)
        v = nn(hb_ref[...], w_up[:, cols]) + up_bias[:, cols]
        v2 = v * v
        half = 0.5 + 0.5 * jnp.tanh(v * (GELU_C + (GELU_C * 0.044715) * v2))
        m = v * half
        s.m[:, cols] = m.astype(BF16)
        s.d[:, cols] = (half + m * (1.0 - half) * (2 * GELU_C + (6 * GELU_C * 0.044715) * v2)).astype(BF16)
    done("m", "d")
    down_bias = vectors.get(layer, "down_bias")
    gain, shift = vectors.get(layer, "gain_two"), vectors.get(layer, "shift_two")
    need("w_down")
    r = h_ref[...] + (nn(s.m[...], w_down[...]) + down_bias)
    s.r2[...] = r
    done("r2")
    return norm_stats(r)[0] * gain + shift


def feed_backward(g_ref, r2_ref, hb_ref, m_ref, d_ref, w_up, w_down, vectors, layer, part, s, need, done):
    length, width = r2_ref.shape
    hidden = w_up.shape[1]
    gain = vectors.get(layer, "gain_two")
    need("g", "r2")
    dr, d_gain, d_shift = norm_backward(r2_ref[...], g_ref[...].astype(F32), gain)
    df = dr.astype(BF16)
    s.dh[...] = dr
    s.df[...] = df
    d_down = col_sums(df.astype(F32))
    tile = 256
    d_up = []
    need("w_down", "d")
    for j in range(hidden // tile):
        cols = slice(j * tile, (j + 1) * tile)
        dz = (nt(s.df[...], w_down[cols, :]) * d_ref[:, cols].astype(F32)).astype(BF16)
        s.dz[:, cols] = dz
        d_up.append(col_sums(dz.astype(F32)))
    summed = [jnp.sum(x, axis=0, keepdims=True) for x in [jnp.concatenate(d_up, axis=1), d_down, d_gain, d_shift]]
    pack_vectors(summed, part, s.vec_keep, s.vec_send)
    done("vec_keep", "vec_send")
    need("hb", "m")
    s.hbt[...] = jnp.transpose(hb_ref[...])
    half, rows = width // 2, hidden // 2
    for which, target in ((1 - part, "f_send"), (part, "f_keep")):
        into = getattr(s, target)
        left = s.hbt[pl.ds(pl.multiple_of(which * half, half), half), :]
        for j in range(hidden // 512):
            cols = slice(j * 512, (j + 1) * 512)
            into[:, cols] = nn(left, s.dz[:, cols]).astype(BF16)
        for j in range(rows // half):
            at = pl.multiple_of(which * rows + j * half, half)
            left = jnp.transpose(m_ref[:, pl.ds(at, half)])
            into[:, hidden + j * width : hidden + (j + 1) * width] = nn(left, s.df[...]).astype(BF16)
        done(target)
    need("w_up")
    s.dh[...] += nt(s.dz[...], w_up[...])
    done("dh")


def attention_backward(
    dh_ref, r1_ref, ub_ref, ot_ref, qkv_ref, p_ref, w_in, w_out, vectors, layer, part, s, need, done
):
    length, width = r1_ref.shape
    gain = vectors.get(layer, "gain_one")
    need("dh", "r1")
    dr, d_gain, d_shift = norm_backward(r1_ref[...], dh_ref[...], gain)
    da = dr.astype(BF16)
    s.du[...] = dr
    s.da[...] = da
    d_out = col_sums(da.astype(F32))
    need("w_out")
    s.do[...] = nt(s.da[...], w_out[...]).astype(BF16)
    need("qkv")
    s.kt[...] = jnp.transpose(qkv_ref[:, width : 2 * width])
    need("p")
    scale = 1.0 / math.sqrt(width // HEADS)
    q_masks, o_masks = head_masks(scale), head_masks(1.0)
    blocks = length // BLOCK
    dk, dv = {}, {}

    def place(t):
        pair, i = divmod(t, blocks)
        low, high = key_range(i)
        return pair * 128, slice(i * BLOCK, (i + 1) * BLOCK), low, high

    def to_p(t, unused):
        lane, queries, low, high = place(t)
        do = stacked(s.do[queries, lane : lane + 128], o_masks)
        return nt(qkv_ref[low:high, 2 * width + lane : 2 * width + lane + 128], do), do

    def to_s(t, held):
        lane, queries, low, high = place(t)
        dp, do = held
        pb = p_ref[t, : high - low, :]
        p = pb.astype(F32)
        weighted = dp * p
        ds = (weighted - p * jnp.sum(weighted, axis=0, keepdims=True)).astype(BF16)
        return ds, pb, do

    def to_qkv(t, held):
        lane, queries, low, high = place(t)
        ds, pb, do = held
        q = stacked(qkv_ref[queries, lane : lane + 128], q_masks)
        more_v, more_k = nn(pb, do), nn(ds, q)
        for b in range(low // BLOCK, high // BLOCK):
            piece = slice(b * BLOCK - low, (b + 1) * BLOCK - low)
            dk[lane, b] = dk[lane, b] + more_k[piece] if (lane, b) in dk else more_k[piece]
            dv[lane, b] = dv[lane, b] + more_v[piece] if (lane, b) in dv else more_v[piece]
        dq = nn(s.kt[lane : lane + 128, low:high], ds) * scale
        s.dqt[lane : lane + 64, queries] = dq[:64, :BLOCK].astype(BF16)
        s.dqt[lane + 64 : lane + 128, queries] = dq[64:, BLOCK:].astype(BF16)
        if high == length:
            for b in range(blocks):
                keys = slice(b * BLOCK, (b + 1) * BLOCK)
                s.dqkv[keys, width + lane : width + lane + 128] = dk[lane, b].astype(BF16)
                s.dqkv[keys, 2 * width + lane : 2 * width + lane + 128] = dv[lane, b].astype(BF16)

    staggered(HEADS // 2 * blocks, (to_p, to_s, to_qkv))
    s.dqkv[:, :width] = jnp.transpose(s.dqt[...])
    d_query = col_sums(s.dqkv[:, :width].astype(F32))
    d_value = col_sums(s.dqkv[:, 2 * width :].astype(F32))
    need("w_in")
    s.du[...] += nt(s.dqkv[...], w_in[...])
    done("du")
    need("ub", "ot")
    s.ubt[...] = jnp.transpose(ub_ref[...])
    summed = [jnp.concatenate([d_query, d_value], axis=1), d_out, d_gain, d_shift]
    pack_vectors([jnp.sum(x, axis=0, keepdims=True) for x in summed], part, s.vec_keep, s.vec_send)
    need("feed_keep", "feed_send")
    half = width // 2
    for which, target, vec, feed in (
        (1 - part, "a_send", s.vec_send, s.feed_send),
        (part, "a_keep", s.vec_keep, s.feed_keep),
    ):
        into = getattr(s, target)
        at = pl.ds(pl.multiple_of(which * half, half), half)
        left = s.ubt[at, :]
        for j in range(3):
            cols = slice(j * width, (j + 1) * width)
            into[:, cols] = nn(left, s.dqkv[:, cols]).astype(BF16)
        into[:, 3 * width : 4 * width] = nn(ot_ref[at, :], s.da[...]).astype(BF16)
        into[:, 4 * width : 5 * width] = s.du[at, :].astype(BF16)
        into[:16, 5 * width :] = vec[...]
        into[16:32, 5 * width :] = feed[...]
        into[32:, 5 * width :] = jnp.zeros((half - 32, 128), BF16)
        done(target)


class Names:
    pass


def call(name, body, inputs, outputs, scratch, flops):
    names_in, names_out, names_scratch = list(inputs), list(outputs), list(scratch)

    def kernel(*refs):
        groups = []
        at = 0
        for names in (names_in, names_out, names_scratch):
            group = Names()
            for key in names:
                setattr(group, key, refs[at])
                at += 1
            groups.append(group)
        copies = Copies(refs[at])
        body(*groups, copies)
        copies.finish()

    moved = sum(math.prod(x.shape) * x.dtype.itemsize for x in list(inputs.values()) + list(outputs.values()))
    results = pl.pallas_call(
        kernel,
        name=name,
        out_shape=tuple(outputs.values()),
        in_specs=[pl.BlockSpec(memory_space=pl.ANY)] * len(inputs),
        out_specs=tuple([pl.BlockSpec(memory_space=pl.ANY)] * len(outputs)),
        scratch_shapes=[pltpu.VMEM(x.shape, x.dtype) for x in scratch.values()] + [pltpu.SemaphoreType.DMA((48,))],
        compiler_params=pltpu.CompilerParams(vmem_limit_bytes=VMEM_LIMIT),
        cost_estimate=pl.CostEstimate(flops=flops, bytes_accessed=moved, transcendentals=0),
    )(*inputs.values())
    return dict(zip(names_out, results))


def needer(copies, loads):
    def need(*names):
        for key in names:
            copies.wait(*loads.pop(key, ()))

    return need


def storer(copies, s, o, names):
    def done(*keys):
        for key in keys:
            target = names.get(key, key)
            if hasattr(o, target):
                copies.start(getattr(s, key), getattr(o, target))

    return done


def shape(dims, dtype):
    return jax.ShapeDtypeStruct(tuple(dims), dtype)


def other_core(value):
    return lax.ppermute(value, "pipe", [(0, 1), (1, 0)])


def reduce_over(value, orders):
    size, part = lax.axis_size("dp"), lax.axis_index("pipe")

    def mirrored(x, distances):
        pairs = [(2 * i + c, 2 * (i ^ distances[c]) + c) for i in range(size) for c in range(2)]
        return lax.ppermute(x, ("dp", "pipe"), pairs)

    def side(distances):
        return lax.axis_index("dp") // jnp.where(part == 0, distances[0], distances[1]) % 2

    steps = list(zip(*orders))
    for distances in steps[:-1]:
        half = value.shape[0] // 2
        bit = side(distances)
        theirs = lax.dynamic_slice_in_dim(value, (1 - bit) * half, half, 0)
        mine = lax.dynamic_slice_in_dim(value, bit * half, half, 0)
        value = mine + mirrored(theirs, distances)
    value = value + mirrored(value, steps[-1])
    for distances in steps[-2::-1]:
        other = mirrored(value, distances)
        low = side(distances) == 0
        value = jnp.concatenate([jnp.where(low, value, other), jnp.where(low, other, value)], axis=0)
    return value


def orders_for(size):
    bits = [1 << i for i in range(size.bit_length() - 1)]
    side_bits = (len(bits) - 1) // 3
    xs, ys, zs = bits[:side_bits], bits[side_bits : 2 * side_bits], bits[2 * side_bits :]
    return xs + zs[:1] + ys + zs[1:], ys + zs[:1] + xs + zs[1:]


def per_device(
    boundary,
    positions,
    w_in,
    qv_bias,
    w_out,
    out_bias,
    gain_one,
    shift_one,
    w_up,
    up_bias,
    w_down,
    down_bias,
    gain_two,
    shift_two,
    segment_ids,
):
    part = lax.axis_index("pipe")
    window_count, length = segment_ids.shape
    layers, half, width = positions.shape
    hidden = w_up.shape[2]
    blocks = length // BLOCK

    small = (qv_bias, out_bias, gain_one, shift_one, up_bias, down_bias, gain_two, shift_two)
    small_names = ("qv_bias", "out_bias", "gain_one", "shift_one", "up_bias", "down_bias", "gain_two", "shift_two")
    sizes = [(key, x.shape[1]) for key, x in zip(small_names, small)]
    vec = jnp.concatenate(small, axis=1)
    windows = boundary.reshape(window_count, length, width)
    got = other_core(lax.dynamic_index_in_dim(windows, 1 - part, 0, keepdims=False))
    vec2, pos2, w_in2, w_out2 = other_core(vec), other_core(positions), other_core(w_in), other_core(w_out)
    late = lax.optimization_barrier((w_up, w_down, got, w_in2, w_out2))
    w_up2, w_down2 = other_core(late[0]), other_core(late[1])
    seg = lax.dynamic_index_in_dim(segment_ids, part, 0, keepdims=True)

    square, wide = (length, width), (length, hidden)
    qkv_shape, p_shape = (length, 3 * width), (HEADS // 2 * blocks, min(length, REACH + BLOCK), 2 * BLOCK)
    vec_in = dict(vec=vec, vec2=vec2)
    vec_scratch = dict(vec=shape(vec.shape, BF16), vec2=shape(vec.shape, BF16))
    attention_in = dict(pos=positions, pos2=pos2, w_in=w_in, w_in2=w_in2, w_out=w_out, w_out2=w_out2, seg=seg)
    attention_out = dict(
        ub=shape(square, BF16), qkv=shape(qkv_shape, BF16), p=shape(p_shape, BF16), ot=shape(square, BF16),
        r1=shape(square, F32),
    )
    attention_scratch = dict(
        pos=shape(square, BF16), w_in=shape((width, 3 * width), BF16), w_out=shape((width, width), BF16),
        seg=shape(seg.shape, seg.dtype), u=shape(square, F32), ub=shape(square, BF16), qkv=shape(qkv_shape, BF16),
        vt=shape(square, BF16), bias=shape((length, length), F32), p=shape(p_shape, BF16), ot=shape(square, BF16),
        r1=shape(square, F32), h=shape(square, F32), hb=shape(square, BF16),
    )
    feed_in = dict(w_up=w_up, w_up2=w_up2, w_down=w_down, w_down2=w_down2)
    feed_weights = dict(w_up=shape((width, hidden), BF16), w_down=shape((hidden, width), BF16))
    feed_scratch = dict(m=shape(wide, BF16), d=shape(wide, BF16), r2=shape(square, F32))
    vec_grads = dict(vec_keep=shape((16, 128), BF16), vec_send=shape((16, 128), BF16))
    feed_grads = dict(f_keep=shape((half, 2 * hidden), BF16), f_send=shape((half, 2 * hidden), BF16))
    attention_grads = dict(a_keep=shape((half, 5 * width + 128), BF16), a_send=shape((half, 5 * width + 128), BF16))
    back_scratch = dict(
        dh=shape(square, F32), df=shape(square, BF16), dz=shape(wide, BF16), hbt=shape(square, BF16),
        **feed_grads, **vec_grads,
    )
    flops_attention = 2 * length * width * (4 * width + length)
    flops_feed = 4 * length * width * hidden

    def load_halves(i, s, copies, layer, keys, place, names={}):
        return {
            names.get(key, key): halves_in(
                copies, getattr(i, key), getattr(i, key + "2"), layer, getattr(s, names.get(key, key)), place
            )
            for key in keys
        }

    def load(i, s, copies, keys):
        return {key: (copies.start(getattr(i, key), getattr(s, key)),) for key in keys}

    def window_in(i, copies, place, owner, target):
        sem = copies.sems.at[copies.count]
        copy = copies.make(i.got, target)

        @pl.when(place == owner)
        def _():
            at = pl.ds(pl.multiple_of(place * length, length), length)
            pltpu.make_async_copy(i.rows.at[0, at], target, sem).start()

        @pl.when(place != owner)
        def _():
            copy.start()

        return (copy,)

    def vectors_of(s, need, place):
        need("vec", "vec2")
        return Vectors(s.vec, s.vec2, place, sizes)

    def attention_first(i, o, s, copies):
        place = lax.axis_index("pipe")
        loads = {"x": window_in(i, copies, place, 0, s.x)}
        loads |= load_halves(i, s, copies, 0, ["pos"], place) | load(i, s, copies, ["seg", "vec", "vec2"])
        loads |= load_halves(i, s, copies, 0, ["w_in", "w_out"], place)
        need, done = needer(copies, loads), storer(copies, s, o, {})
        vectors = vectors_of(s, need, place)
        need("x", "pos")
        u = s.x[...] + s.pos[...].astype(F32)
        s.u[...] = u
        s.ub[...] = u.astype(BF16)
        done("ub")
        attention_forward(s.u, s.ub, s.w_in, s.w_out, vectors, 0, s.seg, s, need, done)
        done("h", "hb")

    first = call(
        "attention_first", attention_first,
        dict(rows=boundary, got=got, **vec_in, **attention_in),
        dict(**attention_out, h=shape(square, F32), hb=shape(square, BF16)),
        dict(x=shape(square, F32), **vec_scratch, **attention_scratch),
        flops_attention,
    )

    def middle(i, o, s, copies):
        place = lax.axis_index("pipe")
        loads = load(i, s, copies, ["vec", "vec2", "hb0"]) | load_halves(i, s, copies, 0, ["w_up"], place)
        loads |= load(i, s, copies, ["h0"]) | load_halves(i, s, copies, 0, ["w_down"], place)
        loads |= load_halves(i, s, copies, 1, ["pos", "w_in"], place) | load(i, s, copies, ["seg"])
        loads |= load_halves(i, s, copies, 1, ["w_out"], place)
        second = load_halves(i, s, copies, 1, ["w_up", "w_down"], place, {"w_up": "last_up", "w_down": "last_down"})
        second["w_up"], second["w_down"] = second.pop("last_up"), second.pop("last_down")
        second["g"] = window_in(i, copies, place, 1, s.g)
        need = needer(copies, loads)
        done = storer(copies, s, o, {"m": "m0", "d": "d0", "r2": "r20"})
        vectors = vectors_of(s, need, place)
        need("hb0", "h0")
        y = feed_forward(s.h0, s.hb0, s.w_up, s.w_down, vectors, 0, s, need, done)
        need("pos")
        u = y.astype(BF16).astype(F32) + s.pos[...].astype(F32)
        s.u[...] = u
        s.ub[...] = u.astype(BF16)
        done("ub")
        attention_forward(s.u, s.ub, s.w_in, s.w_out, vectors, 1, s.seg, s, need, done)
        need = needer(copies, second)
        done = storer(copies, s, o, {"m": "", "d": "", "r2": ""})
        t = Names()
        t.__dict__.update(s.__dict__)
        t.m, t.d, t.r2 = s.last_m, s.last_d, s.last_r2
        s.y[...] = feed_forward(s.h, s.hb, s.last_up, s.last_down, vectors, 1, t, need, done)
        done("y")
        feed_backward(
            s.g, t.r2, s.hb, t.m, t.d, s.last_up, s.last_down, vectors, 1, place, t, need, done
        )

    mid = call(
        "middle", middle,
        dict(h0=first["h"], hb0=first["hb"], rows=boundary, got=got, **vec_in, **attention_in, **feed_in),
        dict(
            **attention_out, m0=shape(wide, BF16), d0=shape(wide, BF16), r20=shape(square, F32),
            y=shape(square, F32), dh=shape(square, F32), **feed_grads, **vec_grads,
        ),
        dict(
            h0=shape(square, F32), hb0=shape(square, BF16), g=shape(square, F32), **vec_scratch,
            **attention_scratch, **feed_weights, last_up=feed_weights["w_up"], last_down=feed_weights["w_down"],
            **feed_scratch, last_m=shape(wide, BF16), last_d=shape(wide, BF16), last_r2=shape(square, F32),
            y=shape(square, F32), **back_scratch,
        ),
        flops_attention + 4 * flops_feed,
    )

    def backward_attention(layer, source, dh, feed):
        def body(i, o, s, copies):
            place = lax.axis_index("pipe")
            loads = load(i, s, copies, ["vec", "vec2", "dh", "r1"])
            loads |= load_halves(i, s, copies, layer, ["w_out"], place)
            loads |= load(i, s, copies, ["qkv", "p"]) | load_halves(i, s, copies, layer, ["w_in"], place)
            loads |= load(i, s, copies, ["ub", "ot", "feed_keep", "feed_send"])
            need, done = needer(copies, loads), storer(copies, s, o, {})
            vectors = vectors_of(s, need, place)

            def done_or_lower(*keys):
                if "du" in keys and layer > 0:
                    s.g[...] = s.du[...].astype(BF16)
                    keys = ("g",)
                done(*keys)

            attention_backward(
                s.dh, s.r1, s.ub, s.ot, s.qkv, s.p, s.w_in, s.w_out, vectors, layer, place, s, need, done_or_lower
            )

        result = dict(g=shape(square, BF16)) if layer > 0 else dict(du=shape(square, F32))
        return call(
            f"attention_backward_{layer}", body,
            dict(
                dh=dh, **{key: source[key] for key in ("r1", "ot", "qkv", "p", "ub")}, **vec_in,
                w_in=w_in, w_in2=w_in2, w_out=w_out, w_out2=w_out2,
                feed_keep=feed["vec_keep"], feed_send=feed["vec_send"],
            ),
            dict(**result, **attention_grads),
            dict(
                dh=shape(square, F32), r1=shape(square, F32), ot=shape(square, BF16), qkv=shape(qkv_shape, BF16),
                p=shape(p_shape, BF16), ub=shape(square, BF16), **vec_scratch,
                w_in=shape((width, 3 * width), BF16), w_out=shape((width, width), BF16),
                du=shape(square, F32), da=shape(square, BF16), do=shape(square, BF16), kt=shape(square, BF16),
                dqt=shape(square, BF16), dqkv=shape(qkv_shape, BF16), ubt=shape(square, BF16),
                g=shape(square, BF16), **vec_grads, feed_keep=vec_grads["vec_keep"], feed_send=vec_grads["vec_keep"],
                **attention_grads,
            ),
            2 * flops_attention,
        )

    def feed_back(i, o, s, copies):
        place = lax.axis_index("pipe")
        loads = load(i, s, copies, ["vec", "vec2", "g", "r2"]) | load_halves(i, s, copies, 0, ["w_down"], place)
        loads |= load(i, s, copies, ["d", "hb", "m"]) | load_halves(i, s, copies, 0, ["w_up"], place)
        need, done = needer(copies, loads), storer(copies, s, o, {})
        vectors = vectors_of(s, need, place)
        feed_backward(s.g, s.r2, s.hb, s.m, s.d, s.w_up, s.w_down, vectors, 0, place, s, need, done)

    orders = orders_for(lax.axis_size("dp"))
    swapped = orders[::-1]

    f1 = other_core(mid["f_send"])
    dh, f1 = lax.optimization_barrier((mid["dh"], f1))
    last_attention = backward_attention(1, mid, dh, mid)
    a1 = other_core(last_attention["a_send"])
    first_feed = call(
        "feed_backward_0", feed_back,
        dict(g=last_attention["g"], r2=mid["r20"], d=mid["d0"], hb=first["hb"], m=mid["m0"], **vec_in, **feed_in),
        dict(dh=shape(square, F32), **feed_grads, **vec_grads),
        dict(
            g=shape(square, BF16), hb=shape(square, BF16), **vec_scratch, **feed_weights, **feed_scratch,
            **back_scratch,
        ),
        2 * flops_feed,
    )
    f0 = other_core(first_feed["f_send"])
    first_attention = backward_attention(0, first, first_feed["dh"], first_feed)
    a0 = other_core(first_attention["a_send"])

    theirs = other_core(jnp.where(part == 0, mid["y"], first_attention["du"]))
    boundary_out = jnp.stack(
        [jnp.where(part == 0, first_attention["du"], theirs), jnp.where(part == 0, theirs, mid["y"])]
    ).reshape(1, window_count * length, width)

    feeds = [
        reduce_over(first_feed["f_keep"] + f0, swapped),
        reduce_over(mid["f_keep"] + f1, orders),
    ]
    attentions = [
        reduce_over(first_attention["a_keep"] + a0, orders),
        reduce_over(last_attention["a_keep"] + a1, swapped),
    ]

    def out(pieces):
        return jnp.stack(pieces).astype(F32)

    def vec_out(offset, count):
        rows = [x[offset : offset + count, 5 * width :] for x in attentions]
        return out([r.reshape(count * 128) for r in rows])

    def down_rows(x):
        return jnp.concatenate(jnp.split(x[:, hidden:], hidden // width, axis=1), axis=0)

    a = width // 256
    u = hidden // 256
    return (
        boundary_out,
        out([x[:, 4 * width : 5 * width] for x in attentions]),
        out([x[:, : 3 * width] for x in attentions]),
        vec_out(0, 2 * a),
        out([x[:, 3 * width : 4 * width] for x in attentions]),
        vec_out(2 * a, a),
        vec_out(3 * a, a),
        vec_out(4 * a, a),
        out([x[:, :hidden] for x in feeds]),
        vec_out(16, u),
        out([down_rows(x) for x in feeds]),
        vec_out(16 + u, a),
        vec_out(16 + u + a, a),
        vec_out(16 + u + 2 * a, a),
    )


def solution(mesh):
    rows, vector = P(None, "pipe", None), P(None, "pipe")
    both = P("pipe", "dp", None)
    params = (rows, rows, vector, rows, vector, vector, vector, rows, vector, rows, vector, vector, vector)
    return jax.shard_map(
        per_device,
        mesh=mesh,
        in_specs=(both,) + params + (P("dp", None),),
        out_specs=(both,) + params,
        check_vma=False,
    )
```

```python
import functools
import math

import jax
import jax.numpy as jnp
from jax import lax
from jax.experimental import pallas as pl
from jax.experimental.pallas import tpu as pltpu
from jax.sharding import PartitionSpec as P

HEADS = 8
EPS = 1e-05
MASKED = -1e30
REACH = 256
BLOCK = 128
F32, BF16 = jnp.float32, jnp.bfloat16
GELU_C = math.sqrt(2.0 / math.pi)
ROOM = 8 * 1024 * 1024
AHEAD = 24 * 1024 * 1024


def nn(a, b):
    return lax.dot_general(a, b, (((1,), (0,)), ((), ())), preferred_element_type=F32)


def nt(a, b):
    return lax.dot_general(a, b, (((1,), (1,)), ((), ())), preferred_element_type=F32)


def col_sums(x):
    return jnp.sum(x.reshape(x.shape[0] // 8, 8, x.shape[1]), axis=0)


class Copies:
    def __init__(self, sems):
        self.sems, self.count, self.open = sems, 0, []

    def make(self, source, target):
        copy = pltpu.make_async_copy(source, target, self.sems.at[self.count])
        self.count += 1
        self.open.append(copy)
        return copy

    def start(self, source, target):
        copy = self.make(source, target)
        copy.start()
        return copy

    def wait(self, *copies):
        for copy in copies:
            copy.wait()
            self.open = [c for c in self.open if c is not copy]

    def finish(self):
        self.wait(*list(self.open))


class Vectors:
    def __init__(self, own, other, part, sizes):
        self.own, self.other, self.part, self.sizes = own, other, part, sizes

    def get(self, layer, name):
        at = 0
        for key, size in self.sizes:
            if key == name:
                break
            at += size
        own = self.own[:, at : at + size].astype(F32)[layer : layer + 1]
        other = self.other[:, at : at + size].astype(F32)[layer : layer + 1]
        low = jnp.where(self.part == 0, own, other)
        high = jnp.where(self.part == 0, other, own)
        return jnp.concatenate([low, high], axis=1)


def halves_in(copies, own, other, layer, target, part):
    rows = own.shape[1]
    mine = pl.ds(pl.multiple_of(part * rows, rows), rows)
    theirs = pl.ds(pl.multiple_of((1 - part) * rows, rows), rows)
    return (
        lambda: copies.start(own.at[layer], target.at[mine]),
        lambda: copies.start(other.at[layer], target.at[theirs]),
    )


def pack_vectors(vectors, part, keep_ref, send_ref):
    keep, send = [], []
    for vector in vectors:
        half = vector.shape[1] // 2
        low, high = vector[:, :half], vector[:, half:]
        mine = jnp.where(part == 0, low, high)
        theirs = jnp.where(part == 0, high, low)
        for j in range(half // 128):
            keep.append(mine[:, j * 128 : (j + 1) * 128])
            send.append(theirs[:, j * 128 : (j + 1) * 128])
    spare = jnp.zeros((keep_ref.shape[0] - len(keep), 128), F32)
    keep_ref[...] = jnp.concatenate(keep + [spare], axis=0).astype(keep_ref.dtype)
    send_ref[...] = jnp.concatenate(send + [spare], axis=0).astype(send_ref.dtype)


def norm_stats(r):
    centred = r - jnp.mean(r, axis=-1, keepdims=True)
    scale = lax.rsqrt(jnp.mean(centred * centred, axis=-1, keepdims=True) + EPS)
    return centred * scale, scale


def norm_backward(r, g, gain):
    xhat, scale = norm_stats(r)
    gy = g * gain
    mean_one = jnp.mean(gy, axis=-1, keepdims=True)
    mean_two = jnp.mean(gy * xhat, axis=-1, keepdims=True)
    return scale * (gy - mean_one - xhat * mean_two), col_sums(g * xhat), col_sums(g)


def key_range(i):
    return max(0, i * BLOCK + 1 - REACH) // BLOCK * BLOCK, (i + 1) * BLOCK


def head_masks(scale):
    lane = lax.broadcasted_iota(jnp.int32, (1, 128), 1)
    first = jnp.where(lane < 64, scale, 0.0).astype(BF16)
    second = jnp.where(lane < 64, 0.0, scale).astype(BF16)
    return first, second


def stacked(x, masks):
    return jnp.concatenate([x * masks[0], x * masks[1]], axis=0)


def write_bias(seg_ref, bias_ref):
    length = seg_ref.shape[1]
    seg = seg_ref[...].astype(F32)
    columns = jnp.broadcast_to(seg, (128, length))
    for j in range(length // 128):
        rows = pl.ds(j * 128, 128)
        own = jnp.broadcast_to(jnp.transpose(columns[:, j * 128 : (j + 1) * 128])[:, :1], (128, length))
        key = lax.broadcasted_iota(jnp.int32, (128, length), 0) + j * 128
        query = lax.broadcasted_iota(jnp.int32, (128, length), 1)
        bias_ref[rows, :] = jnp.where((own == seg) & (key <= query), 0.0, MASKED)


def staggered(count, stages):
    held = {}
    for tick in range(count + len(stages) - 1):
        for number, stage in enumerate(stages):
            t = tick - number
            if 0 <= t < count:
                held[t] = stage(t, held.pop(t, None))


def attention_core(qkv_ref, vt_ref, bias_ref, p_ref, ot_ref, width):
    masks = head_masks(1.0 / math.sqrt(width // HEADS))
    blocks = qkv_ref.shape[0] // BLOCK

    def place(t):
        pair, i = divmod(t, blocks)
        low, high = key_range(i)
        return pair * 128, slice(i * BLOCK, (i + 1) * BLOCK), low, high

    def score(t, unused):
        lane, queries, low, high = place(t)
        q = stacked(qkv_ref[queries, lane : lane + 128], masks)
        return nt(qkv_ref[low:high, width + lane : width + lane + 128], q)

    def soften(t, s):
        lane, queries, low, high = place(t)
        bias = bias_ref[low:high, queries]
        s = s + jnp.concatenate([bias, bias], axis=1)
        e = jnp.exp(s - jnp.max(s, axis=0, keepdims=True))
        p = (e * (1.0 / jnp.sum(e, axis=0, keepdims=True))).astype(BF16)
        p_ref[t, : high - low, :] = p
        return p

    def attend(t, p):
        lane, queries, low, high = place(t)
        o = nn(vt_ref[lane : lane + 128, low:high], p)
        ot_ref[lane : lane + 64, queries] = o[:64, :BLOCK].astype(BF16)
        ot_ref[lane + 64 : lane + 128, queries] = o[64:, BLOCK:].astype(BF16)

    staggered(HEADS // 2 * blocks, (score, soften, attend))


def attention_forward(u_ref, ub_ref, w_in, w_out, vectors, layer, seg_ref, s, need, done):
    length, width = u_ref.shape
    need("seg")
    write_bias(seg_ref, s.bias)
    qv = vectors.get(layer, "qv_bias")
    need("w_in")
    for j in range(3):
        bias = (qv[:, :width], 0.0, qv[:, width:])[j]
        cols = slice(j * width, (j + 1) * width)
        s.qkv[:, cols] = (nn(ub_ref[...], w_in[:, cols]) + bias).astype(BF16)
    done("qkv")
    s.vt[...] = jnp.transpose(s.qkv[:, 2 * width :])
    attention_core(s.qkv, s.vt, s.bias, s.p, s.ot, width)
    done("p", "ot")
    out_bias = vectors.get(layer, "out_bias")
    gain, shift = vectors.get(layer, "gain_one"), vectors.get(layer, "shift_one")
    o = jnp.transpose(s.ot[...])
    need("w_out")
    r = u_ref[...] + (nn(o, w_out[...]) + out_bias)
    s.r1[...] = r
    done("r1")
    h = norm_stats(r)[0] * gain + shift
    s.h[...] = h
    s.hb[...] = h.astype(BF16)


def feed_forward(h_ref, hb_ref, w_up, w_down, vectors, layer, s, need, done):
    length, width = h_ref.shape
    hidden = w_up.shape[1]
    up_bias = vectors.get(layer, "up_bias")
    tile = 256
    need("w_up")
    for j in range(hidden // tile):
        cols = slice(j * tile, (j + 1) * tile)
        v = nn(hb_ref[...], w_up[:, cols]) + up_bias[:, cols]
        v2 = v * v
        half = 0.5 + 0.5 * jnp.tanh(v * (GELU_C + (GELU_C * 0.044715) * v2))
        m = v * half
        s.m[:, cols] = m.astype(BF16)
        s.d[:, cols] = (half + m * (1.0 - half) * (2 * GELU_C + (6 * GELU_C * 0.044715) * v2)).astype(BF16)
    done("m", "d")
    down_bias = vectors.get(layer, "down_bias")
    gain, shift = vectors.get(layer, "gain_two"), vectors.get(layer, "shift_two")
    need("w_down")
    r = h_ref[...] + (nn(s.m[...], w_down[...]) + down_bias)
    s.r2[...] = r
    done("r2")
    return norm_stats(r)[0] * gain + shift


def feed_backward(g_ref, r2_ref, hb_ref, m_ref, d_ref, w_up, w_down, vectors, layer, part, s, need, done):
    length, width = r2_ref.shape
    hidden = w_up.shape[1]
    gain = vectors.get(layer, "gain_two")
    need("g", "r2")
    dr, d_gain, d_shift = norm_backward(r2_ref[...], g_ref[...].astype(F32), gain)
    df = dr.astype(BF16)
    s.dh[...] = dr
    s.df[...] = df
    d_down = col_sums(df.astype(F32))
    tile = 256
    d_up = []
    need("w_down", "d")
    for j in range(hidden // tile):
        cols = slice(j * tile, (j + 1) * tile)
        dz = (nt(s.df[...], w_down[cols, :]) * d_ref[:, cols].astype(F32)).astype(BF16)
        s.dz[:, cols] = dz
        d_up.append(col_sums(dz.astype(F32)))
    summed = [jnp.sum(x, axis=0, keepdims=True) for x in [jnp.concatenate(d_up, axis=1), d_down, d_gain, d_shift]]
    pack_vectors(summed, part, s.feed_keep, s.feed_send)
    need("hb", "m")
    s.hbt[...] = jnp.transpose(hb_ref[...])
    half, rows = width // 2, hidden // 2
    for which, end in ((1 - part, "_send"), (part, "_keep")):
        into, other = getattr(s, "one" + end), getattr(s, "two" + end)
        left = s.hbt[pl.ds(pl.multiple_of(which * half, half), half), :]
        for j in range(hidden // 512):
            cols = slice(j * 512, (j + 1) * 512)
            into[:, cols] = nn(left, s.dz[:, cols]).astype(BF16)
        done("one" + end, 0, hidden)
        for j in range(rows // half):
            at = pl.multiple_of(which * rows + j * half, half)
            left = jnp.transpose(m_ref[:, pl.ds(at, half)])
            other[:, j * width : (j + 1) * width] = nn(left, s.df[...]).astype(BF16)
        done("two" + end, 0, hidden)
    need("w_up")
    s.dh[...] += nt(s.dz[...], w_up[...])


def attention_backward(
    dh_ref, r1_ref, ub_ref, ot_ref, qkv_ref, p_ref, w_in, w_out, vectors, layer, part, s, need, done
):
    length, width = r1_ref.shape
    gain = vectors.get(layer, "gain_one")
    need("dh", "r1")
    dr, d_gain, d_shift = norm_backward(r1_ref[...], dh_ref[...], gain)
    da = dr.astype(BF16)
    s.du[...] = dr
    s.da[...] = da
    d_out = col_sums(da.astype(F32))
    need("w_out")
    s.do[...] = nt(s.da[...], w_out[...]).astype(BF16)
    need("qkv")
    s.kt[...] = jnp.transpose(qkv_ref[:, width : 2 * width])
    need("p")
    scale = 1.0 / math.sqrt(width // HEADS)
    q_masks, o_masks = head_masks(scale), head_masks(1.0)
    blocks = length // BLOCK
    dk, dv = {}, {}

    def place(t):
        pair, i = divmod(t, blocks)
        low, high = key_range(i)
        return pair * 128, slice(i * BLOCK, (i + 1) * BLOCK), low, high

    def to_p(t, unused):
        lane, queries, low, high = place(t)
        do = stacked(s.do[queries, lane : lane + 128], o_masks)
        return nt(qkv_ref[low:high, 2 * width + lane : 2 * width + lane + 128], do), do

    def to_s(t, held):
        lane, queries, low, high = place(t)
        dp, do = held
        pb = p_ref[t, : high - low, :]
        p = pb.astype(F32)
        weighted = dp * p
        ds = (weighted - p * jnp.sum(weighted, axis=0, keepdims=True)).astype(BF16)
        return ds, pb, do

    def to_qkv(t, held):
        lane, queries, low, high = place(t)
        ds, pb, do = held
        q = stacked(qkv_ref[queries, lane : lane + 128], q_masks)
        more_v, more_k = nn(pb, do), nn(ds, q)
        for b in range(low // BLOCK, high // BLOCK):
            piece = slice(b * BLOCK - low, (b + 1) * BLOCK - low)
            dk[lane, b] = dk[lane, b] + more_k[piece] if (lane, b) in dk else more_k[piece]
            dv[lane, b] = dv[lane, b] + more_v[piece] if (lane, b) in dv else more_v[piece]
        dq = nn(s.kt[lane : lane + 128, low:high], ds) * scale
        s.dqt[lane : lane + 64, queries] = dq[:64, :BLOCK].astype(BF16)
        s.dqt[lane + 64 : lane + 128, queries] = dq[64:, BLOCK:].astype(BF16)
        if high == length:
            for b in range(blocks):
                keys = slice(b * BLOCK, (b + 1) * BLOCK)
                s.dqkv[keys, width + lane : width + lane + 128] = dk[lane, b].astype(BF16)
                s.dqkv[keys, 2 * width + lane : 2 * width + lane + 128] = dv[lane, b].astype(BF16)

    staggered(HEADS // 2 * blocks, (to_p, to_s, to_qkv))
    s.dqkv[:, :width] = jnp.transpose(s.dqt[...])
    d_query = col_sums(s.dqkv[:, :width].astype(F32))
    d_value = col_sums(s.dqkv[:, 2 * width :].astype(F32))
    need("w_in")
    s.du[...] += nt(s.dqkv[...], w_in[...])
    done("du")
    need("ub", "ot")
    s.ubt[...] = jnp.transpose(ub_ref[...])
    summed = [jnp.concatenate([d_query, d_value], axis=1), d_out, d_gain, d_shift]
    pack_vectors([jnp.sum(x, axis=0, keepdims=True) for x in summed], part, s.vec_keep, s.vec_send)
    half = width // 2
    hidden, cut = 4 * width, s.one_keep.shape[1] - 4 * width
    for which, end, vec, feed in (
        (1 - part, "_send", s.vec_send, s.feed_send),
        (part, "_keep", s.vec_keep, s.feed_keep),
    ):
        into, other = getattr(s, "one" + end), getattr(s, "two" + end)
        at = pl.ds(pl.multiple_of(which * half, half), half)
        left = s.ubt[at, :]
        for low in range(0, cut, width):
            high = min(cut, low + width)
            into[:, hidden + low : hidden + high] = nn(left, s.dqkv[:, low:high]).astype(BF16)
        done("one" + end, hidden, hidden + cut)
        first = hidden + 3 * width - cut
        other[:, hidden:first] = nn(left, s.dqkv[:, cut:]).astype(BF16)
        other[:, first : first + width] = nn(ot_ref[at, :], s.da[...]).astype(BF16)
        other[:, first + width : first + 2 * width] = s.du[at, :].astype(BF16)
        other[:16, first + 2 * width : first + 2 * width + 128] = vec[...]
        other[16:32, first + 2 * width : first + 2 * width + 128] = feed[...]
        other[32:, first + 2 * width : first + 2 * width + 128] = jnp.zeros((half - 32, 128), BF16)
        spare = other.shape[1] - (first + 2 * width + 128)
        if spare:
            other[:, first + 2 * width + 128 :] = jnp.zeros((half, spare), BF16)
        done("two" + end, hidden, other.shape[1])


def size_of(x):
    return math.prod(x.shape) * x.dtype.itemsize


class Names:
    pass


def call(name, body, inputs, outputs, scratch, flops, after=(), copies=0):
    names_in, names_out, names_scratch = list(inputs), list(outputs), list(scratch)

    def kernel(*refs):
        groups = []
        at = 0
        for names, spare in ((names_in, len(after)), (names_out, 0), (names_scratch, 0)):
            group = Names()
            for key in names:
                setattr(group, key, refs[at])
                at += 1
            at += spare
            groups.append(group)
        moves = Copies(refs[at])
        body(*groups, moves)
        moves.finish()

    moved = sum(size_of(x) for x in list(inputs.values()) + list(outputs.values()))
    held = sum(size_of(x) for x in scratch.values())
    results = pl.pallas_call(
        kernel,
        name=name,
        out_shape=tuple(pltpu.HBM(x.shape, x.dtype) for x in outputs.values()),
        in_specs=[pl.BlockSpec(memory_space=pltpu.HBM)] * len(inputs) + [pl.BlockSpec(memory_space=pl.ANY)] * len(after),
        out_specs=tuple([pl.BlockSpec(memory_space=pltpu.HBM)] * len(outputs)),
        scratch_shapes=[pltpu.VMEM(x.shape, x.dtype) for x in scratch.values()]
        + [pltpu.SemaphoreType.DMA((len(inputs) + len(outputs) + copies,))],
        compiler_params=pltpu.CompilerParams(vmem_limit_bytes=min(60 * 1024 * 1024, held + ROOM)),
        cost_estimate=pl.CostEstimate(flops=flops, bytes_accessed=moved, transcendentals=0),
    )(*[pltpu.with_memory_space_constraint(x, pltpu.HBM) for x in inputs.values()], *after)
    return dict(zip(names_out, results))


class Loads:
    def __init__(self, copies, ahead=AHEAD):
        self.copies, self.ahead, self.waiting, self.begun = copies, ahead, [], {}

    def add(self, name, size, *starts):
        self.waiting.append((name, size, starts))

    def begin(self):
        name, size, starts = self.waiting.pop(0)
        self.begun[name] = (size, [start() for start in starts])

    def top_up(self):
        while self.waiting and sum(size for size, unused in self.begun.values()) < self.ahead:
            self.begin()

    def need(self, *names):
        for name in names:
            while any(name == entry[0] for entry in self.waiting):
                self.begin()
            if name in self.begun:
                self.copies.wait(*self.begun.pop(name)[1])
        self.top_up()


def storer(copies, s, o, names):
    def done(*keys):
        if len(keys) == 3 and not isinstance(keys[1], str):
            key, low, high = keys
            copies.start(getattr(s, key).at[:, low:high], getattr(o, key).at[:, low:high])
            return
        for key in keys:
            target = names.get(key, key)
            if hasattr(o, target):
                copies.start(getattr(s, key), getattr(o, target))

    return done


WAYS = {
    "top_one": ("xyzw", "yxzw"),
    "top_two": ("xyzw", "yxzw"),
    "low_one": ("xyzw", "yxzw"),
    "low_two": ("xyzw", "yxzw"),
}
WAITS = {
    ("top_one", 3): ("low_one", 0),
    ("top_two", 3): ("low_two", 0),
    ("top_one", 5): ("low_one", 1),
    ("top_two", 5): ("low_two", 1),
}


def shape(dims, dtype):
    return jax.ShapeDtypeStruct(tuple(dims), dtype)


def other_core(value):
    return lax.ppermute(value, "pipe", [(0, 1), (1, 0)])


class Reduction:
    def __init__(self, parts, orders):
        self.arrived = [parts[1]]
        self.parts, self.steps, self.at = parts, list(zip(*orders)), 0

    def mirrored(self, x, shifts):
        size = lax.axis_size("dp")
        pairs = [(2 * i + c, 2 * (i ^ (1 << shifts[c])) + c) for i in range(size) for c in range(2)]
        return lax.ppermute(x, ("dp", "pipe"), pairs)

    def side(self, shifts):
        part = lax.axis_index("pipe")
        return lax.shift_right_logical(lax.axis_index("dp"), jnp.where(part == 0, shifts[0], shifts[1])) & 1

    def joined(self):
        value, other = self.parts
        low = self.side(self.steps[2 * len(self.steps) - 1 - self.at]) == 0
        return jnp.concatenate([jnp.where(low, value, other), jnp.where(low, other, value)], axis=0)

    def complete(self):
        return self.at == 2 * len(self.steps) - 1

    def step(self, waits=()):
        def tie(x):
            for row in waits:
                x = x + jnp.broadcast_to(jnp.minimum(jnp.abs(row[:1]), 0), x.shape)
            return x

        inner = len(self.steps) - 1
        if self.at < inner:
            shifts = self.steps[self.at]
            half = self.parts[0].shape[0] // 2
            bit = self.side(shifts)
            theirs, mine = [
                functools.reduce(
                    jnp.add, [lax.dynamic_slice_in_dim(x, which * half, half, 0) for x in self.parts]
                )
                for which in (1 - bit, bit)
            ]
            self.parts = [mine, self.mirrored(tie(theirs), shifts)]
        elif self.at == inner:
            value = self.parts[0] + self.parts[1]
            self.parts = [value, self.mirrored(tie(value), self.steps[inner])]
        else:
            value = self.parts[0] + self.parts[1] if self.at == inner + 1 else self.joined()
            self.parts = [value, self.mirrored(tie(value), self.steps[2 * inner - self.at])]
        self.arrived.append(self.parts[1])
        self.at += 1

    def result(self):
        return self.joined()


def orders_for(size, ways):
    bits = list(range(size.bit_length() - 1))
    side_bits = (len(bits) - 1) // 3
    x, y, z = bits[:side_bits], bits[side_bits : 2 * side_bits], bits[2 * side_bits :]
    runs = {"x": x, "y": y, "z": z[:1], "w": z[1:]}
    return [sum([runs[letter] for letter in way], []) for way in ways]


def per_device(
    boundary,
    positions,
    w_in,
    qv_bias,
    w_out,
    out_bias,
    gain_one,
    shift_one,
    w_up,
    up_bias,
    w_down,
    down_bias,
    gain_two,
    shift_two,
    segment_ids,
):
    part = lax.axis_index("pipe")
    window_count, length = segment_ids.shape
    layers, half, width = positions.shape
    hidden = w_up.shape[2]
    blocks = length // BLOCK

    small = (qv_bias, out_bias, gain_one, shift_one, up_bias, down_bias, gain_two, shift_two)
    small_names = ("qv_bias", "out_bias", "gain_one", "shift_one", "up_bias", "down_bias", "gain_two", "shift_two")
    sizes = [(key, x.shape[1]) for key, x in zip(small_names, small)]
    vec = jnp.concatenate(small, axis=1)
    windows = boundary.reshape(window_count, length, width)
    got = other_core(lax.dynamic_index_in_dim(windows, 1 - part, 0, keepdims=False))
    vec2, pos2, w_in2, w_out2 = other_core(vec), other_core(positions), other_core(w_in), other_core(w_out)
    late = lax.optimization_barrier((w_up, w_down, got, vec2, pos2, w_in2, w_out2))
    w_up2, w_down2 = other_core(late[0]), other_core(late[1])
    seg = lax.dynamic_index_in_dim(segment_ids, part, 0, keepdims=True)

    square, wide = (length, width), (length, hidden)
    qkv_shape, p_shape = (length, 3 * width), (HEADS // 2 * blocks, min(length, REACH + BLOCK), 2 * BLOCK)
    vec_in = dict(vec=vec, vec2=vec2)
    vec_scratch = dict(vec=shape(vec.shape, BF16), vec2=shape(vec.shape, BF16))
    attention_in = dict(pos=positions, pos2=pos2, w_in=w_in, w_in2=w_in2, w_out=w_out, w_out2=w_out2, seg=seg)
    attention_out = dict(
        ub=shape(square, BF16), qkv=shape(qkv_shape, BF16), p=shape(p_shape, BF16), ot=shape(square, BF16),
        r1=shape(square, F32),
    )
    hidden_out = dict(h=shape(square, F32), hb=shape(square, BF16))
    attention_weights = dict(w_in=shape((width, 3 * width), BF16), w_out=shape((width, width), BF16))
    attention_scratch = dict(
        pos=shape(square, BF16), seg=shape(seg.shape, seg.dtype), u=shape(square, F32), vt=shape(square, BF16),
        bias=shape((length, length), F32), **attention_weights, **attention_out, **hidden_out,
    )
    feed_in = dict(w_up=w_up, w_up2=w_up2, w_down=w_down, w_down2=w_down2)
    feed_weights = dict(w_up=shape((width, hidden), BF16), w_down=shape((hidden, width), BF16))
    feed_out = dict(m=shape(wide, BF16), d=shape(wide, BF16), r2=shape(square, F32))
    both = (2 * hidden + 5 * width + 128 + 255) // 256 * 128
    gradients = {key + end: shape((half, both), BF16) for key in ("one", "two") for end in ("_keep", "_send")}
    vec_grads = {key + end: shape((16, 128), BF16) for key in ("vec", "feed") for end in ("_keep", "_send")}
    back_scratch = dict(
        dh=shape(square, F32), df=shape(square, BF16), dz=shape(wide, BF16), hbt=shape(square, BF16),
        du=shape(square, F32), da=shape(square, BF16), do=shape(square, BF16), kt=shape(square, BF16),
        dqt=shape(square, BF16), dqkv=shape(qkv_shape, BF16), ubt=shape(square, BF16), **vec_grads, **gradients,
    )
    flops_attention = 2 * length * width * (4 * width + length)
    flops_feed = 4 * length * width * hidden

    def load_halves(i, s, loads, layer, keys, place, names={}):
        for key in keys:
            target = getattr(s, names.get(key, key))
            loads.add(
                names.get(key, key), size_of(target),
                *halves_in(loads.copies, getattr(i, key), getattr(i, key + "2"), layer, target, place),
            )

    def load(i, s, loads, keys):
        for key in keys:
            target = getattr(s, key)
            loads.add(key, size_of(target), functools.partial(loads.copies.start, getattr(i, key), target))

    def window_in(i, copies, place, owner, target):
        sem = copies.sems.at[copies.count]
        copy = copies.make(i.got, target)

        @pl.when(place == owner)
        def _():
            at = pl.ds(pl.multiple_of(place * length, length), length)
            pltpu.make_async_copy(i.rows.at[0, at], target, sem).start()

        @pl.when(place != owner)
        def _():
            copy.start()

        return copy

    def vectors_of(s, need, place):
        need("vec", "vec2")
        return Vectors(s.vec, s.vec2, place, sizes)

    def attention_first(i, o, s, copies):
        place = lax.axis_index("pipe")
        loads = Loads(copies)
        load(i, s, loads, ["vec", "vec2"])
        loads.add("x", size_of(s.x), lambda: window_in(i, copies, place, 0, s.x))
        load_halves(i, s, loads, 0, ["pos"], place)
        load(i, s, loads, ["seg"])
        load_halves(i, s, loads, 0, ["w_in", "w_out"], place)
        need, done = loads.need, storer(copies, s, o, {})
        vectors = vectors_of(s, need, place)
        need("x", "pos")
        u = s.x[...] + s.pos[...].astype(F32)
        s.u[...] = u
        s.ub[...] = u.astype(BF16)
        done("ub")
        attention_forward(s.u, s.ub, s.w_in, s.w_out, vectors, 0, s.seg, s, need, done)
        done("h", "hb")

    first = call(
        "attention_first", attention_first,
        dict(rows=boundary, got=got, **vec_in, **attention_in),
        dict(**attention_out, **hidden_out),
        dict(x=shape(square, F32), **vec_scratch, **attention_scratch),
        10 * flops_attention,
    )

    def middle(i, o, s, copies):
        place = lax.axis_index("pipe")
        loads = Loads(copies)
        load(i, s, loads, ["vec", "vec2", "hb0"])
        load_halves(i, s, loads, 0, ["w_up"], place)
        load(i, s, loads, ["h0"])
        load_halves(i, s, loads, 0, ["w_down"], place)
        load_halves(i, s, loads, 1, ["pos"], place)
        load(i, s, loads, ["seg"])
        load_halves(i, s, loads, 1, ["w_in", "w_out"], place)
        loads.add("g", size_of(s.g), lambda: window_in(i, copies, place, 1, s.g))
        need, done = loads.need, storer(copies, s, o, {"ub": "", "qkv": "", "p": "", "ot": "", "r1": ""})
        vectors = vectors_of(s, need, place)
        need("hb0", "h0")
        y = feed_forward(s.h0, s.hb0, s.w_up, s.w_down, vectors, 0, s, need, done)
        load_halves(i, s, loads, 1, ["w_up", "w_down"], place)
        need("pos")
        u = y.astype(BF16).astype(F32) + s.pos[...].astype(F32)
        s.u[...] = u
        s.ub[...] = u.astype(BF16)
        attention_forward(s.u, s.ub, s.w_in, s.w_out, vectors, 1, s.seg, s, need, done)
        t = Names()
        t.__dict__.update(s.__dict__)
        t.m, t.d, t.r2 = s.last_m, s.last_d, s.last_r2
        done = storer(copies, s, o, {"m": "", "d": "", "r2": ""})
        s.y[...] = feed_forward(s.h, s.hb, s.w_up, s.w_down, vectors, 1, t, need, done)
        done("y")
        feed_backward(s.g, t.r2, s.hb, t.m, t.d, s.w_up, s.w_down, vectors, 1, place, t, need, done)

        def done_low(*keys):
            if keys == ("du",):
                s.gout[...] = s.du[...].astype(BF16)
                copies.start(s.gout, o.g)
            else:
                done(*keys)

        attention_backward(
            s.dh, s.r1, s.ub, s.ot, s.qkv, s.p, s.w_in, s.w_out, vectors, 1, place, s, need, done_low
        )

    top = call(
        "middle", middle,
        dict(h0=first["h"], hb0=first["hb"], rows=boundary, got=got, **vec_in, **attention_in, **feed_in),
        dict(**feed_out, y=shape(square, F32), g=shape(square, BF16), **gradients),
        dict(
            h0=shape(square, F32), hb0=shape(square, BF16), g=shape(square, F32), gout=shape(square, BF16),
            y=shape(square, F32), **vec_scratch, **attention_scratch, **feed_weights, **feed_out,
            last_m=feed_out["m"], last_d=feed_out["d"], last_r2=feed_out["r2"], **back_scratch,
        ),
        20 * flops_feed, copies=8,
    )

    def lowest(i, o, s, copies):
        place = lax.axis_index("pipe")
        loads = Loads(copies)
        load(i, s, loads, ["vec", "vec2", "g", "r2"])
        load_halves(i, s, loads, 0, ["w_down"], place)
        load(i, s, loads, ["d", "hb", "m"])
        load_halves(i, s, loads, 0, ["w_up"], place)
        load(i, s, loads, ["r1"])
        load_halves(i, s, loads, 0, ["w_out"], place)
        load(i, s, loads, ["qkv", "p"])
        load_halves(i, s, loads, 0, ["w_in"], place)
        load(i, s, loads, ["ub", "ot"])
        need, done = loads.need, storer(copies, s, o, {})
        vectors = vectors_of(s, need, place)
        feed_backward(s.g, s.r2, s.hb, s.m, s.d, s.w_up, s.w_down, vectors, 0, place, s, need, done)
        attention_backward(
            s.dh, s.r1, s.ub, s.ot, s.qkv, s.p, s.w_in, s.w_out, vectors, 0, place, s, need, done
        )

    def begin_sum(name, kernel, key):
        keep, send = kernel[key + "_keep"], kernel[key + "_send"]
        sums[name] = Reduction([keep, other_core(send)], orders_for(lax.axis_size("dp"), WAYS[name]))

    sums = {}
    begin_sum("top_one", top, "one")
    begin_sum("top_two", top, "two")
    low = call(
        "lowest", lowest,
        dict(
            g=top["g"], **{key: top[key] for key in feed_out}, hb=first["hb"],
            **{key: first[key] for key in attention_out}, **vec_in, **feed_in,
            w_in=w_in, w_in2=w_in2, w_out=w_out, w_out2=w_out2,
        ),
        dict(du=shape(square, F32), **gradients),
        dict(
            g=shape(square, BF16), hb=shape(square, BF16), **vec_scratch, **attention_weights, **attention_out,
            **feed_weights, **feed_out, **back_scratch,
        ),
        12 * flops_feed, after=[total.arrived[0] for total in sums.values()], copies=4,
    )
    begin_sum("low_one", low, "one")
    begin_sum("low_two", low, "two")
    turn = 0
    while not all(total.complete() for total in sums.values()):
        for name, total in sums.items():
            wait = WAITS.get((name, total.at + 1)) if len(total.steps) == 4 else None
            ready = wait is None or len(sums[wait[0]].arrived) > wait[1]
            if ready and not total.complete():
                total.step([sums[wait[0]].arrived[wait[1]]] if wait else [])

    theirs = other_core(jnp.where(part == 0, top["y"], low["du"]))
    boundary_out = jnp.stack(
        [jnp.where(part == 0, low["du"], theirs), jnp.where(part == 0, theirs, top["y"])]
    ).reshape(1, window_count * length, width)
    sums = {name: total.result() for name, total in sums.items()}

    def out(piece):
        top_piece, low_piece = piece("top_").astype(F32), piece("low_").astype(F32)
        whole = jnp.zeros((layers,) + top_piece.shape, F32).at[1].set(top_piece)
        return whole.at[0].set(low_piece)

    def columns(low, count):
        return out(lambda layer: sums[layer + "two"][:, low : low + count])

    def vec_out(offset, count):
        return out(lambda layer: sums[layer + "two"][offset : offset + count, at:][:, :128].reshape(count * 128))

    def down_rows(layer):
        return jnp.concatenate(jnp.split(sums[layer + "two"][:, :hidden], hidden // width, axis=1), axis=0)

    cut = both - hidden
    mid = hidden + 3 * width - cut
    at = mid + 2 * width
    a = width // 256
    u = hidden // 256
    return (
        boundary_out,
        columns(mid + width, width),
        out(lambda layer: jnp.concatenate([sums[layer + "one"][:, hidden:], sums[layer + "two"][:, hidden:mid]], axis=1)),
        vec_out(0, 2 * a),
        columns(mid, width),
        vec_out(2 * a, a),
        vec_out(3 * a, a),
        vec_out(4 * a, a),
        out(lambda layer: sums[layer + "one"][:, :hidden]),
        vec_out(16, u),
        out(down_rows),
        vec_out(16 + u, a),
        vec_out(16 + u + a, a),
        vec_out(16 + u + 2 * a, a),
    )


def solution(mesh):
    rows, vector = P(None, "pipe", None), P(None, "pipe")
    both = P("pipe", "dp", None)
    params = (rows, rows, vector, rows, vector, vector, vector, rows, vector, rows, vector, vector, vector)
    return jax.shard_map(
        per_device,
        mesh=mesh,
        in_specs=(both,) + params + (P("dp", None),),
        out_specs=(both,) + params,
        check_vma=False,
    )
```

```python
import functools
import math

import jax
import jax.numpy as jnp
from jax import lax
from jax.experimental import pallas as pl
from jax.experimental.pallas import tpu as pltpu
from jax.sharding import PartitionSpec as P

HEADS = 8
EPS = 1e-05
MASKED = -1e30
REACH = 256
BLOCK = 128
F32, BF16 = jnp.float32, jnp.bfloat16
GELU_C = math.sqrt(2.0 / math.pi)
ROOM = 8 * 1024 * 1024
AHEAD = 24 * 1024 * 1024


def nn(a, b):
    return lax.dot_general(a, b, (((1,), (0,)), ((), ())), preferred_element_type=F32)


def nt(a, b):
    return lax.dot_general(a, b, (((1,), (1,)), ((), ())), preferred_element_type=F32)


def col_sums(x):
    return jnp.sum(x.reshape(x.shape[0] // 8, 8, x.shape[1]), axis=0)


def block(body):
    pl.when(lax.axis_index("dp") < 1 << 20)(body)


class Copies:
    def __init__(self, sems):
        self.sems, self.count, self.open = sems, 0, []

    def reserve(self, ends):
        number = self.count
        self.count += 1

        def make():
            source, target = ends()
            return pltpu.make_async_copy(source, target, self.sems.at[number])

        self.open.append(make)
        return make

    def start(self, ends):
        make = self.reserve(ends)
        make().start()
        return make

    def wait(self, *made):
        for make in made:
            make().wait()
            self.open = [other for other in self.open if other is not make]

    def finish(self):
        self.wait(*list(self.open))


class Vectors:
    def __init__(self, own, other, part, sizes):
        self.own, self.other, self.part, self.sizes = own, other, part, sizes

    def get(self, layer, name):
        at = 0
        for key, size in self.sizes:
            if key == name:
                break
            at += size
        own = self.own[:, at : at + size].astype(F32)[layer : layer + 1]
        other = self.other[:, at : at + size].astype(F32)[layer : layer + 1]
        low = jnp.where(self.part == 0, own, other)
        high = jnp.where(self.part == 0, other, own)
        return jnp.concatenate([low, high], axis=1)


def halves_in(copies, own, other, layer, target, part):
    rows = own.shape[1]
    mine = pl.ds(pl.multiple_of(part * rows, rows), rows)
    theirs = pl.ds(pl.multiple_of((1 - part) * rows, rows), rows)
    return (
        lambda: copies.start(lambda: (own.at[layer], target.at[mine])),
        lambda: copies.start(lambda: (other.at[layer], target.at[theirs])),
    )


def pack_vectors(vectors, part, keep_ref, send_ref):
    keep, send = [], []
    for vector in vectors:
        half = vector.shape[1] // 2
        low, high = vector[:, :half], vector[:, half:]
        mine = jnp.where(part == 0, low, high)
        theirs = jnp.where(part == 0, high, low)
        for j in range(half // 128):
            keep.append(mine[:, j * 128 : (j + 1) * 128])
            send.append(theirs[:, j * 128 : (j + 1) * 128])
    spare = jnp.zeros((keep_ref.shape[0] - len(keep), 128), F32)
    keep_ref[...] = jnp.concatenate(keep + [spare], axis=0).astype(keep_ref.dtype)
    send_ref[...] = jnp.concatenate(send + [spare], axis=0).astype(send_ref.dtype)


def norm_stats(r):
    centred = r - jnp.mean(r, axis=-1, keepdims=True)
    scale = lax.rsqrt(jnp.mean(centred * centred, axis=-1, keepdims=True) + EPS)
    return centred * scale, scale


def norm_backward(r, g, gain):
    xhat, scale = norm_stats(r)
    gy = g * gain
    mean_one = jnp.mean(gy, axis=-1, keepdims=True)
    mean_two = jnp.mean(gy * xhat, axis=-1, keepdims=True)
    return scale * (gy - mean_one - xhat * mean_two), col_sums(g * xhat), col_sums(g)


def key_range(i):
    return max(0, i * BLOCK + 1 - REACH) // BLOCK * BLOCK, (i + 1) * BLOCK


def head_masks(scale):
    lane = lax.broadcasted_iota(jnp.int32, (1, 128), 1)
    first = jnp.where(lane < 64, scale, 0.0).astype(BF16)
    second = jnp.where(lane < 64, 0.0, scale).astype(BF16)
    return first, second


def stacked(x, masks):
    return jnp.concatenate([x * masks[0], x * masks[1]], axis=0)


def write_bias(seg_ref, bias_ref):
    length = seg_ref.shape[1]
    seg = seg_ref[...].astype(F32)
    columns = jnp.broadcast_to(seg, (128, length))
    for j in range(length // 128):
        rows = pl.ds(j * 128, 128)
        own = jnp.broadcast_to(jnp.transpose(columns[:, j * 128 : (j + 1) * 128])[:, :1], (128, length))
        key = lax.broadcasted_iota(jnp.int32, (128, length), 0) + j * 128
        query = lax.broadcasted_iota(jnp.int32, (128, length), 1)
        bias_ref[rows, :] = jnp.where((own == seg) & (key <= query), 0.0, MASKED)


def staggered(count, stages):
    held = {}
    for tick in range(count + len(stages) - 1):
        for number, stage in enumerate(stages):
            t = tick - number
            if 0 <= t < count:
                held[t] = stage(t, held.pop(t, None))


def attention_core(qkv_ref, vt_ref, bias_ref, p_ref, ot_ref, width):
    masks = head_masks(1.0 / math.sqrt(width // HEADS))
    blocks = qkv_ref.shape[0] // BLOCK

    def place(t):
        pair, i = divmod(t, blocks)
        low, high = key_range(i)
        return pair * 128, slice(i * BLOCK, (i + 1) * BLOCK), low, high

    def score(t, unused):
        lane, queries, low, high = place(t)
        q = stacked(qkv_ref[queries, lane : lane + 128], masks)
        return nt(qkv_ref[low:high, width + lane : width + lane + 128], q)

    def soften(t, s):
        lane, queries, low, high = place(t)
        bias = bias_ref[low:high, queries]
        s = s + jnp.concatenate([bias, bias], axis=1)
        e = jnp.exp(s - jnp.max(s, axis=0, keepdims=True))
        p = (e * (1.0 / jnp.sum(e, axis=0, keepdims=True))).astype(BF16)
        p_ref[t, : high - low, :] = p
        return p

    def attend(t, p):
        lane, queries, low, high = place(t)
        o = nn(vt_ref[lane : lane + 128, low:high], p)
        ot_ref[lane : lane + 64, queries] = o[:64, :BLOCK].astype(BF16)
        ot_ref[lane + 64 : lane + 128, queries] = o[64:, BLOCK:].astype(BF16)

    staggered(HEADS // 2 * blocks, (score, soften, attend))


def attention_forward(u_ref, ub_ref, w_in, w_out, vectors, layer, seg_ref, s, need, done):
    length, width = u_ref.shape
    need("seg", "w_in", "w_out")

    @block
    def _():
        write_bias(seg_ref, s.bias)
        qv = vectors.get(layer, "qv_bias")
        for j in range(3):
            bias = (qv[:, :width], 0.0, qv[:, width:])[j]
            cols = slice(j * width, (j + 1) * width)
            s.qkv[:, cols] = (nn(ub_ref[...], w_in[:, cols]) + bias).astype(BF16)
        done("qkv")
        s.vt[...] = jnp.transpose(s.qkv[:, 2 * width :])
        attention_core(s.qkv, s.vt, s.bias, s.p, s.ot, width)
        done("p", "ot")
        out_bias = vectors.get(layer, "out_bias")
        gain, shift = vectors.get(layer, "gain_one"), vectors.get(layer, "shift_one")
        r = u_ref[...] + (nn(jnp.transpose(s.ot[...]), w_out[...]) + out_bias)
        s.r1[...] = r
        done("r1")
        h = norm_stats(r)[0] * gain + shift
        s.h[...] = h
        s.hb[...] = h.astype(BF16)


def feed_forward(h_ref, hb_ref, w_up, w_down, vectors, layer, s, need, done, finish):
    width, hidden = w_up.shape
    tile = 256
    need("w_up", "hb0")

    @block
    def _():
        up_bias = vectors.get(layer, "up_bias")
        for j in range(hidden // tile):
            cols = slice(j * tile, (j + 1) * tile)
            v = nn(hb_ref[...], w_up[:, cols]) + up_bias[:, cols]
            v2 = v * v
            half = 0.5 + 0.5 * jnp.tanh(v * (GELU_C + (GELU_C * 0.044715) * v2))
            m = v * half
            s.m[:, cols] = m.astype(BF16)
            s.d[:, cols] = (half + m * (1.0 - half) * (2 * GELU_C + (6 * GELU_C * 0.044715) * v2)).astype(BF16)
        done("m", "d")

    need("w_down", "h0", "pos")

    @block
    def _():
        down_bias = vectors.get(layer, "down_bias")
        gain, shift = vectors.get(layer, "gain_two"), vectors.get(layer, "shift_two")
        r = h_ref[...] + (nn(s.m[...], w_down[...]) + down_bias)
        s.r2[...] = r
        done("r2")
        finish(norm_stats(r)[0] * gain + shift)


def feed_backward(g_ref, r2_ref, hb_ref, m_ref, d_ref, w_up, w_down, vectors, layer, plan, part, s, need, done):
    length, width = r2_ref.shape
    hidden = w_up.shape[1]
    tile = 256
    need("g", "r2")

    @block
    def _():
        gain = vectors.get(layer, "gain_two")
        dr, d_gain, d_shift = norm_backward(r2_ref[...], g_ref[...].astype(F32), gain)
        df = dr.astype(BF16)
        s.dh[...] = dr
        s.df[...] = df
        s.sums[0:8, :] = d_gain
        s.sums[8:16, :] = d_shift
        s.sums[16:24, :] = col_sums(df.astype(F32))

    need("w_down", "d")

    @block
    def _():
        d_up = []
        for j in range(hidden // tile):
            cols = slice(j * tile, (j + 1) * tile)
            dz = (nt(s.df[...], w_down[cols, :]) * d_ref[:, cols].astype(F32)).astype(BF16)
            s.dz[:, cols] = dz
            d_up.append(col_sums(dz.astype(F32)))
        parts = [jnp.concatenate(d_up, axis=1), s.sums[16:24, :], s.sums[0:8, :], s.sums[8:16, :]]
        pack_vectors([jnp.sum(x, axis=0, keepdims=True) for x in parts], part, s.feed_keep, s.feed_send)

    need("hb", "m")

    @block
    def _():
        s.hbt[...] = jnp.transpose(hb_ref[...])
        half, rows = width // 2, hidden // 2
        for which, end in ((1 - part, "_send"), (part, "_keep")):
            left = s.hbt[pl.ds(pl.multiple_of(which * half, half), half), :]
            for number, column, low, high in pieces_of(plan, "up"):
                key = f"g{number}{end}"
                into = getattr(s, key)
                for at in range(low, high, 512):
                    into[:, column + at - low : column + at - low + 512] = nn(left, s.dz[:, at : at + 512]).astype(BF16)
                done(key, column, column + high - low)
            for number, column, low, high in pieces_of(plan, "down"):
                key = f"g{number}{end}"
                into = getattr(s, key)
                for at in range(low, high, width):
                    row = pl.multiple_of(which * rows + at // width * half, half)
                    left = jnp.transpose(m_ref[:, pl.ds(row, half)])
                    into[:, column + at - low : column + at - low + width] = nn(left, s.df[...]).astype(BF16)
                done(key, column, column + high - low)

    need("w_up")


def attention_backward(
    dh_ref, r1_ref, ub_ref, ot_ref, qkv_ref, p_ref, w_in, w_out, w_up, vectors, layer, plan, part, s, need, done
):
    need("r1", "w_out", "qkv", "p", "w_in", "ub", "ot")
    block(lambda: attention_gradients(
        dh_ref, r1_ref, ub_ref, ot_ref, qkv_ref, p_ref, w_in, w_out, w_up, vectors, layer, plan, part, s, done
    ))


def attention_gradients(
    dh_ref, r1_ref, ub_ref, ot_ref, qkv_ref, p_ref, w_in, w_out, w_up, vectors, layer, plan, part, s, done
):
    length, width = r1_ref.shape
    s.dh[...] += nt(s.dz[...], w_up[...])
    gain = vectors.get(layer, "gain_one")
    dr, d_gain, d_shift = norm_backward(r1_ref[...], dh_ref[...], gain)
    da = dr.astype(BF16)
    s.du[...] = dr
    s.da[...] = da
    d_out = col_sums(da.astype(F32))
    s.do[...] = nt(s.da[...], w_out[...]).astype(BF16)
    s.kt[...] = jnp.transpose(qkv_ref[:, width : 2 * width])
    scale = 1.0 / math.sqrt(width // HEADS)
    q_masks, o_masks = head_masks(scale), head_masks(1.0)
    blocks = length // BLOCK
    dk, dv = {}, {}

    def place(t):
        pair, i = divmod(t, blocks)
        low, high = key_range(i)
        return pair * 128, slice(i * BLOCK, (i + 1) * BLOCK), low, high

    def to_p(t, unused):
        lane, queries, low, high = place(t)
        do = stacked(s.do[queries, lane : lane + 128], o_masks)
        return nt(qkv_ref[low:high, 2 * width + lane : 2 * width + lane + 128], do), do

    def to_s(t, held):
        lane, queries, low, high = place(t)
        dp, do = held
        pb = p_ref[t, : high - low, :]
        p = pb.astype(F32)
        weighted = dp * p
        ds = (weighted - p * jnp.sum(weighted, axis=0, keepdims=True)).astype(BF16)
        return ds, pb, do

    def to_qkv(t, held):
        lane, queries, low, high = place(t)
        ds, pb, do = held
        q = stacked(qkv_ref[queries, lane : lane + 128], q_masks)
        more_v, more_k = nn(pb, do), nn(ds, q)
        for b in range(low // BLOCK, high // BLOCK):
            piece = slice(b * BLOCK - low, (b + 1) * BLOCK - low)
            dk[lane, b] = dk[lane, b] + more_k[piece] if (lane, b) in dk else more_k[piece]
            dv[lane, b] = dv[lane, b] + more_v[piece] if (lane, b) in dv else more_v[piece]
        dq = nn(s.kt[lane : lane + 128, low:high], ds) * scale
        s.dqt[lane : lane + 64, queries] = dq[:64, :BLOCK].astype(BF16)
        s.dqt[lane + 64 : lane + 128, queries] = dq[64:, BLOCK:].astype(BF16)
        if high == length:
            for b in range(blocks):
                keys = slice(b * BLOCK, (b + 1) * BLOCK)
                s.dqkv[keys, width + lane : width + lane + 128] = dk[lane, b].astype(BF16)
                s.dqkv[keys, 2 * width + lane : 2 * width + lane + 128] = dv[lane, b].astype(BF16)

    staggered(HEADS // 2 * blocks, (to_p, to_s, to_qkv))
    s.dqkv[:, :width] = jnp.transpose(s.dqt[...])
    d_query = col_sums(s.dqkv[:, :width].astype(F32))
    d_value = col_sums(s.dqkv[:, 2 * width :].astype(F32))
    s.du[...] += nt(s.dqkv[...], w_in[...])
    done("du")
    s.ubt[...] = jnp.transpose(ub_ref[...])
    summed = [jnp.concatenate([d_query, d_value], axis=1), d_out, d_gain, d_shift]
    pack_vectors([jnp.sum(x, axis=0, keepdims=True) for x in summed], part, s.vec_keep, s.vec_send)
    half = width // 2
    for which, end, vec, feed in (
        (1 - part, "_send", s.vec_send, s.feed_send),
        (part, "_keep", s.vec_keep, s.feed_keep),
    ):
        at = pl.ds(pl.multiple_of(which * half, half), half)
        left = s.ubt[at, :]
        for number, parts in enumerate(plan):
            key = f"g{number}{end}"
            into = getattr(s, key)
            column, first = 0, None
            for kind, low, high in parts:
                here = slice(column, column + high - low)
                if kind in ("up", "down"):
                    column += high - low
                    continue
                first = column if first is None else first
                if kind == "in":
                    for j in range(low, high, 512):
                        k = min(high, j + 512)
                        into[:, column + j - low : column + k - low] = nn(left, s.dqkv[:, j:k]).astype(BF16)
                elif kind == "out":
                    into[:, here] = nn(ot_ref[at, :], s.da[...]).astype(BF16)
                elif kind == "pos":
                    into[:, here] = s.du[at, :].astype(BF16)
                elif kind == "vec":
                    into[:16, here] = vec[...]
                    into[16:32, here] = feed[...]
                    into[32:, here] = jnp.zeros((half - 32, 128), BF16)
                else:
                    into[:, here] = jnp.zeros((half, 128), BF16)
                column += high - low
            done(key, first, column)


def size_of(x):
    return math.prod(x.shape) * x.dtype.itemsize


class Names:
    pass


def call(name, body, inputs, outputs, scratch, flops, after=(), loose=(), aliases={}):
    names_in, names_out, names_scratch = list(inputs), list(outputs), list(scratch)

    def kernel(*refs):
        groups = []
        at = 0
        for names, spare in ((names_in, len(after)), (names_out, 0), (names_scratch, 0)):
            group = Names()
            for key in names:
                setattr(group, key, refs[at])
                at += 1
            at += spare
            groups.append(group)
        moves = Copies(refs[at])
        body(*groups, moves)
        moves.finish()

    moved = sum(size_of(x) for x in list(inputs.values()) + list(outputs.values()))
    held = sum(size_of(x) for x in scratch.values())
    spaces = [pl.ANY if key in loose else pltpu.HBM for key in names_in]
    results = pl.pallas_call(
        kernel,
        name=name,
        out_shape=tuple(pltpu.HBM(x.shape, x.dtype) for x in outputs.values()),
        in_specs=[pl.BlockSpec(memory_space=space) for space in spaces + [pl.ANY] * len(after)],
        out_specs=tuple([pl.BlockSpec(memory_space=pltpu.HBM)] * len(outputs)),
        scratch_shapes=[pltpu.VMEM(x.shape, x.dtype) for x in scratch.values()]
        + [pltpu.SemaphoreType.DMA((len(inputs) + 2 * len(outputs),))],
        compiler_params=pltpu.CompilerParams(vmem_limit_bytes=min(60 * 1024 * 1024, held + ROOM)),
        cost_estimate=pl.CostEstimate(flops=flops, bytes_accessed=moved, transcendentals=0),
        input_output_aliases=aliases,
    )(*[pltpu.with_memory_space_constraint(x, space) for space, x in zip(spaces, inputs.values())], *after)
    return dict(zip(names_out, results))


class Loads:
    def __init__(self, copies, ahead=AHEAD):
        self.copies, self.ahead, self.waiting, self.begun = copies, ahead, [], {}

    def add(self, name, size, *starts):
        self.waiting.append((name, size, starts))

    def begin(self):
        name, size, starts = self.waiting.pop(0)
        self.begun[name] = (size, [start() for start in starts])

    def top_up(self):
        while self.waiting and sum(size for size, unused in self.begun.values()) < self.ahead:
            self.begin()

    def need(self, *names):
        for name in names:
            while any(name == entry[0] for entry in self.waiting):
                self.begin()
            if name in self.begun:
                self.copies.wait(*self.begun.pop(name)[1])
        self.top_up()


def storer(copies, s, o, names):
    def done(*keys):
        if len(keys) == 3 and not isinstance(keys[1], str):
            key, low, high = keys
            copies.start(lambda: (getattr(s, key).at[:, low:high], getattr(o, key).at[:, low:high]))
            return
        for key in keys:
            target = names.get(key, key)
            if hasattr(o, target):
                copies.start(functools.partial(lambda key, target: (getattr(s, key), getattr(o, target)), key, target))

    return done


WAYS = {
    "top0": ("xyzw", "yxzw"),
    "top1": ("zxyw", "xzyw"),
    "low0": ("xyzw", "yxzw"),
    "low1": ("zyxw", "yzxw"),
    "low2": ("xzyw", "yzxw"),
}
WAITS = {("low0", 1): ("top0", 1), ("low1", 1): ("top1", 1)}


def plan_for(layer, width, hidden):
    tail = [("out", 0, width), ("pos", 0, width), ("vec", 0, 128), ("pad", 0, 128)]
    if layer == "top":
        cut = 3 * width - 128
        return [
            [("up", 0, hidden), ("in", 0, cut)],
            [("down", 0, hidden), ("in", cut, 3 * width)] + tail,
        ]
    half = width // 2
    return [
        [("up", 0, hidden), ("in", 0, half)],
        [("down", 0, hidden), ("in", half, width)],
        [("in", width, 3 * width)] + tail,
    ]


def pieces_of(plan, kind):
    found = []
    for number, parts in enumerate(plan):
        at = 0
        for key, low, high in parts:
            if key == kind:
                found.append((number, at, low, high))
            at += high - low
    return found


def columns_of(parts):
    return sum(high - low for unused, low, high in parts)


def shape(dims, dtype):
    return jax.ShapeDtypeStruct(tuple(dims), dtype)


def other_core(value):
    return lax.ppermute(value, "pipe", [(0, 1), (1, 0)])


class Reduction:
    def __init__(self, parts, orders):
        self.arrived = [parts[1]]
        self.parts, self.steps, self.at = parts, list(zip(*orders)), 0

    def mirrored(self, x, shifts):
        size = lax.axis_size("dp")
        pairs = [(2 * i + c, 2 * (i ^ (1 << shifts[c])) + c) for i in range(size) for c in range(2)]
        return lax.ppermute(x, ("dp", "pipe"), pairs)

    def side(self, shifts):
        part = lax.axis_index("pipe")
        return lax.shift_right_logical(lax.axis_index("dp"), jnp.where(part == 0, shifts[0], shifts[1])) & 1

    def joined(self):
        value, other = self.parts
        low = self.side(self.steps[2 * len(self.steps) - 1 - self.at]) == 0
        return jnp.concatenate([jnp.where(low, value, other), jnp.where(low, other, value)], axis=0)

    def complete(self):
        return self.at == 2 * len(self.steps) - 1

    def step(self, waits=()):
        def tie(x):
            for other in waits:
                nothing = jnp.minimum(jnp.abs(other[:1, : x.shape[1]]), 0)
                times = -(-x.shape[1] // nothing.shape[1])
                x = x + jnp.broadcast_to(jnp.concatenate([nothing] * times, axis=1)[:, : x.shape[1]], x.shape)
            return x

        inner = len(self.steps) - 1
        if self.at < inner:
            shifts = self.steps[self.at]
            half = self.parts[0].shape[0] // 2
            bit = self.side(shifts)
            theirs, mine = [
                functools.reduce(
                    jnp.add, [lax.dynamic_slice_in_dim(x, which * half, half, 0) for x in self.parts]
                )
                for which in (1 - bit, bit)
            ]
            self.parts = [mine, self.mirrored(tie(theirs), shifts)]
        elif self.at == inner:
            value = self.parts[0] + self.parts[1]
            self.parts = [value, self.mirrored(tie(value), self.steps[inner])]
        else:
            value = self.parts[0] + self.parts[1] if self.at == inner + 1 else self.joined()
            self.parts = [value, self.mirrored(tie(value), self.steps[2 * inner - self.at])]
        self.arrived.append(self.parts[1])
        self.at += 1

    def result(self):
        return self.joined()


def orders_for(size, ways):
    bits = list(range(size.bit_length() - 1))
    side_bits = (len(bits) - 1) // 3
    x, y, z = bits[:side_bits], bits[side_bits : 2 * side_bits], bits[2 * side_bits :]
    runs = {"x": x, "y": y, "z": z[:1], "w": z[1:]}
    return [sum([runs[letter] for letter in way], []) for way in ways]


def per_device(
    boundary,
    positions,
    w_in,
    qv_bias,
    w_out,
    out_bias,
    gain_one,
    shift_one,
    w_up,
    up_bias,
    w_down,
    down_bias,
    gain_two,
    shift_two,
    segment_ids,
):
    part = lax.axis_index("pipe")
    window_count, length = segment_ids.shape
    layers, half, width = positions.shape
    hidden = w_up.shape[2]
    blocks = length // BLOCK

    small = (qv_bias, out_bias, gain_one, shift_one, up_bias, down_bias, gain_two, shift_two)
    small_names = ("qv_bias", "out_bias", "gain_one", "shift_one", "up_bias", "down_bias", "gain_two", "shift_two")
    sizes = [(key, x.shape[1]) for key, x in zip(small_names, small)]
    vec = jnp.concatenate(small, axis=1)
    windows = boundary.reshape(window_count, length, width)
    got = other_core(lax.dynamic_index_in_dim(windows, 1 - part, 0, keepdims=False))
    vec2, pos2, w_in2, w_out2 = other_core(vec), other_core(positions), other_core(w_in), other_core(w_out)
    late = lax.optimization_barrier((w_up, w_down, got, vec2, pos2, w_in2, w_out2))
    w_up2, w_down2 = other_core(late[0]), other_core(late[1])
    seg = lax.dynamic_index_in_dim(segment_ids, part, 0, keepdims=True)

    square, wide = (length, width), (length, hidden)
    qkv_shape, p_shape = (length, 3 * width), (HEADS // 2 * blocks, min(length, REACH + BLOCK), 2 * BLOCK)
    vec_in = dict(vec=vec, vec2=vec2)
    vec_scratch = dict(vec=shape(vec.shape, BF16), vec2=shape(vec.shape, BF16))
    attention_in = dict(pos=positions, pos2=pos2, w_in=w_in, w_in2=w_in2, w_out=w_out, w_out2=w_out2, seg=seg)
    attention_out = dict(
        ub=shape(square, BF16), qkv=shape(qkv_shape, BF16), p=shape(p_shape, BF16), ot=shape(square, BF16),
        r1=shape(square, F32),
    )
    hidden_out = dict(h=shape(square, F32), hb=shape(square, BF16))
    attention_weights = dict(w_in=shape((width, 3 * width), BF16), w_out=shape((width, width), BF16))
    attention_scratch = dict(
        pos=shape(square, BF16), seg=shape(seg.shape, seg.dtype), u=shape(square, F32), vt=shape(square, BF16),
        bias=shape((length, length), F32), **attention_weights, **attention_out, **hidden_out,
    )
    feed_in = dict(w_up=w_up, w_up2=w_up2, w_down=w_down, w_down2=w_down2)
    feed_weights = dict(w_up=shape((width, hidden), BF16), w_down=shape((hidden, width), BF16))
    feed_out = dict(m=shape(wide, BF16), d=shape(wide, BF16), r2=shape(square, F32))
    plans = {layer: plan_for(layer, width, hidden) for layer in ("top", "low")}
    gradients = {
        layer: {
            f"g{number}{end}": shape((half, columns_of(parts)), BF16)
            for number, parts in enumerate(plan) for end in ("_keep", "_send")
        }
        for layer, plan in plans.items()
    }
    vec_grads = {key + end: shape((16, 128), BF16) for key in ("vec", "feed") for end in ("_keep", "_send")}
    back_scratch = dict(
        dh=shape(square, F32), df=shape(square, BF16), dz=shape(wide, BF16), hbt=shape(square, BF16),
        du=shape(square, F32), da=shape(square, BF16), do=shape(square, BF16), kt=shape(square, BF16),
        dqt=shape(square, BF16), dqkv=shape(qkv_shape, BF16), ubt=shape(square, BF16), sums=shape((24, width), F32), **vec_grads,
    )
    flops_attention = 2 * length * width * (4 * width + length)
    flops_feed = 4 * length * width * hidden

    def load_halves(i, s, loads, layer, keys, place, names={}):
        for key in keys:
            target = getattr(s, names.get(key, key))
            loads.add(
                names.get(key, key), size_of(target),
                *halves_in(loads.copies, getattr(i, key), getattr(i, key + "2"), layer, target, place),
            )

    def load(i, s, loads, keys):
        for key in keys:
            target = getattr(s, key)
            ends = functools.partial(lambda source, target: (source, target), getattr(i, key), target)
            loads.add(key, size_of(target), functools.partial(loads.copies.start, ends))

    def window_in(i, copies, place, owner, target):
        make = copies.reserve(lambda: (i.got, target))

        @pl.when(place == owner)
        def _():
            at = pl.ds(pl.multiple_of(place * length, length), length)
            pltpu.make_async_copy(i.rows.at[0, at], target, copies.sems.at[copies.count - 1]).start()

        @pl.when(place != owner)
        def _():
            make().start()

        return make

    def vectors_of(s, need, place):
        need("vec", "vec2")
        return Vectors(s.vec, s.vec2, place, sizes)

    def attention_first(i, o, s, copies):
        place = lax.axis_index("pipe")
        loads = Loads(copies)
        load(i, s, loads, ["vec", "vec2"])
        loads.add("x", size_of(s.x), lambda: window_in(i, copies, place, 0, s.x))
        load_halves(i, s, loads, 0, ["pos"], place)
        load(i, s, loads, ["seg"])
        load_halves(i, s, loads, 0, ["w_in", "w_out"], place)
        need, done = loads.need, storer(copies, s, o, {})
        vectors = vectors_of(s, need, place)
        need("x", "pos")

        @block
        def _():
            u = s.x[...] + s.pos[...].astype(F32)
            s.u[...] = u
            s.ub[...] = u.astype(BF16)
            done("ub")

        attention_forward(s.u, s.ub, s.w_in, s.w_out, vectors, 0, s.seg, s, need, done)
        done("h", "hb")

    first = call(
        "attention_first", attention_first,
        dict(rows=boundary, got=got, **vec_in, **attention_in),
        dict(**attention_out, **hidden_out),
        dict(x=shape(square, F32), **vec_scratch, **attention_scratch),
        10 * flops_attention,
    )

    def middle(i, o, s, copies):
        place = lax.axis_index("pipe")
        loads = Loads(copies)
        load(i, s, loads, ["vec", "vec2", "hb0"])
        load_halves(i, s, loads, 0, ["w_up"], place)
        load(i, s, loads, ["h0"])
        load_halves(i, s, loads, 0, ["w_down"], place)
        load_halves(i, s, loads, 1, ["pos"], place)
        load(i, s, loads, ["seg"])
        load_halves(i, s, loads, 1, ["w_in", "w_out"], place)
        loads.add("g", size_of(s.g), lambda: window_in(i, copies, place, 1, s.g))
        need, done = loads.need, storer(copies, s, o, {"ub": "", "qkv": "", "p": "", "ot": "", "r1": ""})
        vectors = vectors_of(s, need, place)

        def into_last(y):
            u = y.astype(BF16).astype(F32) + s.pos[...].astype(F32)
            s.u[...] = u
            s.ub[...] = u.astype(BF16)

        feed_forward(s.h0, s.hb0, s.w_up, s.w_down, vectors, 0, s, need, done, into_last)
        load_halves(i, s, loads, 1, ["w_up", "w_down"], place)
        attention_forward(s.u, s.ub, s.w_in, s.w_out, vectors, 1, s.seg, s, need, done)
        t = Names()
        t.__dict__.update(s.__dict__)
        t.m, t.d, t.r2 = s.last_m, s.last_d, s.last_r2
        done = storer(copies, s, o, {"m": "", "d": "", "r2": ""})

        def out_last(y):
            s.y[...] = y
            done("y")

        feed_forward(s.h, s.hb, s.w_up, s.w_down, vectors, 1, t, need, done, out_last)
        feed_backward(s.g, t.r2, s.hb, t.m, t.d, s.w_up, s.w_down, vectors, 1, plans["top"], place, t, need, done)

        def done_low(*keys):
            if keys == ("du",):
                s.gout[...] = s.du[...].astype(BF16)
                copies.start(lambda: (s.gout, o.g))
            else:
                done(*keys)

        attention_backward(
            s.dh, s.r1, s.ub, s.ot, s.qkv, s.p, s.w_in, s.w_out, s.w_up, vectors, 1, plans["top"], place, s, need, done_low
        )

    top = call(
        "middle", middle,
        dict(h0=first["h"], hb0=first["hb"], rows=boundary, got=got, **vec_in, **attention_in, **feed_in),
        dict(**feed_out, y=shape(square, F32), g=shape(square, BF16), **gradients["top"]),
        dict(
            h0=shape(square, F32), hb0=shape(square, BF16), g=shape(square, F32), gout=shape(square, BF16),
            y=shape(square, F32), **vec_scratch, **attention_scratch, **feed_weights, **feed_out,
            last_m=feed_out["m"], last_d=feed_out["d"], last_r2=feed_out["r2"], **back_scratch, **gradients["top"],
        ),
        20 * flops_feed,
    )

    def lowest(i, o, s, copies):
        place = lax.axis_index("pipe")
        loads = Loads(copies)
        load(i, s, loads, ["vec", "vec2", "g", "r2"])
        load_halves(i, s, loads, 0, ["w_down"], place)
        load(i, s, loads, ["d", "hb", "m"])
        load_halves(i, s, loads, 0, ["w_up"], place)
        load(i, s, loads, ["r1"])
        load_halves(i, s, loads, 0, ["w_out"], place)
        load(i, s, loads, ["qkv", "p"])
        load_halves(i, s, loads, 0, ["w_in"], place)
        load(i, s, loads, ["ub", "ot"])
        need, done = loads.need, storer(copies, s, o, {})
        vectors = vectors_of(s, need, place)
        feed_backward(s.g, s.r2, s.hb, s.m, s.d, s.w_up, s.w_down, vectors, 0, plans["low"], place, s, need, done)
        attention_backward(
            s.dh, s.r1, s.ub, s.ot, s.qkv, s.p, s.w_in, s.w_out, s.w_up, vectors, 0, plans["low"], place, s, need, done
        )

    sums = {}

    def begin_sums(layer, kernel):
        for number in range(len(plans[layer])):
            name = f"{layer}{number}"
            keep, send = kernel[f"g{number}_keep"], kernel[f"g{number}_send"]
            sums[name] = Reduction([keep, other_core(send)], orders_for(lax.axis_size("dp"), WAYS[name]))

    begin_sums("top", top)
    low = call(
        "lowest", lowest,
        dict(
            g=top["g"], **{key: top[key] for key in feed_out}, hb=first["hb"],
            **{key: first[key] for key in attention_out}, **vec_in, **feed_in,
            w_in=w_in, w_in2=w_in2, w_out=w_out, w_out2=w_out2,
        ),
        dict(du=shape(square, F32), **gradients["low"]),
        dict(
            g=shape(square, BF16), hb=shape(square, BF16), **vec_scratch, **attention_weights, **attention_out,
            **feed_weights, **feed_out, **back_scratch, **gradients["low"],
        ),
        12 * flops_feed, after=[total.arrived[0] for total in sums.values()],
    )
    begin_sums("low", low)
    while not all(total.complete() for total in sums.values()):
        for name, total in sums.items():
            wait = WAITS.get((name, total.at + 1)) if len(total.steps) == 4 else None
            ready = wait is None or len(sums[wait[0]].arrived) > wait[1]
            if ready and not total.complete():
                total.step([sums[wait[0]].arrived[wait[1]]] if wait else [])

    theirs = other_core(jnp.where(part == 0, top["y"], low["du"]))
    boundary_out = jnp.stack(
        [jnp.where(part == 0, low["du"], theirs), jnp.where(part == 0, theirs, top["y"])]
    ).reshape(1, window_count * length, width)

    units, more = width // 256, hidden // 256
    big = dict(
        pos=shape((layers, half, width), F32), w_in=shape((layers, half, 3 * width), F32),
        out=shape((layers, half, width), F32), up=shape((layers, half, hidden), F32),
        down=shape((layers, hidden // 2, width), F32),
    )
    big["in"] = big.pop("w_in")
    runs = dict(
        qv_bias=(0, 2 * units), out_bias=(2 * units, units), gain_one=(3 * units, units), shift_one=(4 * units, units),
        up_bias=(16, more), down_bias=(16 + more, units), gain_two=(16 + more + units, units),
        shift_two=(16 + more + 2 * units, units),
    )
    small_out = {key: shape((layers, 128 * count), F32) for key, (unused, count) in runs.items()}

    def lower_side(name, place):
        shifts = sums[name].steps[0]
        return (lax.shift_right_logical(lax.axis_index("dp"), jnp.where(place == 0, *shifts)) & 1) == 0

    def assemble(name, layer, parts, extra, so_far):
        kinds = [kind for kind, unused, unused_too in parts if kind in big]
        rows = half // 2

        def body(i, o, s, copies):
            place = lax.axis_index("pipe")
            loads = Loads(copies)
            low = lower_side(name, place).astype(jnp.int32)
            for key, row in (("value", (1 - low) * rows), ("other", low * rows)):
                at = pl.ds(pl.multiple_of(row, rows), rows)
                ends = functools.partial(lambda a, b, at: (a, b.at[at]), getattr(i, key), s.whole, at)
                loads.add(key, size_of(s.whole) // 2, functools.partial(copies.start, ends))
            for key in extra:
                column = pieces_of(plans["top"], "vec")[0][1]
                ends = functools.partial(
                    lambda a, b, column: (a.at[:32, column : column + 128], b), getattr(i, key), getattr(s, key), column
                )
                loads.add(key, 8192, functools.partial(copies.start, ends))
            loads.need("value", "other", *extra)

            def store(key, low, high):
                if key in ("in", "up"):
                    copies.start(lambda: (getattr(s, key), getattr(o, key).at[layer, :, low:high]))
                else:
                    copies.start(lambda: (getattr(s, key), getattr(o, key).at[layer]))

            @block
            def _():
                column = 0
                for kind, low, high in parts:
                    here = slice(column, column + high - low)
                    if kind == "down":
                        for j in range(hidden // width):
                            one = s.whole[:, column + j * width : column + (j + 1) * width]
                            s.down[j * half : (j + 1) * half, :] = one.astype(F32)
                    elif kind in big:
                        getattr(s, kind)[...] = s.whole[:, here].astype(F32)
                    if kind in big:
                        store(kind, low, high)
                    if kind == "vec" and extra:
                        side = lower_side("top1", place)
                        upper = jnp.where(side, s.last_value[...].astype(F32), s.last_other[...].astype(F32))
                        lower = s.whole[:32, here].astype(F32)
                        for key, (at, count) in runs.items():
                            lines = [
                                jnp.concatenate([x[at + j : at + j + 1] for j in range(count)], axis=1)
                                for x in (lower, upper)
                            ]
                            getattr(s, key)[...] = jnp.concatenate(lines, axis=0)
                            copies.start(functools.partial(lambda key: (getattr(s, key), getattr(o, key)), key))
                    column += high - low

        values = dict(zip(("value", "other"), sums[name].parts))
        before = {key: so_far[key] for key in kinds if key in so_far}
        outputs = {**{key: big[key] for key in kinds}, **(small_out if extra else {})}
        scratch = {
            kind: shape(big[kind].shape[1:] if kind == "down" else (half, high - low), F32)
            for kind, low, high in parts if kind in big
        }
        return call(
            "assemble_" + name, body, {**values, **extra, **before}, outputs,
            dict(
                whole=shape((half, columns_of(parts)), BF16), **{key: shape((32, 128), BF16) for key in extra},
                **scratch, **(small_out if extra else {}),
            ),
            flops_feed, loose=list(values) + list(extra),
            aliases={len(values) + len(extra) + n: list(outputs).index(key) for n, key in enumerate(before)},
        )

    result = {}
    for number, parts in enumerate(plans["top"]):
        result.update(assemble(f"top{number}", 1, parts, {}, result))
    last = dict(zip(("last_value", "last_other"), sums["top1"].parts))
    for number, parts in enumerate(plans["low"]):
        extra = last if any(kind == "vec" for kind, unused, unused_too in parts) else {}
        result.update(assemble(f"low{number}", 0, parts, extra, result))
    order = ("pos", "in", "qv_bias", "out", "out_bias", "gain_one", "shift_one", "up", "up_bias", "down", "down_bias",
             "gain_two", "shift_two")
    return (boundary_out,) + tuple(result[key] for key in order)


def solution(mesh):
    rows, vector = P(None, "pipe", None), P(None, "pipe")
    both = P("pipe", "dp", None)
    params = (rows, rows, vector, rows, vector, vector, vector, rows, vector, rows, vector, vector, vector)
    return jax.shard_map(
        per_device,
        mesh=mesh,
        in_specs=(both,) + params + (P("dp", None),),
        out_specs=(both,) + params,
        check_vma=False,
    )
```

```python
import functools
import math

import jax
import jax.numpy as jnp
from jax import lax
from jax.experimental import pallas as pl
from jax.experimental.pallas import tpu as pltpu
from jax.sharding import PartitionSpec as P

HEADS = 8
EPS = 1e-05
MASKED = -1e30
REACH = 256
BLOCK = 128
F32, BF16 = jnp.float32, jnp.bfloat16
GELU_C = math.sqrt(2.0 / math.pi)
ROOM = 8 * 1024 * 1024
AHEAD = 24 * 1024 * 1024


def nn(a, b):
    return lax.dot_general(a, b, (((1,), (0,)), ((), ())), preferred_element_type=F32)


def nt(a, b):
    return lax.dot_general(a, b, (((1,), (1,)), ((), ())), preferred_element_type=F32)


def col_sums(x):
    return jnp.sum(x.reshape(x.shape[0] // 8, 8, x.shape[1]), axis=0)


def block(body):
    pl.when(lax.axis_index("dp") < 1 << 20)(body)


class Copies:
    def __init__(self, sems):
        self.sems, self.count, self.open = sems, 0, []

    def reserve(self, ends):
        number = self.count
        self.count += 1

        def make():
            source, target = ends()
            return pltpu.make_async_copy(source, target, self.sems.at[number])

        self.open.append(make)
        return make

    def start(self, ends):
        make = self.reserve(ends)
        make().start()
        return make

    def wait(self, *made):
        for make in made:
            make().wait()
            self.open = [other for other in self.open if other is not make]

    def finish(self):
        self.wait(*list(self.open))


class Vectors:
    def __init__(self, own, other, part, sizes):
        self.own, self.other, self.part, self.sizes = own, other, part, sizes

    def get(self, layer, name):
        at = 0
        for key, size in self.sizes:
            if key == name:
                break
            at += size
        own = self.own[:, at : at + size].astype(F32)[layer : layer + 1]
        other = self.other[:, at : at + size].astype(F32)[layer : layer + 1]
        low = jnp.where(self.part == 0, own, other)
        high = jnp.where(self.part == 0, other, own)
        return jnp.concatenate([low, high], axis=1)


def halves_in(copies, own, other, layer, target, part):
    rows = own.shape[1]
    mine = pl.ds(pl.multiple_of(part * rows, rows), rows)
    theirs = pl.ds(pl.multiple_of((1 - part) * rows, rows), rows)
    return (
        lambda: copies.start(lambda: (own.at[layer], target.at[mine])),
        lambda: copies.start(lambda: (other.at[layer], target.at[theirs])),
    )


def pack_vectors(vectors, part, keep_ref, send_ref):
    keep, send = [], []
    for vector in vectors:
        half = vector.shape[1] // 2
        low, high = vector[:, :half], vector[:, half:]
        mine = jnp.where(part == 0, low, high)
        theirs = jnp.where(part == 0, high, low)
        for j in range(half // 128):
            keep.append(mine[:, j * 128 : (j + 1) * 128])
            send.append(theirs[:, j * 128 : (j + 1) * 128])
    spare = jnp.zeros((keep_ref.shape[0] - len(keep), 128), F32)
    keep_ref[...] = jnp.concatenate(keep + [spare], axis=0).astype(keep_ref.dtype)
    send_ref[...] = jnp.concatenate(send + [spare], axis=0).astype(send_ref.dtype)


def norm_stats(r):
    centred = r - jnp.mean(r, axis=-1, keepdims=True)
    scale = lax.rsqrt(jnp.mean(centred * centred, axis=-1, keepdims=True) + EPS)
    return centred * scale, scale


def norm_backward(r, g, gain):
    xhat, scale = norm_stats(r)
    gy = g * gain
    mean_one = jnp.mean(gy, axis=-1, keepdims=True)
    mean_two = jnp.mean(gy * xhat, axis=-1, keepdims=True)
    return scale * (gy - mean_one - xhat * mean_two), col_sums(g * xhat), col_sums(g)


def key_range(i):
    return max(0, i * BLOCK + 1 - REACH) // BLOCK * BLOCK, (i + 1) * BLOCK


def head_masks(scale):
    lane = lax.broadcasted_iota(jnp.int32, (1, 128), 1)
    first = jnp.where(lane < 64, scale, 0.0).astype(BF16)
    second = jnp.where(lane < 64, 0.0, scale).astype(BF16)
    return first, second


def stacked(x, masks):
    return jnp.concatenate([x * masks[0], x * masks[1]], axis=0)


def write_bias(seg_ref, bias_ref):
    length = seg_ref.shape[1]
    seg = seg_ref[...].astype(F32)
    columns = jnp.broadcast_to(seg, (128, length))
    for j in range(length // 128):
        rows = pl.ds(j * 128, 128)
        own = jnp.broadcast_to(jnp.transpose(columns[:, j * 128 : (j + 1) * 128])[:, :1], (128, length))
        key = lax.broadcasted_iota(jnp.int32, (128, length), 0) + j * 128
        query = lax.broadcasted_iota(jnp.int32, (128, length), 1)
        bias_ref[rows, :] = jnp.where((own == seg) & (key <= query), 0.0, MASKED)


def staggered(count, stages):
    held = {}
    for tick in range(count + len(stages) - 1):
        for number, stage in enumerate(stages):
            t = tick - number
            if 0 <= t < count:
                held[t] = stage(t, held.pop(t, None))


def attention_core(qkv_ref, vt_ref, bias_ref, p_ref, ot_ref, width):
    masks = head_masks(1.0 / math.sqrt(width // HEADS))
    blocks = qkv_ref.shape[0] // BLOCK

    def place(t):
        pair, i = divmod(t, blocks)
        low, high = key_range(i)
        return pair * 128, slice(i * BLOCK, (i + 1) * BLOCK), low, high

    def score(t, unused):
        lane, queries, low, high = place(t)
        q = stacked(qkv_ref[queries, lane : lane + 128], masks)
        return nt(qkv_ref[low:high, width + lane : width + lane + 128], q)

    def soften(t, s):
        lane, queries, low, high = place(t)
        bias = bias_ref[low:high, queries]
        s = s + jnp.concatenate([bias, bias], axis=1)
        e = jnp.exp(s - jnp.max(s, axis=0, keepdims=True))
        p = (e * (1.0 / jnp.sum(e, axis=0, keepdims=True))).astype(BF16)
        p_ref[t, : high - low, :] = p
        return p

    def attend(t, p):
        lane, queries, low, high = place(t)
        o = nn(vt_ref[lane : lane + 128, low:high], p)
        ot_ref[lane : lane + 64, queries] = o[:64, :BLOCK].astype(BF16)
        ot_ref[lane + 64 : lane + 128, queries] = o[64:, BLOCK:].astype(BF16)

    staggered(HEADS // 2 * blocks, (score, soften, attend))


def attention_forward(u_ref, ub_ref, w_in, w_out, vectors, layer, seg_ref, s, need, done):
    length, width = u_ref.shape
    need("seg", "w_in", "w_out")

    @block
    def _():
        write_bias(seg_ref, s.bias)
        qv = vectors.get(layer, "qv_bias")
        for j in range(3):
            bias = (qv[:, :width], 0.0, qv[:, width:])[j]
            cols = slice(j * width, (j + 1) * width)
            s.qkv[:, cols] = (nn(ub_ref[...], w_in[:, cols]) + bias).astype(BF16)
        done("qkv")
        s.vt[...] = jnp.transpose(s.qkv[:, 2 * width :])
        attention_core(s.qkv, s.vt, s.bias, s.p, s.ot, width)
        done("p", "ot")
        out_bias = vectors.get(layer, "out_bias")
        gain, shift = vectors.get(layer, "gain_one"), vectors.get(layer, "shift_one")
        r = u_ref[...] + (nn(jnp.transpose(s.ot[...]), w_out[...]) + out_bias)
        s.r1[...] = r
        done("r1")
        h = norm_stats(r)[0] * gain + shift
        s.h[...] = h
        s.hb[...] = h.astype(BF16)


def feed_forward(h_ref, hb_ref, w_up, w_down, vectors, layer, s, need, done, finish):
    width, hidden = w_up.shape
    tile = 256
    need("w_up", "hb0")

    @block
    def _():
        up_bias = vectors.get(layer, "up_bias")
        for j in range(hidden // tile):
            cols = slice(j * tile, (j + 1) * tile)
            v = nn(hb_ref[...], w_up[:, cols]) + up_bias[:, cols]
            v2 = v * v
            half = 0.5 + 0.5 * jnp.tanh(v * (GELU_C + (GELU_C * 0.044715) * v2))
            m = v * half
            s.m[:, cols] = m.astype(BF16)
            s.d[:, cols] = (half + m * (1.0 - half) * (2 * GELU_C + (6 * GELU_C * 0.044715) * v2)).astype(BF16)
        done("m", "d")

    need("w_down", "h0", "pos")

    @block
    def _():
        down_bias = vectors.get(layer, "down_bias")
        gain, shift = vectors.get(layer, "gain_two"), vectors.get(layer, "shift_two")
        r = h_ref[...] + (nn(s.m[...], w_down[...]) + down_bias)
        s.r2[...] = r
        done("r2")
        finish(norm_stats(r)[0] * gain + shift)


def feed_backward(g_ref, r2_ref, hb_ref, m_ref, d_ref, w_up, w_down, vectors, layer, plan, part, s, need, done):
    length, width = r2_ref.shape
    hidden = w_up.shape[1]
    tile = 256
    need("g", "r2")

    @block
    def _():
        gain = vectors.get(layer, "gain_two")
        dr, d_gain, d_shift = norm_backward(r2_ref[...], g_ref[...].astype(F32), gain)
        df = dr.astype(BF16)
        s.dh[...] = dr
        s.df[...] = df
        s.sums[0:8, :] = d_gain
        s.sums[8:16, :] = d_shift
        s.sums[16:24, :] = col_sums(df.astype(F32))

    need("w_down", "d")

    @block
    def _():
        d_up = []
        for j in range(hidden // tile):
            cols = slice(j * tile, (j + 1) * tile)
            dz = (nt(s.df[...], w_down[cols, :]) * d_ref[:, cols].astype(F32)).astype(BF16)
            s.dz[:, cols] = dz
            d_up.append(col_sums(dz.astype(F32)))
        parts = [jnp.concatenate(d_up, axis=1), s.sums[16:24, :], s.sums[0:8, :], s.sums[8:16, :]]
        pack_vectors([jnp.sum(x, axis=0, keepdims=True) for x in parts], part, s.feed_keep, s.feed_send)

    need("hb", "m")

    @block
    def _():
        s.hbt[...] = jnp.transpose(hb_ref[...])
        half, rows = width // 2, hidden // 2
        for which, end in ((1 - part, "_send"), (part, "_keep")):
            left = s.hbt[pl.ds(pl.multiple_of(which * half, half), half), :]
            for number, column, low, high in pieces_of(plan, "up"):
                key = f"g{number}{end}"
                into = getattr(s, key)
                for at in range(low, high, 512):
                    into[:, column + at - low : column + at - low + 512] = nn(left, s.dz[:, at : at + 512]).astype(BF16)
                done(key, column, column + high - low)
            for number, column, low, high in pieces_of(plan, "down"):
                key = f"g{number}{end}"
                into = getattr(s, key)
                for at in range(low, high, width):
                    row = pl.multiple_of(which * rows + at // width * half, half)
                    left = jnp.transpose(m_ref[:, pl.ds(row, half)])
                    into[:, column + at - low : column + at - low + width] = nn(left, s.df[...]).astype(BF16)
                done(key, column, column + high - low)

    need("w_up")


def attention_backward(
    dh_ref, r1_ref, ub_ref, ot_ref, qkv_ref, p_ref, w_in, w_out, w_up, vectors, layer, plan, part, s, need, done
):
    need("r1", "w_out", "qkv", "p", "w_in", "ub", "ot")
    block(lambda: attention_gradients(
        dh_ref, r1_ref, ub_ref, ot_ref, qkv_ref, p_ref, w_in, w_out, w_up, vectors, layer, part, s, done
    ))
    block(lambda: attention_weight_gradients(ot_ref, 1 - part, "_send", plan, s, done))
    block(lambda: attention_weight_gradients(ot_ref, part, "_keep", plan, s, done))


def attention_gradients(
    dh_ref, r1_ref, ub_ref, ot_ref, qkv_ref, p_ref, w_in, w_out, w_up, vectors, layer, part, s, done
):
    length, width = r1_ref.shape
    s.dh[...] += nt(s.dz[...], w_up[...])
    gain = vectors.get(layer, "gain_one")
    dr, d_gain, d_shift = norm_backward(r1_ref[...], dh_ref[...], gain)
    da = dr.astype(BF16)
    s.du[...] = dr
    s.da[...] = da
    d_out = col_sums(da.astype(F32))
    s.do[...] = nt(s.da[...], w_out[...]).astype(BF16)
    s.kt[...] = jnp.transpose(qkv_ref[:, width : 2 * width])
    scale = 1.0 / math.sqrt(width // HEADS)
    q_masks, o_masks = head_masks(scale), head_masks(1.0)
    blocks = length // BLOCK
    dk, dv = {}, {}

    def place(t):
        pair, i = divmod(t, blocks)
        low, high = key_range(i)
        return pair * 128, slice(i * BLOCK, (i + 1) * BLOCK), low, high

    def to_p(t, unused):
        lane, queries, low, high = place(t)
        do = stacked(s.do[queries, lane : lane + 128], o_masks)
        return nt(qkv_ref[low:high, 2 * width + lane : 2 * width + lane + 128], do), do

    def to_s(t, held):
        lane, queries, low, high = place(t)
        dp, do = held
        pb = p_ref[t, : high - low, :]
        p = pb.astype(F32)
        weighted = dp * p
        ds = (weighted - p * jnp.sum(weighted, axis=0, keepdims=True)).astype(BF16)
        return ds, pb, do

    def to_qkv(t, held):
        lane, queries, low, high = place(t)
        ds, pb, do = held
        q = stacked(qkv_ref[queries, lane : lane + 128], q_masks)
        more_v, more_k = nn(pb, do), nn(ds, q)
        for b in range(low // BLOCK, high // BLOCK):
            piece = slice(b * BLOCK - low, (b + 1) * BLOCK - low)
            dk[lane, b] = dk[lane, b] + more_k[piece] if (lane, b) in dk else more_k[piece]
            dv[lane, b] = dv[lane, b] + more_v[piece] if (lane, b) in dv else more_v[piece]
        dq = nn(s.kt[lane : lane + 128, low:high], ds) * scale
        s.dqt[lane : lane + 64, queries] = dq[:64, :BLOCK].astype(BF16)
        s.dqt[lane + 64 : lane + 128, queries] = dq[64:, BLOCK:].astype(BF16)
        if high == length:
            for b in range(blocks):
                keys = slice(b * BLOCK, (b + 1) * BLOCK)
                s.dqkv[keys, width + lane : width + lane + 128] = dk[lane, b].astype(BF16)
                s.dqkv[keys, 2 * width + lane : 2 * width + lane + 128] = dv[lane, b].astype(BF16)

    staggered(HEADS // 2 * blocks, (to_p, to_s, to_qkv))
    s.dqkv[:, :width] = jnp.transpose(s.dqt[...])
    d_query = col_sums(s.dqkv[:, :width].astype(F32))
    d_value = col_sums(s.dqkv[:, 2 * width :].astype(F32))
    s.du[...] += nt(s.dqkv[...], w_in[...])
    done("du")
    s.ubt[...] = jnp.transpose(ub_ref[...])
    summed = [jnp.concatenate([d_query, d_value], axis=1), d_out, d_gain, d_shift]
    pack_vectors([jnp.sum(x, axis=0, keepdims=True) for x in summed], part, s.vec_keep, s.vec_send)

def attention_weight_gradients(ot_ref, which, end, plan, s, done):
    width, half = s.ubt.shape[0], s.ubt.shape[0] // 2
    at = pl.ds(pl.multiple_of(which * half, half), half)
    left = s.ubt[at, :]
    for number, parts in enumerate(plan):
        key = f"g{number}{end}"
        into = getattr(s, key)
        column, first = 0, None
        for kind, low, high in parts:
            here = slice(column, column + high - low)
            if kind in ("up", "down"):
                column += high - low
                continue
            first = column if first is None else first
            if kind == "in":
                for j in range(low, high, width):
                    k = min(high, j + width)
                    into[:, column + j - low : column + k - low] = nn(left, s.dqkv[:, j:k]).astype(BF16)
            elif kind == "out":
                into[:, here] = nn(ot_ref[at, :], s.da[...]).astype(BF16)
            elif kind == "pos":
                into[:, here] = s.du[at, :].astype(BF16)
            elif kind == "vec":
                into[:16, here] = getattr(s, "vec" + end)[...]
                into[16:32, here] = getattr(s, "feed" + end)[...]
                into[32:, here] = jnp.zeros((half - 32, 128), BF16)
            else:
                into[:, here] = jnp.zeros((half, 128), BF16)
            column += high - low
        done(key, first, column)


def size_of(x):
    return math.prod(x.shape) * x.dtype.itemsize


class Names:
    pass


def call(name, body, inputs, outputs, scratch, flops, after=(), loose=(), aliases={}):
    names_in, names_out, names_scratch = list(inputs), list(outputs), list(scratch)

    def kernel(*refs):
        groups = []
        at = 0
        for names, spare in ((names_in, len(after)), (names_out, 0), (names_scratch, 0)):
            group = Names()
            for key in names:
                setattr(group, key, refs[at])
                at += 1
            at += spare
            groups.append(group)
        moves = Copies(refs[at])
        body(*groups, moves)
        moves.finish()

    moved = sum(size_of(x) for x in list(inputs.values()) + list(outputs.values()))
    held = sum(size_of(x) for x in scratch.values())
    spaces = [pl.ANY if key in loose else pltpu.HBM for key in names_in]
    results = pl.pallas_call(
        kernel,
        name=name,
        out_shape=tuple(pltpu.HBM(x.shape, x.dtype) for x in outputs.values()),
        in_specs=[pl.BlockSpec(memory_space=space) for space in spaces + [pl.ANY] * len(after)],
        out_specs=tuple([pl.BlockSpec(memory_space=pltpu.HBM)] * len(outputs)),
        scratch_shapes=[pltpu.VMEM(x.shape, x.dtype) for x in scratch.values()]
        + [pltpu.SemaphoreType.DMA((len(inputs) + 2 * len(outputs),))],
        compiler_params=pltpu.CompilerParams(vmem_limit_bytes=min(60 * 1024 * 1024, held + ROOM)),
        cost_estimate=pl.CostEstimate(flops=flops, bytes_accessed=moved, transcendentals=0),
        input_output_aliases=aliases,
    )(*[pltpu.with_memory_space_constraint(x, space) for space, x in zip(spaces, inputs.values())], *after)
    return dict(zip(names_out, results))


class Loads:
    def __init__(self, copies, ahead=AHEAD):
        self.copies, self.ahead, self.waiting, self.begun = copies, ahead, [], {}

    def add(self, name, size, *starts):
        self.waiting.append((name, size, starts))

    def begin(self):
        name, size, starts = self.waiting.pop(0)
        self.begun[name] = (size, [start() for start in starts])

    def top_up(self):
        while self.waiting and sum(size for size, unused in self.begun.values()) < self.ahead:
            self.begin()

    def need(self, *names):
        while any(entry[0] in names for entry in self.waiting):
            self.begin()
        for name in names:
            if name in self.begun:
                self.copies.wait(*self.begun.pop(name)[1])
        self.top_up()


def storer(copies, s, o, names, sides=None):
    offsets = {}
    for key, side in (sides or {}).items():
        rows = getattr(s, key).shape[0] // 2
        offsets[key] = rows, ("_a", (1 - side) * rows), ("_b", side * rows)

    def halves(key, low, high):
        if key not in offsets:
            copies.start(lambda: (getattr(s, key).at[:, low:high], getattr(o, key).at[:, low:high]))
            return
        rows = offsets[key][0]
        for letter, row in offsets[key][1:]:

            def ends(letter=letter, row=row):
                at = pl.ds(pl.multiple_of(row, rows), rows)
                return getattr(s, key).at[at, low:high], getattr(o, key + letter).at[:, low:high]

            copies.start(ends)

    def done(*keys):
        if len(keys) == 3 and not isinstance(keys[1], str):
            halves(*keys)
            return
        for key in keys:
            target = names.get(key, key)
            if hasattr(o, target):
                copies.start(functools.partial(lambda key, target: (getattr(s, key), getattr(o, target)), key, target))

    return done


WAYS = {
    "top0": ("xyzw", "yxzw"),
    "top1": ("zxyw", "xzyw"),
    "low0": ("xyzw", "yxzw"),
    "low1": ("zyxw", "yzxw"),
    "low2": ("xzyw", "yzxw"),
}
WAITS = {("low0", 1): ("top0", 1), ("low1", 1): ("top1", 1)}
SPLIT = ("top0", "top1")
MARK = None


def plan_for(layer, width, hidden):
    tail = [("out", 0, width), ("pos", 0, width), ("vec", 0, 128), ("pad", 0, 128)]
    if layer == "top":
        cut = 3 * width - 128
        return [
            [("up", 0, hidden), ("in", 0, cut)],
            [("down", 0, hidden), ("in", cut, 3 * width)] + tail,
        ]
    half = width // 2
    return [
        [("up", 0, hidden), ("in", 0, half)],
        [("down", 0, hidden), ("in", half, width)],
        [("in", width, 3 * width)] + tail,
    ]


def pieces_of(plan, kind):
    found = []
    for number, parts in enumerate(plan):
        at = 0
        for key, low, high in parts:
            if key == kind:
                found.append((number, at, low, high))
            at += high - low
    return found


def columns_of(parts):
    return sum(high - low for unused, low, high in parts)


def shape(dims, dtype):
    return jax.ShapeDtypeStruct(tuple(dims), dtype)


def other_core(value):
    return lax.ppermute(value, "pipe", [(0, 1), (1, 0)])


class Reduction:
    def __init__(self, kept, sent, orders):
        self.steps, self.at = list(zip(*orders)), 0
        halves = [[keep, other_core(send)] for keep, send in zip(kept, sent)]
        self.parts, self.split = halves[0], halves if len(halves) == 2 else None
        self.arrived = [halves[0][1]]

    def mirrored(self, x, shifts):
        size = lax.axis_size("dp")
        pairs = [(2 * i + c, 2 * (i ^ (1 << shifts[c])) + c) for i in range(size) for c in range(2)]
        return lax.ppermute(x, ("dp", "pipe"), pairs)

    def side(self, shifts):
        part = lax.axis_index("pipe")
        return lax.shift_right_logical(lax.axis_index("dp"), jnp.where(part == 0, shifts[0], shifts[1])) & 1

    def joined(self):
        value, other = self.parts
        low = self.side(self.steps[2 * len(self.steps) - 1 - self.at]) == 0
        return jnp.concatenate([jnp.where(low, value, other), jnp.where(low, other, value)], axis=0)

    def complete(self):
        return self.at == 2 * len(self.steps) - 1

    def step(self, waits=()):
        def tie(x):
            for other in waits:
                nothing = jnp.minimum(jnp.abs(other[:1, : x.shape[1]]), 0)
                times = -(-x.shape[1] // nothing.shape[1])
                x = x + jnp.broadcast_to(jnp.concatenate([nothing] * times, axis=1)[:, : x.shape[1]], x.shape)
            return x

        inner = len(self.steps) - 1
        if self.at == 0 and self.split:
            theirs, mine = [half[0] + half[1] for half in self.split]
            self.parts = [mine, self.mirrored(tie(theirs), self.steps[0])]
        elif self.at < inner:
            shifts = self.steps[self.at]
            half = self.parts[0].shape[0] // 2
            bit = self.side(shifts)
            theirs, mine = [
                functools.reduce(
                    jnp.add, [lax.dynamic_slice_in_dim(x, which * half, half, 0) for x in self.parts]
                )
                for which in (1 - bit, bit)
            ]
            self.parts = [mine, self.mirrored(tie(theirs), shifts)]
        elif self.at == inner:
            value = self.parts[0] + self.parts[1]
            self.parts = [value, self.mirrored(tie(value), self.steps[inner])]
        else:
            value = self.parts[0] + self.parts[1] if self.at == inner + 1 else self.joined()
            self.parts = [value, self.mirrored(tie(value), self.steps[2 * inner - self.at])]
        self.arrived.append(self.parts[1])
        self.at += 1

    def result(self):
        return self.joined()


def orders_for(size, ways):
    bits = list(range(size.bit_length() - 1))
    side_bits = (len(bits) - 1) // 3
    x, y, z = bits[:side_bits], bits[side_bits : 2 * side_bits], bits[2 * side_bits :]
    runs = {"x": x, "y": y, "z": z[:1], "w": z[1:]}
    return [sum([runs[letter] for letter in way], []) for way in ways]


def per_device(
    boundary,
    positions,
    w_in,
    qv_bias,
    w_out,
    out_bias,
    gain_one,
    shift_one,
    w_up,
    up_bias,
    w_down,
    down_bias,
    gain_two,
    shift_two,
    segment_ids,
):
    part = lax.axis_index("pipe")
    window_count, length = segment_ids.shape
    layers, half, width = positions.shape
    hidden = w_up.shape[2]
    blocks = length // BLOCK

    small = (qv_bias, out_bias, gain_one, shift_one, up_bias, down_bias, gain_two, shift_two)
    small_names = ("qv_bias", "out_bias", "gain_one", "shift_one", "up_bias", "down_bias", "gain_two", "shift_two")
    sizes = [(key, x.shape[1]) for key, x in zip(small_names, small)]
    vec = jnp.concatenate(small, axis=1)
    windows = boundary.reshape(window_count, length, width)
    got = other_core(lax.dynamic_index_in_dim(windows, 1 - part, 0, keepdims=False))
    vec2, pos2, w_in2, w_out2 = other_core(vec), other_core(positions), other_core(w_in), other_core(w_out)
    late = lax.optimization_barrier((w_up, w_down, got, vec2, pos2, w_in2, w_out2))
    w_up2, w_down2 = other_core(late[0]), other_core(late[1])
    seg = lax.dynamic_index_in_dim(segment_ids, part, 0, keepdims=True)

    square, wide = (length, width), (length, hidden)
    qkv_shape, p_shape = (length, 3 * width), (HEADS // 2 * blocks, min(length, REACH + BLOCK), 2 * BLOCK)
    vec_in = dict(vec=vec, vec2=vec2)
    vec_scratch = dict(vec=shape(vec.shape, BF16), vec2=shape(vec.shape, BF16))
    attention_in = dict(pos=positions, pos2=pos2, w_in=w_in, w_in2=w_in2, w_out=w_out, w_out2=w_out2, seg=seg)
    attention_out = dict(
        ub=shape(square, BF16), qkv=shape(qkv_shape, BF16), p=shape(p_shape, BF16), ot=shape(square, BF16),
        r1=shape(square, F32),
    )
    hidden_out = dict(h=shape(square, F32), hb=shape(square, BF16))
    attention_weights = dict(w_in=shape((width, 3 * width), BF16), w_out=shape((width, width), BF16))
    attention_scratch = dict(
        pos=shape(square, BF16), seg=shape(seg.shape, seg.dtype), u=shape(square, F32), vt=shape(square, BF16),
        bias=shape((length, length), F32), **attention_weights, **attention_out, **hidden_out,
    )
    feed_in = dict(w_up=w_up, w_up2=w_up2, w_down=w_down, w_down2=w_down2)
    feed_weights = dict(w_up=shape((width, hidden), BF16), w_down=shape((hidden, width), BF16))
    feed_out = dict(m=shape(wide, BF16), d=shape(wide, BF16), r2=shape(square, F32))
    plans = {layer: plan_for(layer, width, hidden) for layer in ("top", "low")}
    gradients = {
        layer: {
            f"g{number}{end}": shape((half, columns_of(parts)), BF16)
            for number, parts in enumerate(plan) for end in ("_keep", "_send")
        }
        for layer, plan in plans.items()
    }
    gradients_out = {
        layer: {
            key + letter: shape((x.shape[0] // 2 if letter else x.shape[0], x.shape[1]), BF16)
            for key, x in arrays.items() for letter in (("_a", "_b") if layer + key[1] in SPLIT else ("",))
        }
        for layer, arrays in gradients.items()
    }

    def side_of(name, core):
        low, high = [way[0] for way in orders_for(lax.axis_size("dp"), WAYS[name])]
        return lax.shift_right_logical(lax.axis_index("dp"), jnp.where(core == 0, low, high)) & 1

    def sides_of(layer, place):
        cores = {"_keep": place, "_send": 1 - place}
        return {
            f"g{number}{end}": side_of(f"{layer}{number}", core)
            for number in range(len(plans[layer])) for end, core in cores.items() if f"{layer}{number}" in SPLIT
        }

    vec_grads = {key + end: shape((16, 128), BF16) for key in ("vec", "feed") for end in ("_keep", "_send")}
    back_scratch = dict(
        dh=shape(square, F32), df=shape(square, BF16), dz=shape(wide, BF16), hbt=shape(square, BF16),
        du=shape(square, F32), da=shape(square, BF16), do=shape(square, BF16), kt=shape(square, BF16),
        dqt=shape(square, BF16), dqkv=shape(qkv_shape, BF16), ubt=shape(square, BF16), sums=shape((24, width), F32), **vec_grads,
    )
    flops_attention = 2 * length * width * (4 * width + length)
    flops_feed = 4 * length * width * hidden

    def load_halves(i, s, loads, layer, keys, place, names={}):
        for key in keys:
            target = getattr(s, names.get(key, key))
            loads.add(
                names.get(key, key), size_of(target),
                *halves_in(loads.copies, getattr(i, key), getattr(i, key + "2"), layer, target, place),
            )

    def load(i, s, loads, keys):
        for key in keys:
            target = getattr(s, key)
            ends = functools.partial(lambda source, target: (source, target), getattr(i, key), target)
            loads.add(key, size_of(target), functools.partial(loads.copies.start, ends))

    def window_in(i, copies, place, owner, target):
        make = copies.reserve(lambda: (i.got, target))

        @pl.when(place == owner)
        def _():
            at = pl.ds(pl.multiple_of(place * length, length), length)
            pltpu.make_async_copy(i.rows.at[0, at], target, copies.sems.at[copies.count - 1]).start()

        @pl.when(place != owner)
        def _():
            make().start()

        return make

    def vectors_of(s, need, place):
        need("vec", "vec2")
        return Vectors(s.vec, s.vec2, place, sizes)

    def attention_first(i, o, s, copies):
        place = lax.axis_index("pipe")
        loads = Loads(copies)
        load(i, s, loads, ["vec", "vec2"])
        loads.add("x", size_of(s.x), lambda: window_in(i, copies, place, 0, s.x))
        load_halves(i, s, loads, 0, ["pos"], place)
        load(i, s, loads, ["seg"])
        load_halves(i, s, loads, 0, ["w_in", "w_out"], place)
        need, done = loads.need, storer(copies, s, o, {})
        vectors = vectors_of(s, need, place)
        need("x", "pos")

        @block
        def _():
            u = s.x[...] + s.pos[...].astype(F32)
            s.u[...] = u
            s.ub[...] = u.astype(BF16)
            done("ub")

        attention_forward(s.u, s.ub, s.w_in, s.w_out, vectors, 0, s.seg, s, need, done)
        done("h", "hb")

    first = call(
        "attention_first", attention_first,
        dict(rows=boundary, got=got, **vec_in, **attention_in),
        dict(**attention_out, **hidden_out),
        dict(x=shape(square, F32), **vec_scratch, **attention_scratch),
        10 * flops_attention,
    )

    def middle(i, o, s, copies):
        place = lax.axis_index("pipe")
        loads = Loads(copies)
        load(i, s, loads, ["vec", "vec2", "hb0"])
        load_halves(i, s, loads, 0, ["w_up"], place)
        load(i, s, loads, ["h0"])
        load_halves(i, s, loads, 0, ["w_down"], place)
        load_halves(i, s, loads, 1, ["pos"], place)
        load(i, s, loads, ["seg"])
        load_halves(i, s, loads, 1, ["w_in", "w_out"], place)
        loads.add("g", size_of(s.g), lambda: window_in(i, copies, place, 1, s.g))
        need, done = loads.need, storer(copies, s, o, {"ub": "", "qkv": "", "p": "", "ot": "", "r1": ""})
        vectors = vectors_of(s, need, place)

        def into_last(y):
            u = y.astype(BF16).astype(F32) + s.pos[...].astype(F32)
            s.u[...] = u
            s.ub[...] = u.astype(BF16)

        feed_forward(s.h0, s.hb0, s.w_up, s.w_down, vectors, 0, s, need, done, into_last)
        load_halves(i, s, loads, 1, ["w_up", "w_down"], place)
        attention_forward(s.u, s.ub, s.w_in, s.w_out, vectors, 1, s.seg, s, need, done)
        t = Names()
        t.__dict__.update(s.__dict__)
        t.m, t.d, t.r2 = s.last_m, s.last_d, s.last_r2
        done = storer(copies, s, o, {"m": "", "d": "", "r2": ""}, sides_of("top", place))

        def out_last(y):
            s.y[...] = y
            done("y")

        feed_forward(s.h, s.hb, s.w_up, s.w_down, vectors, 1, t, need, done, out_last)
        feed_backward(s.g, t.r2, s.hb, t.m, t.d, s.w_up, s.w_down, vectors, 1, plans["top"], place, t, need, done)

        def done_low(*keys):
            if keys == ("du",):
                s.gout[...] = s.du[...].astype(BF16)
                copies.start(lambda: (s.gout, o.g))
            else:
                done(*keys)

        attention_backward(
            s.dh, s.r1, s.ub, s.ot, s.qkv, s.p, s.w_in, s.w_out, s.w_up, vectors, 1, plans["top"], place, s, need, done_low
        )

    top = call(
        "middle", middle,
        dict(h0=first["h"], hb0=first["hb"], rows=boundary, got=got, **vec_in, **attention_in, **feed_in),
        dict(**feed_out, y=shape(square, F32), g=shape(square, BF16), **gradients_out["top"]),
        dict(
            h0=shape(square, F32), hb0=shape(square, BF16), g=shape(square, F32), gout=shape(square, BF16),
            y=shape(square, F32), **vec_scratch, **attention_scratch, **feed_weights, **feed_out,
            last_m=feed_out["m"], last_d=feed_out["d"], last_r2=feed_out["r2"], **back_scratch, **gradients["top"],
        ),
        20 * flops_feed,
    )

    def lowest(i, o, s, copies):
        place = lax.axis_index("pipe")
        loads = Loads(copies)
        load(i, s, loads, ["vec", "vec2", "g", "r2"])
        load_halves(i, s, loads, 0, ["w_down"], place)
        load(i, s, loads, ["d", "hb", "m"])
        load_halves(i, s, loads, 0, ["w_up"], place)
        load(i, s, loads, ["r1"])
        load_halves(i, s, loads, 0, ["w_out"], place)
        load(i, s, loads, ["qkv", "p"])
        load_halves(i, s, loads, 0, ["w_in"], place)
        load(i, s, loads, ["ub", "ot"])
        need, done = loads.need, storer(copies, s, o, {}, sides_of("low", place))
        vectors = vectors_of(s, need, place)
        feed_backward(s.g, s.r2, s.hb, s.m, s.d, s.w_up, s.w_down, vectors, 0, plans["low"], place, s, need, done)
        attention_backward(
            s.dh, s.r1, s.ub, s.ot, s.qkv, s.p, s.w_in, s.w_out, s.w_up, vectors, 0, plans["low"], place, s, need, done
        )

    sums = {}

    def begin_sums(layer, kernel):
        for number in range(len(plans[layer])):
            name = f"{layer}{number}"
            letters = ("_a", "_b") if name in SPLIT else ("",)
            kept, sent = [[kernel[f"g{number}{end}{letter}"] for letter in letters] for end in ("_keep", "_send")]
            sums[name] = Reduction(kept, sent, orders_for(lax.axis_size("dp"), WAYS[name]))

    begin_sums("top", top)
    low = call(
        "lowest", lowest,
        dict(
            g=top["g"], **{key: top[key] for key in feed_out}, hb=first["hb"],
            **{key: first[key] for key in attention_out}, **vec_in, **feed_in,
            w_in=w_in, w_in2=w_in2, w_out=w_out, w_out2=w_out2,
        ),
        dict(du=shape(square, F32), **gradients_out["low"]),
        dict(
            g=shape(square, BF16), hb=shape(square, BF16), **vec_scratch, **attention_weights, **attention_out,
            **feed_weights, **feed_out, **back_scratch, **gradients["low"],
        ),
        12 * flops_feed, after=[total.arrived[0] for total in sums.values()],
    )
    begin_sums("low", low)
    while not all(total.complete() for total in sums.values()):
        for name, total in sums.items():
            wait = WAITS.get((name, total.at + 1)) if len(total.steps) == 4 else None
            ready = wait is None or len(sums[wait[0]].arrived) > wait[1]
            if ready and not total.complete():
                total.step([sums[wait[0]].arrived[wait[1]]] if wait else [])

    theirs = jnp.where(part == 0, top["y"], low["du"])
    if MARK and len(sums[MARK[0]].arrived) > MARK[1]:
        theirs = theirs + jnp.minimum(jnp.abs(sums[MARK[0]].arrived[MARK[1]][:1, :width].astype(F32)), 0)
    theirs = other_core(theirs)
    boundary_out = jnp.stack(
        [jnp.where(part == 0, low["du"], theirs), jnp.where(part == 0, theirs, top["y"])]
    ).reshape(1, window_count * length, width)
    units, more = width // 256, hidden // 256
    big = dict(
        pos=shape((layers, half, width), F32), w_in=shape((layers, half, 3 * width), F32),
        out=shape((layers, half, width), F32), up=shape((layers, half, hidden), F32),
        down=shape((layers, hidden // 2, width), F32),
    )
    big["in"] = big.pop("w_in")
    runs = dict(
        qv_bias=(0, 2 * units), out_bias=(2 * units, units), gain_one=(3 * units, units), shift_one=(4 * units, units),
        up_bias=(16, more), down_bias=(16 + more, units), gain_two=(16 + more + units, units),
        shift_two=(16 + more + 2 * units, units),
    )
    small_out = {key: shape((layers, 128 * count), F32) for key, (unused, count) in runs.items()}

    def assemble(name, layer, parts, extra, so_far):
        kinds = [kind for kind, unused, unused_too in parts if kind in big]
        rows = half // 2

        def body(i, o, s, copies):
            place = lax.axis_index("pipe")
            loads = Loads(copies)
            side = side_of(name, place)
            for key, row in (("value", side * rows), ("other", (1 - side) * rows)):
                at = pl.ds(pl.multiple_of(row, rows), rows)
                ends = functools.partial(lambda a, b, at: (a, b.at[at]), getattr(i, key), s.whole, at)
                loads.add(key, size_of(s.whole) // 2, functools.partial(copies.start, ends))
            for key in extra:
                column = pieces_of(plans["top"], "vec")[0][1]
                ends = functools.partial(
                    lambda a, b, column: (a.at[:32, column : column + 128], b), getattr(i, key), getattr(s, key), column
                )
                loads.add(key, 8192, functools.partial(copies.start, ends))
            loads.need("value", "other", *extra)

            def store(key, low, high):
                if key in ("in", "up"):
                    copies.start(lambda: (getattr(s, key), getattr(o, key).at[layer, :, low:high]))
                else:
                    copies.start(lambda: (getattr(s, key), getattr(o, key).at[layer]))

            @block
            def _():
                column = 0
                for kind, low, high in parts:
                    here = slice(column, column + high - low)
                    if kind == "down":
                        for j in range(hidden // width):
                            one = s.whole[:, column + j * width : column + (j + 1) * width]
                            s.down[j * half : (j + 1) * half, :] = one.astype(F32)
                    elif kind in big:
                        getattr(s, kind)[...] = s.whole[:, here].astype(F32)
                    if kind in big:
                        store(kind, low, high)
                    if kind == "vec" and extra:
                        side = side_of("top1", place) == 0
                        upper = jnp.where(side, s.last_value[...].astype(F32), s.last_other[...].astype(F32))
                        lower = s.whole[:32, here].astype(F32)
                        for key, (at, count) in runs.items():
                            lines = [
                                jnp.concatenate([x[at + j : at + j + 1] for j in range(count)], axis=1)
                                for x in (lower, upper)
                            ]
                            getattr(s, key)[...] = jnp.concatenate(lines, axis=0)
                            copies.start(functools.partial(lambda key: (getattr(s, key), getattr(o, key)), key))
                    column += high - low

        values = dict(zip(("value", "other"), sums[name].parts))
        before = {key: so_far[key] for key in kinds if key in so_far}
        outputs = {**{key: big[key] for key in kinds}, **(small_out if extra else {})}
        scratch = {
            kind: shape(big[kind].shape[1:] if kind == "down" else (half, high - low), F32)
            for kind, low, high in parts if kind in big
        }
        return call(
            "assemble_" + name, body, {**values, **extra, **before}, outputs,
            dict(
                whole=shape((half, columns_of(parts)), BF16), **{key: shape((32, 128), BF16) for key in extra},
                **scratch, **(small_out if extra else {}),
            ),
            flops_feed, loose=list(values) + list(extra),
            aliases={len(values) + len(extra) + n: list(outputs).index(key) for n, key in enumerate(before)},
        )

    result = {}
    for number, parts in enumerate(plans["top"]):
        result.update(assemble(f"top{number}", 1, parts, {}, result))
    last = dict(zip(("last_value", "last_other"), sums["top1"].parts))
    for number, parts in enumerate(plans["low"]):
        extra = last if any(kind == "vec" for kind, unused, unused_too in parts) else {}
        result.update(assemble(f"low{number}", 0, parts, extra, result))
    order = ("pos", "in", "qv_bias", "out", "out_bias", "gain_one", "shift_one", "up", "up_bias", "down", "down_bias",
             "gain_two", "shift_two")
    return (boundary_out,) + tuple(result[key] for key in order)


def solution(mesh):
    rows, vector = P(None, "pipe", None), P(None, "pipe")
    both = P("pipe", "dp", None)
    params = (rows, rows, vector, rows, vector, vector, vector, rows, vector, rows, vector, vector, vector)
    return jax.shard_map(
        per_device,
        mesh=mesh,
        in_specs=(both,) + params + (P("dp", None),),
        out_specs=(both,) + params,
        check_vma=False,
    )
```

```python
import functools
import math

import jax
import jax.numpy as jnp
from jax import lax
from jax.experimental import pallas as pl
from jax.experimental.pallas import tpu as pltpu
from jax.sharding import PartitionSpec as P

HEADS = 8
EPS = 1e-05
MASKED = -1e30
REACH = 256
BLOCK = 128
F32, BF16 = jnp.float32, jnp.bfloat16
GELU_C = math.sqrt(2.0 / math.pi)
ROOM = 8 * 1024 * 1024
AHEAD = 24 * 1024 * 1024


def nn(a, b):
    return lax.dot_general(a, b, (((1,), (0,)), ((), ())), preferred_element_type=F32)


def nt(a, b):
    return lax.dot_general(a, b, (((1,), (1,)), ((), ())), preferred_element_type=F32)


def col_sums(x):
    return jnp.sum(x.reshape(x.shape[0] // 8, 8, x.shape[1]), axis=0)


def block(body):
    pl.when(lax.axis_index("dp") < 1 << 20)(body)


class Copies:
    def __init__(self, sems):
        self.sems, self.count, self.open = sems, 0, []

    def reserve(self, ends):
        number = self.count
        self.count += 1

        def make():
            source, target = ends()
            return pltpu.make_async_copy(source, target, self.sems.at[number])

        self.open.append(make)
        return make

    def start(self, ends):
        make = self.reserve(ends)
        make().start()
        return make

    def wait(self, *made):
        for make in made:
            make().wait()
            self.open = [other for other in self.open if other is not make]

    def finish(self):
        self.wait(*list(self.open))


class Vectors:
    def __init__(self, own, other, part, sizes):
        self.own, self.other, self.part, self.sizes = own, other, part, sizes

    def get(self, layer, name):
        at = 0
        for key, size in self.sizes:
            if key == name:
                break
            at += size
        own = self.own[:, at : at + size].astype(F32)[layer : layer + 1]
        other = self.other[:, at : at + size].astype(F32)[layer : layer + 1]
        low = jnp.where(self.part == 0, own, other)
        high = jnp.where(self.part == 0, other, own)
        return jnp.concatenate([low, high], axis=1)


def halves_in(copies, own, other, layer, target, part):
    rows = own.shape[1]
    mine = pl.ds(pl.multiple_of(part * rows, rows), rows)
    theirs = pl.ds(pl.multiple_of((1 - part) * rows, rows), rows)
    return (
        lambda: copies.start(lambda: (own.at[layer], target.at[mine])),
        lambda: copies.start(lambda: (other.at[layer], target.at[theirs])),
    )


def pack_vectors(vectors, part, keep_ref, send_ref):
    keep, send = [], []
    for vector in vectors:
        half = vector.shape[1] // 2
        low, high = vector[:, :half], vector[:, half:]
        mine = jnp.where(part == 0, low, high)
        theirs = jnp.where(part == 0, high, low)
        for j in range(half // 128):
            keep.append(mine[:, j * 128 : (j + 1) * 128])
            send.append(theirs[:, j * 128 : (j + 1) * 128])
    spare = jnp.zeros((keep_ref.shape[0] - len(keep), 128), F32)
    keep_ref[...] = jnp.concatenate(keep + [spare], axis=0).astype(keep_ref.dtype)
    send_ref[...] = jnp.concatenate(send + [spare], axis=0).astype(send_ref.dtype)


def norm_stats(r):
    centred = r - jnp.mean(r, axis=-1, keepdims=True)
    scale = lax.rsqrt(jnp.mean(centred * centred, axis=-1, keepdims=True) + EPS)
    return centred * scale, scale


def norm_backward(r, g, gain):
    xhat, scale = norm_stats(r)
    gy = g * gain
    mean_one = jnp.mean(gy, axis=-1, keepdims=True)
    mean_two = jnp.mean(gy * xhat, axis=-1, keepdims=True)
    return scale * (gy - mean_one - xhat * mean_two), col_sums(g * xhat), col_sums(g)


def key_range(i):
    return max(0, i * BLOCK + 1 - REACH) // BLOCK * BLOCK, (i + 1) * BLOCK


def head_masks(scale):
    lane = lax.broadcasted_iota(jnp.int32, (1, 128), 1)
    first = jnp.where(lane < 64, scale, 0.0).astype(BF16)
    second = jnp.where(lane < 64, 0.0, scale).astype(BF16)
    return first, second


def stacked(x, masks):
    return jnp.concatenate([x * masks[0], x * masks[1]], axis=0)


def write_bias(seg_ref, bias_ref):
    length = seg_ref.shape[1]
    seg = seg_ref[...].astype(F32)
    columns = jnp.broadcast_to(seg, (128, length))
    for j in range(length // 128):
        rows = pl.ds(j * 128, 128)
        own = jnp.broadcast_to(jnp.transpose(columns[:, j * 128 : (j + 1) * 128])[:, :1], (128, length))
        key = lax.broadcasted_iota(jnp.int32, (128, length), 0) + j * 128
        query = lax.broadcasted_iota(jnp.int32, (128, length), 1)
        bias_ref[rows, :] = jnp.where((own == seg) & (key <= query), 0.0, MASKED)


def staggered(count, stages):
    held = {}
    for tick in range(count + len(stages) - 1):
        for number, stage in enumerate(stages):
            t = tick - number
            if 0 <= t < count:
                held[t] = stage(t, held.pop(t, None))


def p_slot(t, blocks):
    return t % blocks * (HEADS // 2) + t // blocks


def p_parts(blocks):
    found = []
    for i in range(blocks):
        low, high = key_range(i)
        found.append((i * (HEADS // 2), (i + 1) * (HEADS // 2), high - low))
    full = [part for part in found if part[2] == found[-1][2]]
    return [part for part in found if part not in full] + [(full[0][0], full[-1][1], full[0][2])]


def attention_core(qkv_ref, vt_ref, bias_ref, p_ref, ot_ref, width):
    masks = head_masks(1.0 / math.sqrt(width // HEADS))
    blocks = qkv_ref.shape[0] // BLOCK

    def place(t):
        pair, i = divmod(t, blocks)
        low, high = key_range(i)
        return pair * 128, slice(i * BLOCK, (i + 1) * BLOCK), low, high

    def score(t, unused):
        lane, queries, low, high = place(t)
        q = stacked(qkv_ref[queries, lane : lane + 128], masks)
        return nt(qkv_ref[low:high, width + lane : width + lane + 128], q)

    def soften(t, s):
        lane, queries, low, high = place(t)
        bias = bias_ref[low:high, queries]
        s = s + jnp.concatenate([bias, bias], axis=1)
        e = jnp.exp(s - jnp.max(s, axis=0, keepdims=True))
        p = (e * (1.0 / jnp.sum(e, axis=0, keepdims=True))).astype(BF16)
        p_ref[p_slot(t, blocks), : high - low, :] = p
        return p

    def attend(t, p):
        lane, queries, low, high = place(t)
        o = nn(vt_ref[lane : lane + 128, low:high], p)
        ot_ref[lane : lane + 64, queries] = o[:64, :BLOCK].astype(BF16)
        ot_ref[lane + 64 : lane + 128, queries] = o[64:, BLOCK:].astype(BF16)

    staggered(HEADS // 2 * blocks, (score, soften, attend))


def attention_forward(u_ref, ub_ref, w_in, w_out, vectors, layer, seg_ref, s, need, done):
    length, width = u_ref.shape
    need("seg", "w_in", "w_out")

    @block
    def _():
        write_bias(seg_ref, s.bias)
        qv = vectors.get(layer, "qv_bias")
        for j in range(3):
            bias = (qv[:, :width], 0.0, qv[:, width:])[j]
            cols = slice(j * width, (j + 1) * width)
            s.qkv[:, cols] = (nn(ub_ref[...], w_in[:, cols]) + bias).astype(BF16)
        done("qkv")
        s.vt[...] = jnp.transpose(s.qkv[:, 2 * width :])
        attention_core(s.qkv, s.vt, s.bias, s.p, s.ot, width)
        done("p", "ot")
        out_bias = vectors.get(layer, "out_bias")
        gain, shift = vectors.get(layer, "gain_one"), vectors.get(layer, "shift_one")
        r = u_ref[...] + (nn(jnp.transpose(s.ot[...]), w_out[...]) + out_bias)
        s.r1[...] = r
        done("r1")
        if hasattr(s, "h"):
            h = norm_stats(r)[0] * gain + shift
            s.h[...] = h
            s.hb[...] = h.astype(BF16)


def feed_forward(h_ref, hb_ref, w_up, w_down, vectors, layer, s, need, done, finish):
    width, hidden = w_up.shape
    tile = 256
    need("w_up")

    @block
    def _():
        up_bias = vectors.get(layer, "up_bias")
        for j in range(hidden // tile):
            cols = slice(j * tile, (j + 1) * tile)
            v = nn(hb_ref[...], w_up[:, cols]) + up_bias[:, cols]
            v2 = v * v
            half = 0.5 + 0.5 * jnp.tanh(v * (GELU_C + (GELU_C * 0.044715) * v2))
            m = v * half
            s.m[:, cols] = m.astype(BF16)
            s.d[:, cols] = (half + m * (1.0 - half) * (2 * GELU_C + (6 * GELU_C * 0.044715) * v2)).astype(BF16)
        done("m", "d")

    need("w_down", "pos")

    @block
    def _():
        down_bias = vectors.get(layer, "down_bias")
        gain, shift = vectors.get(layer, "gain_two"), vectors.get(layer, "shift_two")
        r = h_ref[...] + (nn(s.m[...], w_down[...]) + down_bias)
        s.r2[...] = r
        done("r2")
        finish(norm_stats(r)[0] * gain + shift)


def feed_backward(g_ref, r2_ref, hb_ref, m_ref, d_ref, w_up, w_down, vectors, layer, plan, part, s, need, done):
    length, width = r2_ref.shape
    hidden = w_up.shape[1]
    tile = 256
    need("g", "r2")

    @block
    def _():
        gain = vectors.get(layer, "gain_two")
        dr, d_gain, d_shift = norm_backward(r2_ref[...], g_ref[...].astype(F32), gain)
        df = dr.astype(BF16)
        s.dh[...] = dr
        s.df[...] = df
        s.sums[0:8, :] = d_gain
        s.sums[8:16, :] = d_shift
        s.sums[16:24, :] = col_sums(df.astype(F32))

    need("w_down", "d")

    @block
    def _():
        d_up = []
        for j in range(hidden // tile):
            cols = slice(j * tile, (j + 1) * tile)
            dz = (nt(s.df[...], w_down[cols, :]) * d_ref[:, cols].astype(F32)).astype(BF16)
            s.dz[:, cols] = dz
            d_up.append(col_sums(dz.astype(F32)))
        parts = [jnp.concatenate(d_up, axis=1), s.sums[16:24, :], s.sums[0:8, :], s.sums[8:16, :]]
        pack_vectors([jnp.sum(x, axis=0, keepdims=True) for x in parts], part, s.feed_keep, s.feed_send)

    need("r1", "m")

    @block
    def _():
        if hb_ref is None:
            h = norm_stats(s.r1[...])[0] * vectors.get(layer, "gain_one") + vectors.get(layer, "shift_one")
            s.hbt[...] = jnp.transpose(h.astype(BF16))
        else:
            s.hbt[...] = jnp.transpose(hb_ref[...])
        half, rows = width // 2, hidden // 2
        for which, end in ((1 - part, "_send"), (part, "_keep")):
            left = s.hbt[pl.ds(pl.multiple_of(which * half, half), half), :]
            for number, column, low, high in pieces_of(plan, "up"):
                key = f"g{number}{end}"
                into = getattr(s, key)
                for at in range(low, high, 512):
                    into[:, column + at - low : column + at - low + 512] = nn(left, s.dz[:, at : at + 512]).astype(BF16)
                done(key, column, column + high - low)
            for number, column, low, high in pieces_of(plan, "down"):
                key = f"g{number}{end}"
                into = getattr(s, key)
                for at in range(low, high, width):
                    row = pl.multiple_of(which * rows + at // width * half, half)
                    left = jnp.transpose(m_ref[:, pl.ds(row, half)])
                    into[:, column + at - low : column + at - low + width] = nn(left, s.df[...]).astype(BF16)
                done(key, column, column + high - low)

    need("w_up")


def attention_backward(
    dh_ref, r1_ref, ub_ref, ot_ref, qkv_ref, p_ref, w_in, w_out, w_up, vectors, layer, plan, part, s, need, done
):
    need("r1", "w_out", "qkv", "p", "w_in", "ub", "ot")
    block(lambda: attention_gradients(
        dh_ref, r1_ref, ub_ref, ot_ref, qkv_ref, p_ref, w_in, w_out, w_up, vectors, layer, part, s, done
    ))
    block(lambda: attention_weight_gradients(ot_ref, 1 - part, "_send", plan, s, done))
    block(lambda: attention_weight_gradients(ot_ref, part, "_keep", plan, s, done))


def attention_gradients(
    dh_ref, r1_ref, ub_ref, ot_ref, qkv_ref, p_ref, w_in, w_out, w_up, vectors, layer, part, s, done
):
    length, width = r1_ref.shape
    s.dh[...] += nt(s.dz[...], w_up[...])
    gain = vectors.get(layer, "gain_one")
    dr, d_gain, d_shift = norm_backward(r1_ref[...], dh_ref[...], gain)
    da = dr.astype(BF16)
    s.du[...] = dr
    s.da[...] = da
    d_out = col_sums(da.astype(F32))
    s.do[...] = nt(s.da[...], w_out[...]).astype(BF16)
    s.kt[...] = jnp.transpose(qkv_ref[:, width : 2 * width])
    scale = 1.0 / math.sqrt(width // HEADS)
    q_masks, o_masks = head_masks(scale), head_masks(1.0)
    blocks = length // BLOCK
    dk, dv = {}, {}

    def place(t):
        pair, i = divmod(t, blocks)
        low, high = key_range(i)
        return pair * 128, slice(i * BLOCK, (i + 1) * BLOCK), low, high

    def to_p(t, unused):
        lane, queries, low, high = place(t)
        do = stacked(s.do[queries, lane : lane + 128], o_masks)
        return nt(qkv_ref[low:high, 2 * width + lane : 2 * width + lane + 128], do), do

    def to_s(t, held):
        lane, queries, low, high = place(t)
        dp, do = held
        pb = p_ref[p_slot(t, blocks), : high - low, :]
        p = pb.astype(F32)
        weighted = dp * p
        ds = (weighted - p * jnp.sum(weighted, axis=0, keepdims=True)).astype(BF16)
        return ds, pb, do

    def to_qkv(t, held):
        lane, queries, low, high = place(t)
        ds, pb, do = held
        q = stacked(qkv_ref[queries, lane : lane + 128], q_masks)
        more_v, more_k = nn(pb, do), nn(ds, q)
        for b in range(low // BLOCK, high // BLOCK):
            piece = slice(b * BLOCK - low, (b + 1) * BLOCK - low)
            dk[lane, b] = dk[lane, b] + more_k[piece] if (lane, b) in dk else more_k[piece]
            dv[lane, b] = dv[lane, b] + more_v[piece] if (lane, b) in dv else more_v[piece]
        dq = nn(s.kt[lane : lane + 128, low:high], ds) * scale
        s.dqt[lane : lane + 64, queries] = dq[:64, :BLOCK].astype(BF16)
        s.dqt[lane + 64 : lane + 128, queries] = dq[64:, BLOCK:].astype(BF16)
        if high == length:
            for b in range(blocks):
                keys = slice(b * BLOCK, (b + 1) * BLOCK)
                s.dqkv[keys, width + lane : width + lane + 128] = dk[lane, b].astype(BF16)
                s.dqkv[keys, 2 * width + lane : 2 * width + lane + 128] = dv[lane, b].astype(BF16)

    staggered(HEADS // 2 * blocks, (to_p, to_s, to_qkv))
    s.dqkv[:, :width] = jnp.transpose(s.dqt[...])
    d_query = col_sums(s.dqkv[:, :width].astype(F32))
    d_value = col_sums(s.dqkv[:, 2 * width :].astype(F32))
    s.du[...] += nt(s.dqkv[...], w_in[...])
    done("du")
    s.ubt[...] = jnp.transpose(ub_ref[...])
    summed = [jnp.concatenate([d_query, d_value], axis=1), d_out, d_gain, d_shift]
    pack_vectors([jnp.sum(x, axis=0, keepdims=True) for x in summed], part, s.vec_keep, s.vec_send)

def attention_weight_gradients(ot_ref, which, end, plan, s, done):
    width, half = s.ubt.shape[0], s.ubt.shape[0] // 2
    at = pl.ds(pl.multiple_of(which * half, half), half)
    left = s.ubt[at, :]
    for number, parts in enumerate(plan):
        key = f"g{number}{end}"
        into = getattr(s, key)
        column, first = 0, None
        for kind, low, high in parts:
            here = slice(column, column + high - low)
            if kind in ("up", "down"):
                column += high - low
                continue
            first = column if first is None else first
            if kind == "in":
                for j in range(low, high, width):
                    k = min(high, j + width)
                    into[:, column + j - low : column + k - low] = nn(left, s.dqkv[:, j:k]).astype(BF16)
            elif kind == "out":
                into[:, here] = nn(ot_ref[at, :], s.da[...]).astype(BF16)
            elif kind == "pos":
                into[:, here] = s.du[at, :].astype(BF16)
            elif kind == "vec":
                into[:16, here] = getattr(s, "vec" + end)[...]
                into[16:32, here] = getattr(s, "feed" + end)[...]
                into[32:, here] = jnp.zeros((half - 32, 128), BF16)
            else:
                into[:, here] = jnp.zeros((half, 128), BF16)
            column += high - low
        done(key, first, column)


def size_of(x):
    return math.prod(x.shape) * x.dtype.itemsize


class Names:
    pass


def call(name, body, inputs, outputs, scratch, flops, after=(), loose=(), aliases={}):
    names_in, names_out, names_scratch = list(inputs), list(outputs), list(scratch)

    def kernel(*refs):
        groups = []
        at = 0
        for names, spare in ((names_in, len(after)), (names_out, 0), (names_scratch, 0)):
            group = Names()
            for key in names:
                setattr(group, key, refs[at])
                at += 1
            at += spare
            groups.append(group)
        moves = Copies(refs[at])
        body(*groups, moves)
        moves.finish()

    moved = sum(size_of(x) for x in list(inputs.values()) + list(outputs.values()))
    held = sum(size_of(x) for x in scratch.values())
    spaces = [pl.ANY if key in loose else pltpu.HBM for key in names_in]
    results = pl.pallas_call(
        kernel,
        name=name,
        out_shape=tuple(pltpu.HBM(x.shape, x.dtype) for x in outputs.values()),
        in_specs=[pl.BlockSpec(memory_space=space) for space in spaces + [pl.ANY] * len(after)],
        out_specs=tuple([pl.BlockSpec(memory_space=pltpu.HBM)] * len(outputs)),
        scratch_shapes=[pltpu.VMEM(x.shape, x.dtype) for x in scratch.values()]
        + [pltpu.SemaphoreType.DMA((len(inputs) + 2 * len(outputs),))],
        compiler_params=pltpu.CompilerParams(vmem_limit_bytes=min(60 * 1024 * 1024, held + ROOM)),
        cost_estimate=pl.CostEstimate(flops=flops, bytes_accessed=moved, transcendentals=0),
        input_output_aliases=aliases,
    )(*[pltpu.with_memory_space_constraint(x, space) for space, x in zip(spaces, inputs.values())], *after)
    return dict(zip(names_out, results))


class Loads:
    def __init__(self, copies, ahead=AHEAD):
        self.copies, self.ahead, self.waiting, self.begun = copies, ahead, [], {}

    def add(self, name, size, *starts):
        self.waiting.append((name, size, starts))

    def begin(self):
        name, size, starts = self.waiting.pop(0)
        self.begun[name] = (size, [start() for start in starts])

    def top_up(self):
        while self.waiting and sum(size for size, unused in self.begun.values()) < self.ahead:
            self.begin()

    def need(self, *names):
        while any(entry[0] in names for entry in self.waiting):
            self.begin()
        for name in names:
            if name in self.begun:
                self.copies.wait(*self.begun.pop(name)[1])
        self.top_up()


def storer(copies, s, o, names, sides=None):
    offsets = {}
    for key, side in (sides or {}).items():
        rows = getattr(s, key).shape[0] // 2
        offsets[key] = rows, ("_a", (1 - side) * rows), ("_b", side * rows)

    def halves(key, low, high):
        if key not in offsets:
            copies.start(lambda: (getattr(s, key).at[:, low:high], getattr(o, key).at[:, low:high]))
            return
        rows = offsets[key][0]
        for letter, row in offsets[key][1:]:

            def ends(letter=letter, row=row):
                at = pl.ds(pl.multiple_of(row, rows), rows)
                return getattr(s, key).at[at, low:high], getattr(o, key + letter).at[:, low:high]

            copies.start(ends)

    def done(*keys):
        if len(keys) == 3 and not isinstance(keys[1], str):
            halves(*keys)
            return
        for key in keys:
            target = names.get(key, key)
            if target == "p" and hasattr(o, "p"):
                for first, end, count in p_parts(s.p.shape[0] // (HEADS // 2)):
                    copies.start(functools.partial(
                        lambda *at: (s.p.at[at[0] : at[1], : at[2]], o.p.at[at[0] : at[1], : at[2]]), first, end, count
                    ))
            elif hasattr(o, target):
                copies.start(functools.partial(lambda key, target: (getattr(s, key), getattr(o, target)), key, target))

    return done


WAYS = {
    "top0": ("xyzw", "yzxw"),
    "top1": ("yxzw", "xzyw"),
    "low0": ("xyzw", "yzxw"),
    "low1": ("yxzw", "xzyw"),
    "low2": ("xzyw", "yzxw"),
}
WAITS = {("low0", 1): ("top0", 1), ("low1", 1): ("top1", 1)}
SPLIT = ("top0", "top1")
MARK = None


def plan_for(layer, width, hidden):
    tail = [("out", 0, width), ("pos", 0, width), ("vec", 0, 128), ("pad", 0, 128)]
    if layer == "top":
        cut = 3 * width - 128
        return [
            [("up", 0, hidden), ("in", 0, cut)],
            [("down", 0, hidden), ("in", cut, 3 * width)] + tail,
        ]
    half = width // 2
    return [
        [("up", 0, hidden), ("in", 0, half)],
        [("down", 0, hidden), ("in", half, width)],
        [("in", width, 3 * width)] + tail,
    ]


def pieces_of(plan, kind):
    found = []
    for number, parts in enumerate(plan):
        at = 0
        for key, low, high in parts:
            if key == kind:
                found.append((number, at, low, high))
            at += high - low
    return found


def columns_of(parts):
    return sum(high - low for unused, low, high in parts)


def shape(dims, dtype):
    return jax.ShapeDtypeStruct(tuple(dims), dtype)


def other_core(value):
    return lax.ppermute(value, "pipe", [(0, 1), (1, 0)])


class Reduction:
    def __init__(self, kept, sent, orders):
        self.steps, self.at = list(zip(*orders)), 0
        halves = [[keep, other_core(send)] for keep, send in zip(kept, sent)]
        self.parts, self.split = halves[0], halves if len(halves) == 2 else None
        self.arrived = [halves[0][1]]

    def mirrored(self, x, shifts):
        size = lax.axis_size("dp")
        pairs = [(2 * i + c, 2 * (i ^ (1 << shifts[c])) + c) for i in range(size) for c in range(2)]
        return lax.ppermute(x, ("dp", "pipe"), pairs)

    def side(self, shifts):
        part = lax.axis_index("pipe")
        return lax.shift_right_logical(lax.axis_index("dp"), jnp.where(part == 0, shifts[0], shifts[1])) & 1

    def joined(self):
        value, other = self.parts
        low = self.side(self.steps[2 * len(self.steps) - 1 - self.at]) == 0
        return jnp.concatenate([jnp.where(low, value, other), jnp.where(low, other, value)], axis=0)

    def complete(self):
        return self.at == 2 * len(self.steps) - 1

    def step(self, waits=()):
        def tie(x):
            for other in waits:
                nothing = jnp.minimum(jnp.abs(other[:1, : x.shape[1]]), 0)
                times = -(-x.shape[1] // nothing.shape[1])
                x = x + jnp.broadcast_to(jnp.concatenate([nothing] * times, axis=1)[:, : x.shape[1]], x.shape)
            return x

        inner = len(self.steps) - 1
        if self.at == 0 and self.split:
            theirs, mine = [half[0] + half[1] for half in self.split]
            self.parts = [mine, self.mirrored(tie(theirs), self.steps[0])]
        elif self.at < inner:
            shifts = self.steps[self.at]
            half = self.parts[0].shape[0] // 2
            bit = self.side(shifts)
            theirs, mine = [
                functools.reduce(
                    jnp.add, [lax.dynamic_slice_in_dim(x, which * half, half, 0) for x in self.parts]
                )
                for which in (1 - bit, bit)
            ]
            self.parts = [mine, self.mirrored(tie(theirs), shifts)]
        elif self.at == inner:
            value = self.parts[0] + self.parts[1]
            self.parts = [value, self.mirrored(tie(value), self.steps[inner])]
        else:
            value = self.parts[0] + self.parts[1] if self.at == inner + 1 else self.joined()
            self.parts = [value, self.mirrored(tie(value), self.steps[2 * inner - self.at])]
        self.arrived.append(self.parts[1])
        self.at += 1

    def result(self):
        return self.joined()


def orders_for(size, ways):
    bits = list(range(size.bit_length() - 1))
    side_bits = (len(bits) - 1) // 3
    x, y, z = bits[:side_bits], bits[side_bits : 2 * side_bits], bits[2 * side_bits :]
    runs = {"x": x, "y": y, "z": z[:1], "w": z[1:]}
    return [sum([runs[letter] for letter in way], []) for way in ways]


def per_device(
    boundary,
    positions,
    w_in,
    qv_bias,
    w_out,
    out_bias,
    gain_one,
    shift_one,
    w_up,
    up_bias,
    w_down,
    down_bias,
    gain_two,
    shift_two,
    segment_ids,
):
    part = lax.axis_index("pipe")
    window_count, length = segment_ids.shape
    layers, half, width = positions.shape
    hidden = w_up.shape[2]
    blocks = length // BLOCK

    small = (qv_bias, out_bias, gain_one, shift_one, up_bias, down_bias, gain_two, shift_two)
    small_names = ("qv_bias", "out_bias", "gain_one", "shift_one", "up_bias", "down_bias", "gain_two", "shift_two")
    sizes = [(key, x.shape[1]) for key, x in zip(small_names, small)]
    vec = jnp.concatenate(small, axis=1)
    windows = boundary.reshape(window_count, length, width)
    got = other_core(lax.dynamic_index_in_dim(windows, 1 - part, 0, keepdims=False))
    vec2, pos2, w_in2, w_out2 = other_core(vec), other_core(positions), other_core(w_in), other_core(w_out)
    late = lax.optimization_barrier((w_up, w_down, got, vec2, pos2, w_in2, w_out2))
    w_up2, w_down2 = other_core(late[0]), other_core(late[1])
    seg = lax.dynamic_index_in_dim(segment_ids, part, 0, keepdims=True)

    square, wide = (length, width), (length, hidden)
    qkv_shape, p_shape = (length, 3 * width), (HEADS // 2 * blocks, min(length, REACH + BLOCK), 2 * BLOCK)
    vec_in = dict(vec=vec, vec2=vec2)
    vec_scratch = dict(vec=shape(vec.shape, BF16), vec2=shape(vec.shape, BF16))
    attention_in = dict(pos=positions, pos2=pos2, w_in=w_in, w_in2=w_in2, w_out=w_out, w_out2=w_out2, seg=seg)
    attention_out = dict(
        ub=shape(square, BF16), qkv=shape(qkv_shape, BF16), p=shape(p_shape, BF16), ot=shape(square, BF16),
        r1=shape(square, F32),
    )
    hidden_out = dict(h=shape(square, F32), hb=shape(square, BF16))
    attention_weights = dict(w_in=shape((width, 3 * width), BF16), w_out=shape((width, width), BF16))
    attention_scratch = dict(
        pos=shape(square, BF16), seg=shape(seg.shape, seg.dtype), u=shape(square, F32), vt=shape(square, BF16),
        bias=shape((length, length), F32), **attention_weights, **attention_out,
    )
    feed_in = dict(w_up=w_up, w_up2=w_up2, w_down=w_down, w_down2=w_down2)
    feed_weights = dict(w_up=shape((width, hidden), BF16), w_down=shape((hidden, width), BF16))
    feed_out = dict(m=shape(wide, BF16), d=shape(wide, BF16), r2=shape(square, F32))
    plans = {layer: plan_for(layer, width, hidden) for layer in ("top", "low")}
    gradients = {
        layer: {
            f"g{number}{end}": shape((half, columns_of(parts)), BF16)
            for number, parts in enumerate(plan) for end in ("_keep", "_send")
        }
        for layer, plan in plans.items()
    }
    gradients_out = {
        layer: {
            key + letter: shape((x.shape[0] // 2 if letter else x.shape[0], x.shape[1]), BF16)
            for key, x in arrays.items() for letter in (("_a", "_b") if layer + key[1] in SPLIT else ("",))
        }
        for layer, arrays in gradients.items()
    }

    def side_of(name, core):
        low, high = [way[0] for way in orders_for(lax.axis_size("dp"), WAYS[name])]
        return lax.shift_right_logical(lax.axis_index("dp"), jnp.where(core == 0, low, high)) & 1

    def sides_of(layer, place):
        cores = {"_keep": place, "_send": 1 - place}
        return {
            f"g{number}{end}": side_of(f"{layer}{number}", core)
            for number in range(len(plans[layer])) for end, core in cores.items() if f"{layer}{number}" in SPLIT
        }

    vec_grads = {key + end: shape((16, 128), BF16) for key in ("vec", "feed") for end in ("_keep", "_send")}
    back_scratch = dict(
        dh=shape(square, F32), df=shape(square, BF16), dz=shape(wide, BF16), hbt=shape(square, BF16),
        du=shape(square, F32), da=shape(square, BF16), do=shape(square, BF16), kt=shape(square, BF16),
        dqt=shape(square, BF16), dqkv=shape(qkv_shape, BF16), ubt=shape(square, BF16), sums=shape((24, width), F32), **vec_grads,
    )
    flops_attention = 2 * length * width * (4 * width + length)
    flops_feed = 4 * length * width * hidden

    def load_halves(i, s, loads, layer, keys, place, names={}):
        for key in keys:
            target = getattr(s, names.get(key, key))
            loads.add(
                names.get(key, key), size_of(target),
                *halves_in(loads.copies, getattr(i, key), getattr(i, key + "2"), layer, target, place),
            )

    def load(i, s, loads, keys):
        for key in keys:
            target = getattr(s, key)
            ends = functools.partial(lambda source, target: (source, target), getattr(i, key), target)
            loads.add(key, size_of(target), functools.partial(loads.copies.start, ends))

    def window_in(i, copies, place, owner, target):
        make = copies.reserve(lambda: (i.got, target))

        @pl.when(place == owner)
        def _():
            at = pl.ds(pl.multiple_of(place * length, length), length)
            pltpu.make_async_copy(i.rows.at[0, at], target, copies.sems.at[copies.count - 1]).start()

        @pl.when(place != owner)
        def _():
            make().start()

        return make

    def vectors_of(s, need, place):
        need("vec", "vec2")
        return Vectors(s.vec, s.vec2, place, sizes)

    def attention_first(i, o, s, copies):
        place = lax.axis_index("pipe")
        loads = Loads(copies)
        load(i, s, loads, ["vec", "vec2"])
        loads.add("x", size_of(s.x), lambda: window_in(i, copies, place, 0, s.x))
        load_halves(i, s, loads, 0, ["pos"], place)
        load(i, s, loads, ["seg"])
        load_halves(i, s, loads, 0, ["w_in", "w_out"], place)
        need, done = loads.need, storer(copies, s, o, {})
        vectors = vectors_of(s, need, place)
        need("x", "pos")

        @block
        def _():
            u = s.x[...] + s.pos[...].astype(F32)
            s.u[...] = u
            s.ub[...] = u.astype(BF16)
            done("ub")

        attention_forward(s.u, s.ub, s.w_in, s.w_out, vectors, 0, s.seg, s, need, done)

    first = call(
        "attention_first", attention_first,
        dict(rows=boundary, got=got, **vec_in, **attention_in),
        attention_out,
        dict(x=shape(square, F32), **vec_scratch, **attention_scratch),
        10 * flops_attention,
    )

    def middle(i, o, s, copies):
        place = lax.axis_index("pipe")
        loads = Loads(copies)
        load(i, s, loads, ["vec", "vec2", "r10"])
        load_halves(i, s, loads, 0, ["w_up", "w_down"], place)
        load_halves(i, s, loads, 1, ["pos"], place)
        load(i, s, loads, ["seg"])
        load_halves(i, s, loads, 1, ["w_in", "w_out"], place)
        loads.add("g", size_of(s.g), lambda: window_in(i, copies, place, 1, s.g))
        need, done = loads.need, storer(copies, s, o, {"ub": "", "qkv": "", "p": "", "ot": "", "r1": ""})
        vectors = vectors_of(s, need, place)
        need("r10")

        @block
        def _():
            gain, shift = vectors.get(0, "gain_one"), vectors.get(0, "shift_one")
            h = norm_stats(s.r10[...])[0] * gain + shift
            s.h0[...] = h
            s.hb0[...] = h.astype(BF16)

        def into_last(y):
            u = y.astype(BF16).astype(F32) + s.pos[...].astype(F32)
            s.u[...] = u
            s.ub[...] = u.astype(BF16)

        feed_forward(s.h0, s.hb0, s.w_up, s.w_down, vectors, 0, s, need, done, into_last)
        load_halves(i, s, loads, 1, ["w_up", "w_down"], place)
        attention_forward(s.u, s.ub, s.w_in, s.w_out, vectors, 1, s.seg, s, need, done)
        t = Names()
        t.__dict__.update(s.__dict__)
        t.m, t.d, t.r2 = s.last_m, s.last_d, s.last_r2
        done = storer(copies, s, o, {"m": "", "d": "", "r2": ""}, sides_of("top", place))

        def out_last(y):
            s.y[...] = y
            done("y")

        feed_forward(s.h, s.hb, s.w_up, s.w_down, vectors, 1, t, need, done, out_last)
        feed_backward(s.g, t.r2, s.hb, t.m, t.d, s.w_up, s.w_down, vectors, 1, plans["top"], place, t, need, done)

        def done_low(*keys):
            if keys == ("du",):
                s.gout[...] = s.du[...].astype(BF16)
                copies.start(lambda: (s.gout, o.g))
            else:
                done(*keys)

        attention_backward(
            s.dh, s.r1, s.ub, s.ot, s.qkv, s.p, s.w_in, s.w_out, s.w_up, vectors, 1, plans["top"], place, s, need, done_low
        )

    top = call(
        "middle", middle,
        dict(r10=first["r1"], rows=boundary, got=got, **vec_in, **attention_in, **feed_in),
        dict(**feed_out, y=shape(square, F32), g=shape(square, BF16), **gradients_out["top"]),
        dict(
            r10=shape(square, F32), h0=shape(square, F32), hb0=shape(square, BF16), **hidden_out, g=shape(square, F32), gout=shape(square, BF16),
            y=shape(square, F32), **vec_scratch, **attention_scratch, **feed_weights, **feed_out,
            last_m=feed_out["m"], last_d=feed_out["d"], last_r2=feed_out["r2"], **back_scratch, **gradients["top"],
        ),
        20 * flops_feed,
    )

    def lowest(i, o, s, copies):
        place = lax.axis_index("pipe")
        loads = Loads(copies)
        load(i, s, loads, ["vec", "vec2", "g", "r2"])
        load_halves(i, s, loads, 0, ["w_down"], place)
        load(i, s, loads, ["d", "r1", "m"])
        load_halves(i, s, loads, 0, ["w_up", "w_out"], place)
        load(i, s, loads, ["qkv"])
        moves = []
        for span in p_parts(blocks):
            ends = functools.partial(
                lambda *at: (i.p.at[at[0] : at[1], : at[2]], s.p.at[at[0] : at[1], : at[2]]), *span
            )
            moves.append(functools.partial(copies.start, ends))
        loads.add("p", size_of(s.p), *moves)
        load_halves(i, s, loads, 0, ["w_in"], place)
        load(i, s, loads, ["ub", "ot"])
        need, done = loads.need, storer(copies, s, o, {}, sides_of("low", place))
        vectors = vectors_of(s, need, place)
        feed_backward(s.g, s.r2, None, s.m, s.d, s.w_up, s.w_down, vectors, 0, plans["low"], place, s, need, done)
        attention_backward(
            s.dh, s.r1, s.ub, s.ot, s.qkv, s.p, s.w_in, s.w_out, s.w_up, vectors, 0, plans["low"], place, s, need, done
        )

    sums = {}

    def begin_sums(layer, kernel):
        for number in range(len(plans[layer])):
            name = f"{layer}{number}"
            letters = ("_a", "_b") if name in SPLIT else ("",)
            kept, sent = [[kernel[f"g{number}{end}{letter}"] for letter in letters] for end in ("_keep", "_send")]
            sums[name] = Reduction(kept, sent, orders_for(lax.axis_size("dp"), WAYS[name]))

    begin_sums("top", top)
    low = call(
        "lowest", lowest,
        dict(
            g=top["g"], **{key: top[key] for key in feed_out},
            **{key: first[key] for key in attention_out}, **vec_in, **feed_in,
            w_in=w_in, w_in2=w_in2, w_out=w_out, w_out2=w_out2,
        ),
        dict(du=shape(square, F32), **gradients_out["low"]),
        dict(
            g=shape(square, BF16), **vec_scratch, **attention_weights, **attention_out,
            **feed_weights, **feed_out, **back_scratch, **gradients["low"],
        ),
        12 * flops_feed, after=[total.arrived[0] for total in sums.values()],
    )
    begin_sums("low", low)
    while not all(total.complete() for total in sums.values()):
        for name, total in sums.items():
            wait = WAITS.get((name, total.at + 1)) if len(total.steps) == 4 else None
            ready = wait is None or len(sums[wait[0]].arrived) > wait[1]
            if ready and not total.complete():
                total.step([sums[wait[0]].arrived[wait[1]]] if wait else [])

    theirs = jnp.where(part == 0, top["y"], low["du"])
    if MARK and len(sums[MARK[0]].arrived) > MARK[1]:
        theirs = theirs + jnp.minimum(jnp.abs(sums[MARK[0]].arrived[MARK[1]][:1, :width].astype(F32)), 0)
    theirs = other_core(theirs)
    boundary_out = jnp.stack(
        [jnp.where(part == 0, low["du"], theirs), jnp.where(part == 0, theirs, top["y"])]
    ).reshape(1, window_count * length, width)
    units, more = width // 256, hidden // 256
    big = dict(
        pos=shape((layers, half, width), F32), w_in=shape((layers, half, 3 * width), F32),
        out=shape((layers, half, width), F32), up=shape((layers, half, hidden), F32),
        down=shape((layers, hidden // 2, width), F32),
    )
    big["in"] = big.pop("w_in")
    runs = dict(
        qv_bias=(0, 2 * units), out_bias=(2 * units, units), gain_one=(3 * units, units), shift_one=(4 * units, units),
        up_bias=(16, more), down_bias=(16 + more, units), gain_two=(16 + more + units, units),
        shift_two=(16 + more + 2 * units, units),
    )
    small_out = {key: shape((layers, 128 * count), F32) for key, (unused, count) in runs.items()}

    def assemble(name, layer, parts, extra, so_far):
        kinds = [kind for kind, unused, unused_too in parts if kind in big]
        rows = half // 2

        def body(i, o, s, copies):
            place = lax.axis_index("pipe")
            loads = Loads(copies)
            side = side_of(name, place)
            for key, row in (("value", side * rows), ("other", (1 - side) * rows)):
                at = pl.ds(pl.multiple_of(row, rows), rows)
                ends = functools.partial(lambda a, b, at: (a, b.at[at]), getattr(i, key), s.whole, at)
                loads.add(key, size_of(s.whole) // 2, functools.partial(copies.start, ends))
            for key in extra:
                column = pieces_of(plans["top"], "vec")[0][1]
                ends = functools.partial(
                    lambda a, b, column: (a.at[:32, column : column + 128], b), getattr(i, key), getattr(s, key), column
                )
                loads.add(key, 8192, functools.partial(copies.start, ends))
            loads.need("value", "other", *extra)

            def store(key, low, high):
                if key in ("in", "up"):
                    copies.start(lambda: (getattr(s, key), getattr(o, key).at[layer, :, low:high]))
                else:
                    copies.start(lambda: (getattr(s, key), getattr(o, key).at[layer]))

            @block
            def _():
                column = 0
                for kind, low, high in parts:
                    here = slice(column, column + high - low)
                    if kind == "down":
                        for j in range(hidden // width):
                            one = s.whole[:, column + j * width : column + (j + 1) * width]
                            s.down[j * half : (j + 1) * half, :] = one.astype(F32)
                    elif kind in big:
                        getattr(s, kind)[...] = s.whole[:, here].astype(F32)
                    if kind in big:
                        store(kind, low, high)
                    if kind == "vec" and extra:
                        side = side_of("top1", place) == 0
                        upper = jnp.where(side, s.last_value[...].astype(F32), s.last_other[...].astype(F32))
                        lower = s.whole[:32, here].astype(F32)
                        for key, (at, count) in runs.items():
                            lines = [
                                jnp.concatenate([x[at + j : at + j + 1] for j in range(count)], axis=1)
                                for x in (lower, upper)
                            ]
                            getattr(s, key)[...] = jnp.concatenate(lines, axis=0)
                            copies.start(functools.partial(lambda key: (getattr(s, key), getattr(o, key)), key))
                    column += high - low

        values = dict(zip(("value", "other"), sums[name].parts))
        before = {key: so_far[key] for key in kinds if key in so_far}
        outputs = {**{key: big[key] for key in kinds}, **(small_out if extra else {})}
        scratch = {
            kind: shape(big[kind].shape[1:] if kind == "down" else (half, high - low), F32)
            for kind, low, high in parts if kind in big
        }
        return call(
            "assemble_" + name, body, {**values, **extra, **before}, outputs,
            dict(
                whole=shape((half, columns_of(parts)), BF16), **{key: shape((32, 128), BF16) for key in extra},
                **scratch, **(small_out if extra else {}),
            ),
            flops_feed, loose=list(values) + list(extra),
            aliases={len(values) + len(extra) + n: list(outputs).index(key) for n, key in enumerate(before)},
        )

    result = {}
    for number, parts in enumerate(plans["top"]):
        result.update(assemble(f"top{number}", 1, parts, {}, result))
    last = dict(zip(("last_value", "last_other"), sums["top1"].parts))
    for number, parts in enumerate(plans["low"]):
        extra = last if any(kind == "vec" for kind, unused, unused_too in parts) else {}
        result.update(assemble(f"low{number}", 0, parts, extra, result))
    order = ("pos", "in", "qv_bias", "out", "out_bias", "gain_one", "shift_one", "up", "up_bias", "down", "down_bias",
             "gain_two", "shift_two")
    return (boundary_out,) + tuple(result[key] for key in order)


def solution(mesh):
    rows, vector = P(None, "pipe", None), P(None, "pipe")
    both = P("pipe", "dp", None)
    params = (rows, rows, vector, rows, vector, vector, vector, rows, vector, rows, vector, vector, vector)
    return jax.shard_map(
        per_device,
        mesh=mesh,
        in_specs=(both,) + params + (P("dp", None),),
        out_specs=(both,) + params,
        check_vma=False,
    )
```
